32 devices in a mesh: blk: 8 (over y, x, core), uly: 4 (over z).
Axes of the slice: x: 2, y: 2, z: 4, core: 2. Of those that a mesh axis runs over, the one named last changes fastest.
Arguments:
- tokens: bfloat16 [1536, 2048], P(('blk', 'uly')), may hold values from -6 to 6
- mod_shift: float32 [2048], replicated, may hold values from -3 to 3
- mod_scale: float32 [2048], replicated, may hold values from -2.5 to 2.5
- mod_gate: float32 [2048], replicated, may hold values from 0.25 to 1.5
- w_query: bfloat16 [2048, 2048], P(None, 'uly'), may hold values from -0.125 to 0.125
- w_key: bfloat16 [2048, 2048], P(None, 'uly'), may hold values from -0.125 to 0.125
- w_value: bfloat16 [2048, 2048], P(None, 'uly'), may hold values from -0.125 to 0.125
- w_out: bfloat16 [2048, 2048], P('uly'), may hold values from -0.125 to 0.125
- score_gain: float32 [32], replicated, may hold values from 4 to 40, as said below
Outputs:
- block_out: bfloat16 [1536, 2048], P(('blk', 'uly'))
The draws below stay inside these ranges and needn't reach their ends.
Inputs may be any that keep to these rules, and one draw needn't show every extreme that they name: `score_gain`: one positive factor for each head.
All inputs are finite; a program needn't handle non-finite values.
Results may differ from the reference program's by a relative error of at most 0.012.
The reference program's roundings to bfloat16 on the way (of `modded`, `value`, `weights` and `attended`) count: a program that leaves them out, or rounds other values in their place, can miss the bound.
Values may be sent and summed in bfloat16 or wider, within the bound.
A program may use at most 192 MiB of HBM per device.

```python
import math
import jax
import jax.numpy as jnp
from jax import lax

D = 2048
HEADS = 32
SEQ = 1536


def draw_score_gain(key, part):
    level = jax.random.uniform(key, (HEADS,), jnp.float32)
    return 4.0 * jnp.exp(level * jnp.log(4.0))


def block_scale(stream_key, dims, shards, smallest, largest):
    factor_of, own = 1.0, jax.random.fold_in(stream_key, 6)
    for position, blocks in shards:
        draws = jnp.exp(jax.random.uniform(jax.random.fold_in(own, position), (blocks,), jnp.float32, smallest / len(shards), largest / len(shards)))
        factor_of = factor_of * jnp.repeat(draws, dims[position] // blocks).reshape([-1 if axis == position else 1 for axis in range(len(dims))])
    return factor_of


def centred(rng, extent, scale, limit, cuts=(), held_as=jnp.bfloat16):
    level = block_scale(rng, extent, cuts, -0.22, 0.18) if cuts else 1.0
    entries = jax.random.normal(rng, extent, jnp.float32) * scale * level
    return jnp.minimum(jnp.maximum(entries, -limit), limit).astype(held_as)


def setup_inputs(seed: int = 0) -> dict:
    arg_keys = jax.random.split(jax.random.key(seed), 10)
    tokens = centred(arg_keys[0], (SEQ, D), 1.0, 6.0, ((0, 32),))
    mod_shift = centred(arg_keys[1], (D,), 0.5, 3.0, (), jnp.float32)
    mod_scale = centred(arg_keys[2], (D,), 0.5, 2.5, (), jnp.float32)
    mod_gate = jnp.clip(jax.random.uniform(arg_keys[3], (D,), jnp.float32, 0.25, 1.5), 0.25, 1.5)
    w_query = centred(arg_keys[4], (D, D), D ** -0.5, 0.125, ((1, 4),))
    w_key = centred(arg_keys[5], (D, D), D ** -0.5, 0.125, ((1, 4),))
    w_value = centred(arg_keys[6], (D, D), D ** -0.5, 0.125, ((1, 4),))
    w_out = centred(arg_keys[7], (D, D), D ** -0.5, 0.125, ((0, 4),))
    score_gain = draw_score_gain(jax.random.fold_in(arg_keys[9], 71), 0)
    return {"tokens": tokens, "mod_shift": mod_shift, "mod_scale": mod_scale, "mod_gate": mod_gate, "w_query": w_query, "w_key": w_key, "w_value": w_value, "w_out": w_out, "score_gain": score_gain}


def modulate(tokens, mod_shift, mod_scale):
    values = tokens.astype(jnp.float32)
    center = values - lax.optimization_barrier(jnp.mean(values, axis=-1, keepdims=True))
    spread = lax.optimization_barrier(jnp.mean(center * center, axis=-1, keepdims=True))
    normed = center * lax.rsqrt(spread + 1e-06)
    return (normed * (1.0 + mod_scale) + mod_shift).astype(jnp.bfloat16)

def head_norm(projected, width):
    count = projected.shape[0]
    split = projected.reshape(count, -1, width)
    power = lax.optimization_barrier(jnp.mean(split * split, axis=-1, keepdims=True))
    return (split * lax.rsqrt(power + 1e-06)).reshape(count, -1).astype(jnp.bfloat16)

def reference(tokens, mod_shift, mod_scale, mod_gate, w_query, w_key, w_value, w_out, score_gain):
    width = D // HEADS
    modded = modulate(tokens, mod_shift, mod_scale)
    query = head_norm(jnp.dot(modded, w_query, preferred_element_type=jnp.float32), width)
    key = head_norm(jnp.dot(modded, w_key, preferred_element_type=jnp.float32), width)
    value = jnp.dot(modded, w_value, preferred_element_type=jnp.float32).astype(jnp.bfloat16)
    query_heads = query.reshape(SEQ, HEADS, width).transpose(1, 0, 2)
    key_heads = key.reshape(SEQ, HEADS, width).transpose(1, 0, 2)
    value_heads = value.reshape(SEQ, HEADS, width).transpose(1, 0, 2)
    block_rows = math.gcd(SEQ, 1024)

    def one_head(packed):
        query_head, key_head, value_head, gain = packed
        factor = gain / math.sqrt(width)

        def one_block(query_block):
            scores = jnp.dot(query_block, key_head.T, preferred_element_type=jnp.float32) * factor
            top = lax.optimization_barrier(jnp.max(scores, axis=-1, keepdims=True))
            expo = jnp.exp(scores - top)
            total = lax.optimization_barrier(jnp.sum(expo, axis=-1, keepdims=True))
            weights = expo.astype(jnp.bfloat16)
            summed = jnp.dot(weights, value_head, preferred_element_type=jnp.float32)
            return (summed / total).astype(jnp.bfloat16)
        blocks = query_head.reshape(SEQ // block_rows, block_rows, width)
        return lax.map(one_block, blocks).reshape(SEQ, width)
    attended = lax.map(one_head, (query_heads, key_heads, value_heads, score_gain))
    attended = attended.transpose(1, 0, 2).reshape(SEQ, D)
    projected = jnp.dot(attended, w_out, preferred_element_type=jnp.float32)
    return (tokens.astype(jnp.float32) + mod_gate * projected).astype(jnp.bfloat16)
```

```python
import functools
import math

import jax
import jax.numpy as jnp
from jax import lax
from jax.experimental import pallas as pl
from jax.experimental.pallas import tpu as pltpu
from jax.sharding import PartitionSpec as P

D = 2048
HEADS = 32
LOG2E = math.log2(math.e)
MESH = pl.DeviceIdType.MESH
SUB = 192


def kernel(
    nb, tok_h, shift_h, scale_h, gate_h, gain_h, wq, wk, wv, wo, out,
    tok, shift, scale, gate, gain, mod, wq_v, wk_v, wv_v, wo_v, kv_s, q_s, kv_r, q_r, top_v, sum_v, acc_v,
    att_s, att_r, part_v, part_s, pair_r, near_r, far_r,
    wsem, gs, gr, fs, hs, hr, bs, br, rs, rr,
):
    width = D // HEADS
    rows = tok.shape[0]
    span = nb * rows
    chunks = mod.shape[1]
    deep = mod.shape[3]
    tile = part_s.shape[-1]
    parts = D // tile
    mb, mz = lax.axis_index("blk"), lax.axis_index("uly")
    high = mz // 2
    middle = (mz + 1) // 2 == 1
    near = mz + 1 - 2 * lax.rem(mz, 2)
    inner = 2 - high
    outer = 3 - 3 * high

    barrier = pltpu.get_barrier_semaphore()
    for z in (inner, near):
        pl.semaphore_signal(barrier, inc=1, device_id={"uly": z}, device_id_type=MESH)

    @pl.when(middle)
    def _():
        pl.semaphore_signal(barrier, inc=1, device_id={"uly": outer}, device_id_type=MESH)

    for j in range(1, nb):
        pl.semaphore_signal(barrier, inc=1, device_id={"blk": lax.rem(mb + j, nb)}, device_id_type=MESH)

    pairs = (
        (tok_h, tok), (shift_h, shift), (scale_h, scale), (wk, wk_v), (wv, wv_v), (wq, wq_v),
        (wo, wo_v), (gate_h, gate), (gain_h, gain),
    )
    loads = [
        pltpu.make_async_copy(src, dst, wsem.at[i])
        for i, (src, dst) in enumerate(pairs)
    ]
    for load in loads:
        load.start()
    for load in loads[:3]:
        load.wait()

    values = tok[...].astype(jnp.float32)
    center = values - jnp.mean(values, axis=-1, keepdims=True)
    spread = jnp.mean(center * center, axis=-1, keepdims=True)
    normed = center * lax.rsqrt(spread + 1e-06)
    modded = (normed * (1.0 + scale[...]) + shift[...]).astype(jnp.bfloat16)
    for c in range(chunks):
        mod[0, c] = modded[:, c * deep : (c + 1) * deep]

    pl.semaphore_wait(barrier, nb + 1 + middle.astype(jnp.int32))

    def gather(way, c):
        slot = 1 if way == 0 else 3 - middle.astype(jnp.int32)
        return pltpu.make_async_remote_copy(
            src_ref=mod.at[0, c], dst_ref=mod.at[slot, c], send_sem=gs.at[way, c], recv_sem=gr.at[slot, c],
            device_id={"uly": inner if way else near}, device_id_type=MESH)

    def landed(k, c):
        return pltpu.make_async_remote_copy(
            src_ref=mod.at[0, c], dst_ref=mod.at[k, c], send_sem=gs.at[0, c], recv_sem=gr.at[k, c],
            device_id={"uly": near}, device_id_type=MESH)

    def forward(k, c):
        return pltpu.make_async_remote_copy(
            src_ref=mod.at[k, c], dst_ref=mod.at[k, c], send_sem=fs.at[k, c], recv_sem=gr.at[k, c],
            device_id={"uly": near}, device_id_type=MESH)

    @pl.when(middle)
    def _():
        for c in range(chunks):
            for way in (0, 1):
                gather(way, c).start()

    @pl.when(jnp.logical_not(middle))
    def _():
        for way in (0, 1):
            for c in range(chunks):
                gather(way, c).start()

    for load in loads[3:6]:
        load.wait()

    def place(k, b):
        return pl.ds(pl.multiple_of(k * span + b * rows, rows), rows)

    def heads_to(k, kind, b):
        src, dst = ((kv_s, kv_r), (q_s, q_r))[kind]
        return pltpu.make_async_remote_copy(
            src_ref=src.at[k, b], dst_ref=dst.at[place(k, mb), :], send_sem=hs.at[k, kind, b],
            recv_sem=hr.at[k, kind, mb], device_id={"blk": b}, device_id_type=MESH)

    def heads_from(k, kind, b):
        src, dst = ((kv_s, kv_r), (q_s, q_r))[kind]
        return pltpu.make_async_remote_copy(
            src_ref=src.at[k, b], dst_ref=dst.at[place(k, b), :], send_sem=hs.at[k, kind, b],
            recv_sem=hr.at[k, kind, b], device_id={"blk": b}, device_id_type=MESH)

    loads[8].wait()
    chosen = lax.broadcasted_iota(jnp.int32, gain.shape, 1) == mz * nb + mb
    factor = jnp.sum(jnp.where(chosen, gain[...], 0.0), axis=-1, keepdims=True) * (LOG2E / math.sqrt(width))

    def await_heads(k, kind):
        for j in range(1, nb):
            heads_from(k, kind, lax.rem(mb + j, nb)).wait_recv()

    def begin(start, size, first, last):
        where = pl.ds(pl.multiple_of(start, rows), size)
        kv = kv_r[first * span : last * span, :]
        scores = lax.dot_general(q_r[where, :], kv, (((1,), (1,)), ((), ())), preferred_element_type=jnp.float32)
        top = jnp.max(scores, axis=-1, keepdims=True)
        expo = jnp.exp2((scores - top) * factor)
        total = jnp.sum(expo, axis=-1, keepdims=True)
        summed = jnp.dot(expo.astype(jnp.bfloat16), kv, preferred_element_type=jnp.float32)
        return top, total, summed

    def keep(start, size, first, last):
        where = pl.ds(pl.multiple_of(start, rows), size)
        top_v[where, :], sum_v[where, :], acc_v[where, :] = begin(start, size, first, last)

    def more(start, size, first, last):
        where = pl.ds(pl.multiple_of(start, rows), size)
        kv = kv_r[first * span : last * span, :]
        scores = lax.dot_general(q_r[where, :], kv, (((1,), (1,)), ((), ())), preferred_element_type=jnp.float32)
        old = top_v[where, :]
        top = jnp.maximum(old, jnp.max(scores, axis=-1, keepdims=True))
        shrink = jnp.exp2((old - top) * factor)
        expo = jnp.exp2((scores - top) * factor)
        total = sum_v[where, :] * shrink + jnp.sum(expo, axis=-1, keepdims=True)
        summed = jnp.dot(expo.astype(jnp.bfloat16), kv, preferred_element_type=jnp.float32)
        return total, acc_v[where, :] * shrink + summed

    def first_attend():
        for k in (0, 1):
            await_heads(k, 0)
            await_heads(k, 1)

        def step(i, carry):
            keep(i * SUB, SUB, 0, 2)
            return carry

        lax.fori_loop(0, 2 * span // SUB, step, 0)

    def piece(k, carry):
        @pl.when((k == 3) & jnp.logical_not(middle))
        def _():
            first_attend()

        query = key = value = None
        for c in range(chunks):
            @pl.when((k > 0) & (jnp.logical_not(middle) | (k == 1)))
            def _():
                landed(k, c).wait_recv()

            @pl.when(middle & (k > 0) & (k < 3))
            def _():
                landed(k + 1, c).wait_recv()
                forward(k + 1, c).start()

            x = mod[k, c]
            deeps = slice(c * deep, (c + 1) * deep)
            more_k = jnp.dot(x, wk_v[deeps, :], preferred_element_type=jnp.float32)
            more_v = jnp.dot(x, wv_v[deeps, :], preferred_element_type=jnp.float32)
            more_q = jnp.dot(x, wq_v[deeps, :], preferred_element_type=jnp.float32)
            key = more_k if c == 0 else key + more_k
            value = more_v if c == 0 else value + more_v
            query = more_q if c == 0 else query + more_q

        def unit(part):
            power = jnp.mean(part * part, axis=-1, keepdims=True)
            return part * lax.rsqrt(power + 1e-06)

        def send(kind):
            def one(j, carry):
                heads_to(k, kind, lax.rem(mb + j, nb)).start()
                return carry

            lax.fori_loop(1, nb, one, 0)

        for h in range(nb):
            cols = slice(h * width, (h + 1) * width)
            kv_s[k, h] = jnp.concatenate([unit(key[:, cols]), value[:, cols]], axis=1).astype(jnp.bfloat16)
        send(0)
        kv_r[place(k, mb), :] = kv_s[k, mb]
        for h in range(nb):
            cols = slice(h * width, (h + 1) * width)
            line = unit(query[:, cols])
            q_s[k, h] = jnp.concatenate([line, jnp.zeros_like(line)], axis=1).astype(jnp.bfloat16)
        send(1)
        q_r[place(k, mb), :] = q_s[k, mb]
        return carry

    lax.fori_loop(0, 4, piece, 0)

    @pl.when(middle)
    def _():
        first_attend()

    await_heads(2, 0)
    await_heads(2, 1)

    def step(i, carry):
        keep(2 * span + i * SUB, SUB, 0, 3)
        return carry

    lax.fori_loop(0, span // SUB, step, 0)
    await_heads(3, 0)

    def back_to(k, b):
        return pltpu.make_async_remote_copy(
            src_ref=att_s.at[k, pl.ds(pl.multiple_of(b * rows, rows), rows), :], dst_ref=att_r.at[k, mb],
            send_sem=bs.at[k, b], recv_sem=br.at[k, mb], device_id={"blk": b}, device_id_type=MESH)

    def back_from(k, b):
        return pltpu.make_async_remote_copy(
            src_ref=att_s.at[k, pl.ds(pl.multiple_of(b * rows, rows), rows), :], dst_ref=att_r.at[k, b],
            send_sem=bs.at[k, b], recv_sem=br.at[k, b], device_id={"blk": b}, device_id_type=MESH)

    def finish(k):
        def step(i, carry):
            if k == 3:
                unused, total, summed = begin(k * span + i * SUB, SUB, 0, 4)
            else:
                total, summed = more(k * span + i * SUB, SUB, 3 if k == 2 else 2, 4)
            att_s[k, pl.ds(pl.multiple_of(i * SUB, rows), SUB), :] = (summed / total).astype(jnp.bfloat16)
            return carry

        lax.fori_loop(0, span // SUB, step, 0)

        def one(j, carry):
            back_to(k, lax.rem(mb + j, nb)).start()
            return carry

        lax.fori_loop(1, nb, one, 0)
        att_r[k, mb] = att_s[k, pl.ds(pl.multiple_of(mb * rows, rows), rows), :]

    def near_to(n):
        return pltpu.make_async_remote_copy(
            src_ref=part_s.at[1, n], dst_ref=near_r.at[n], send_sem=rs.at[1, n], recv_sem=rr.at[1, n],
            device_id={"uly": near}, device_id_type=MESH)

    def pair_to(k, n):
        return pltpu.make_async_remote_copy(
            src_ref=part_s.at[k, n], dst_ref=pair_r.at[k - 2, n], send_sem=rs.at[k, n], recv_sem=rr.at[k, n],
            device_id={"uly": near}, device_id_type=MESH)

    def far_to(k, n):
        return pltpu.make_async_remote_copy(
            src_ref=part_s.at[k, n], dst_ref=far_r.at[n], send_sem=rs.at[k, n], recv_sem=rr.at[0, n],
            device_id={"uly": inner if k == 2 else outer}, device_id_type=MESH)

    def project(k):
        for j in range(1, nb):
            back_from(k, lax.rem(mb + j, nb)).wait_recv()
        attended = jnp.concatenate([att_r[k, h][:, width:] for h in range(nb)], axis=1)
        for n in range(parts):
            part = jnp.dot(attended, wo_v[:, n * tile : (n + 1) * tile], preferred_element_type=jnp.float32)
            if k == 1:
                part_s[1, n] = part.astype(jnp.bfloat16)
                near_to(n).start()
            elif k == 0:
                part_v[0, n] = part
            else:
                @pl.when(middle)
                def _():
                    part_v[k, n] = part

                @pl.when(jnp.logical_not(middle))
                def _():
                    part_s[k, n] = part.astype(jnp.bfloat16)
                    pair_to(k, n).start()

    finish(2)
    await_heads(3, 1)
    finish(3)
    loads[6].wait()
    loads[7].wait()
    project(2)
    finish(1)
    project(3)
    finish(0)
    project(1)
    project(0)

    @pl.when(middle)
    def _():
        for k in (2, 3):
            for n in range(parts):
                pair_to(k, n).wait_recv()
                part_s[k, n] = (part_v[k, n] + pair_r[k - 2, n].astype(jnp.float32)).astype(jnp.bfloat16)
                far_to(k, n).start()

    for n in range(parts):
        far_to(2, n).wait_recv()
        near_to(n).wait_recv()
        total = part_v[0, n] + near_r[n].astype(jnp.float32) + far_r[n].astype(jnp.float32)
        cols = slice(n * tile, (n + 1) * tile)
        out[:, cols] = (tok[:, cols].astype(jnp.float32) + gate[:, cols] * total).astype(jnp.bfloat16)

    for way in (0, 1):
        for c in range(chunks):
            gather(way, c).wait_send()

    @pl.when(middle)
    def _():
        for k in (2, 3):
            for c in range(chunks):
                forward(k, c).wait_send()

    def sent(i, carry):
        b = lax.rem(mb + 1 + lax.rem(i, nb - 1), nb)
        k = i // (nb - 1)
        heads_to(k, 0, b).wait_send()
        heads_to(k, 1, b).wait_send()
        back_to(k, b).wait_send()
        return carry

    lax.fori_loop(0, 4 * (nb - 1), sent, 0)
    for k in (1, 2, 3):
        for n in range(parts):
            near_to(n).wait_send() if k == 1 else pair_to(k, n).wait_send()


def fused(nb, tokens, mod_shift, mod_scale, mod_gate, w_query, w_key, w_value, w_out, score_gain):
    rows = tokens.shape[0]
    cols = w_query.shape[1]
    chunks = 4
    tile = 512
    parts = D // tile
    span = nb * rows
    bf16, f32 = jnp.bfloat16, jnp.float32
    vmem = pl.BlockSpec(memory_space=pltpu.VMEM)
    hbm = pl.BlockSpec(memory_space=pltpu.HBM)
    dma = pltpu.SemaphoreType.DMA
    return pl.pallas_call(
        functools.partial(kernel, nb),
        out_shape=jax.ShapeDtypeStruct((rows, D), bf16),
        in_specs=[hbm] * 9,
        out_specs=vmem,
        scratch_shapes=[
            pltpu.VMEM((rows, D), bf16),
            pltpu.VMEM((1, D), f32),
            pltpu.VMEM((1, D), f32),
            pltpu.VMEM((1, D), f32),
            pltpu.VMEM((1, HEADS), f32),
            pltpu.VMEM((4, chunks, rows, D // chunks), bf16),
            pltpu.VMEM((D, cols), bf16),
            pltpu.VMEM((D, cols), bf16),
            pltpu.VMEM((D, cols), bf16),
            pltpu.VMEM((cols, D), bf16),
            pltpu.VMEM((4, nb, rows, 128), bf16),
            pltpu.VMEM((4, nb, rows, 128), bf16),
            pltpu.VMEM((4 * span, 128), bf16),
            pltpu.VMEM((4 * span, 128), bf16),
            pltpu.VMEM((4 * span, 1), f32),
            pltpu.VMEM((4 * span, 1), f32),
            pltpu.VMEM((4 * span, 128), f32),
            pltpu.VMEM((4, span, 128), bf16),
            pltpu.VMEM((4, nb, rows, 128), bf16),
            pltpu.VMEM((4, parts, rows, tile), f32),
            pltpu.VMEM((4, parts, rows, tile), bf16),
            pltpu.VMEM((2, parts, rows, tile), bf16),
            pltpu.VMEM((parts, rows, tile), bf16),
            pltpu.VMEM((parts, rows, tile), bf16),
            dma((9,)),
            dma((2, chunks)),
            dma((4, chunks)),
            dma((4, chunks)),
            dma((4, 2, nb)),
            dma((4, 2, nb)),
            dma((4, nb)),
            dma((4, nb)),
            dma((4, parts)),
            dma((4, parts)),
        ],
        compiler_params=pltpu.CompilerParams(
            collective_id=0, has_side_effects=True, vmem_limit_bytes=56 * 1024 * 1024
        ),
    )(
        tokens, mod_shift[None], mod_scale[None], mod_gate[None], score_gain[None],
        w_query, w_key, w_value, w_out,
    )


def modulate(tokens, mod_shift, mod_scale):
    values = tokens.astype(jnp.float32)
    center = values - jnp.mean(values, axis=-1, keepdims=True)
    spread = jnp.mean(center * center, axis=-1, keepdims=True)
    normed = center * lax.rsqrt(spread + 1e-06)
    return (normed * (1.0 + mod_scale) + mod_shift).astype(jnp.bfloat16)


def head_norm(projected, width):
    count = projected.shape[0]
    split = projected.reshape(count, -1, width)
    power = jnp.mean(split * split, axis=-1, keepdims=True)
    return (split * lax.rsqrt(power + 1e-06)).reshape(count, -1).astype(jnp.bfloat16)


def body(tokens, mod_shift, mod_scale, mod_gate, w_query, w_key, w_value, w_out, score_gain):
    width = D // HEADS
    local_cols = w_query.shape[1]
    local_heads = local_cols // width
    modded = modulate(tokens, mod_shift, mod_scale)
    piece = lax.all_gather(modded, "uly", axis=0, tiled=True)
    joined = jnp.concatenate(
        [
            jnp.dot(piece, w_query, preferred_element_type=jnp.float32),
            jnp.dot(piece, w_key, preferred_element_type=jnp.float32),
            jnp.dot(piece, w_value, preferred_element_type=jnp.float32),
        ],
        axis=1,
    )
    queries = head_norm(joined[:, :local_cols], width)
    keys = head_norm(joined[:, local_cols : 2 * local_cols], width)
    values = joined[:, 2 * local_cols :].astype(jnp.bfloat16)
    gains = lax.dynamic_slice_in_dim(score_gain, lax.axis_index("uly") * local_heads, local_heads)
    factors = gains / math.sqrt(width)
    rows = queries.shape[0]
    query_heads = queries.reshape(rows, local_heads, width)
    initial = (
        jnp.full((local_heads, rows), -jnp.inf, jnp.float32),
        jnp.zeros((local_heads, rows), jnp.float32),
        jnp.zeros((local_heads, rows, width), jnp.float32),
    )
    key_piece = lax.all_gather(keys, "blk", axis=0, tiled=True)
    value_piece = lax.all_gather(values, "blk", axis=0, tiled=True)
    count = key_piece.shape[0]
    groups = count // rows
    limit = max(rows, 1024)
    depth = max(
        [step for step in range(1, groups + 1) if groups % step == 0 and step * rows <= limit]
    )
    stride = depth * rows
    key_blocks = key_piece.reshape(count // stride, stride, local_heads, width)
    value_blocks = value_piece.reshape(count // stride, stride, local_heads, width)

    def one_block(carry, blocks):
        run_max, run_total, run_acc = carry
        key_block, value_block = blocks
        scores = jnp.einsum(
            "rhd,khd->hrk", query_heads, key_block, preferred_element_type=jnp.float32
        )
        scores = scores * factors[:, None, None]
        new_max = jnp.maximum(run_max, jnp.max(scores, axis=-1))
        expo = jnp.exp(scores - new_max[..., None])
        rescale = jnp.exp(run_max - new_max)
        new_total = run_total * rescale + jnp.sum(expo, axis=-1)
        summed = jnp.einsum(
            "hrk,khd->hrd",
            expo.astype(jnp.bfloat16),
            value_block,
            preferred_element_type=jnp.float32,
        )
        new_acc = run_acc * rescale[..., None] + summed
        return ((new_max, new_total, new_acc), None)

    result, unused = lax.scan(one_block, initial, (key_blocks, value_blocks))
    run_max, run_total, run_acc = result
    attended = (run_acc / run_total[..., None]).astype(jnp.bfloat16)
    attended = attended.transpose(1, 0, 2).reshape(rows, local_cols)
    returned = lax.all_to_all(attended, "uly", split_axis=0, concat_axis=1, tiled=True)
    projected = jnp.dot(
        returned,
        lax.all_gather(w_out, "uly", axis=0, tiled=True),
        preferred_element_type=jnp.float32,
    )
    return (tokens.astype(jnp.float32) + mod_gate * projected).astype(jnp.bfloat16)


def solution(mesh):
    in_specs = (
        P(("blk", "uly"), None),
        P(),
        P(),
        P(),
        P(None, "uly"),
        P(None, "uly"),
        P(None, "uly"),
        P("uly", None),
        P(),
    )
    out_specs = P(("blk", "uly"), None)
    nb, nz = mesh.shape["blk"], mesh.shape["uly"]
    run = body
    if HEADS == nb * nz and nz == 4:
        run = functools.partial(fused, nb)
    return jax.shard_map(run, mesh=mesh, in_specs=in_specs, out_specs=out_specs, check_vma=False)
```

```python
import functools
import math

import jax
import jax.numpy as jnp
from jax import lax
from jax.experimental import pallas as pl
from jax.experimental.pallas import tpu as pltpu
from jax.sharding import PartitionSpec as P

D = 2048
HEADS = 32
LOG2E = math.log2(math.e)
MESH = pl.DeviceIdType.MESH
SUB = 384


def kernel(
    nb, tok_h, shift_h, scale_h, gate_h, gain_h, wq, wk, wv, wo, out,
    tok, shift, scale, gate, gain, mod, wq_v, wk_v, wv_v, wo_v, kv_s, q_s, kv_r, q_r, vt, top_v, sum_v, acc_v,
    att_s, att_r, part_v, part_s, pair_r, near_r, far_r,
    wsem, gs, gr, fs, hs, hr, bs, br, rs, rr,
):
    width = D // HEADS
    rows = tok.shape[0]
    span = nb * rows
    chunks = mod.shape[1]
    deep = mod.shape[3]
    tile = part_s.shape[-1]
    parts = D // tile
    mb, mz = lax.axis_index("blk"), lax.axis_index("uly")
    high = mz // 2
    middle = (mz + 1) // 2 == 1
    near = mz + 1 - 2 * lax.rem(mz, 2)
    inner = 2 - high
    outer = 3 - 3 * high

    barrier = pltpu.get_barrier_semaphore()
    for z in (inner, near):
        pl.semaphore_signal(barrier, inc=1, device_id={"uly": z}, device_id_type=MESH)

    @pl.when(middle)
    def _():
        pl.semaphore_signal(barrier, inc=1, device_id={"uly": outer}, device_id_type=MESH)

    for j in range(1, nb):
        pl.semaphore_signal(barrier, inc=1, device_id={"blk": lax.rem(mb + j, nb)}, device_id_type=MESH)

    pairs = (
        (tok_h, tok), (shift_h, shift), (scale_h, scale), (wk, wk_v), (wv, wv_v), (wq, wq_v),
        (wo, wo_v), (gate_h, gate), (gain_h, gain),
    )
    loads = [
        pltpu.make_async_copy(src, dst, wsem.at[i])
        for i, (src, dst) in enumerate(pairs)
    ]
    for load in loads:
        load.start()
    for load in loads[:3]:
        load.wait()

    values = tok[...].astype(jnp.float32)
    center = values - jnp.mean(values, axis=-1, keepdims=True)
    spread = jnp.mean(center * center, axis=-1, keepdims=True)
    normed = center * lax.rsqrt(spread + 1e-06)
    modded = (normed * (1.0 + scale[...]) + shift[...]).astype(jnp.bfloat16)
    for c in range(chunks):
        mod[0, c] = modded[:, c * deep : (c + 1) * deep]

    pl.semaphore_wait(barrier, nb + 1 + middle.astype(jnp.int32))

    def gather(way, c):
        slot = 1 if way == 0 else 3 - middle.astype(jnp.int32)
        return pltpu.make_async_remote_copy(
            src_ref=mod.at[0, c], dst_ref=mod.at[slot, c], send_sem=gs.at[way, c], recv_sem=gr.at[slot, c],
            device_id={"uly": inner if way else near}, device_id_type=MESH)

    def landed(k, c):
        return pltpu.make_async_remote_copy(
            src_ref=mod.at[0, c], dst_ref=mod.at[k, c], send_sem=gs.at[0, c], recv_sem=gr.at[k, c],
            device_id={"uly": near}, device_id_type=MESH)

    def forward(k, c):
        return pltpu.make_async_remote_copy(
            src_ref=mod.at[k, c], dst_ref=mod.at[k, c], send_sem=fs.at[k, c], recv_sem=gr.at[k, c],
            device_id={"uly": near}, device_id_type=MESH)

    @pl.when(middle)
    def _():
        for c in range(chunks):
            for way in (0, 1):
                gather(way, c).start()

    @pl.when(jnp.logical_not(middle))
    def _():
        for way in (0, 1):
            for c in range(chunks):
                gather(way, c).start()

    for load in loads[3:6]:
        load.wait()

    def place(k, b):
        return pl.ds(pl.multiple_of(k * span + b * rows, rows), rows)

    def heads_to(k, kind, b):
        src, dst = ((kv_s, kv_r), (q_s, q_r))[kind]
        return pltpu.make_async_remote_copy(
            src_ref=src.at[k, b], dst_ref=dst.at[place(k, mb), :], send_sem=hs.at[k, kind, b],
            recv_sem=hr.at[k, kind, mb], device_id={"blk": b}, device_id_type=MESH)

    def heads_from(k, kind, b):
        src, dst = ((kv_s, kv_r), (q_s, q_r))[kind]
        return pltpu.make_async_remote_copy(
            src_ref=src.at[k, b], dst_ref=dst.at[place(k, b), :], send_sem=hs.at[k, kind, b],
            recv_sem=hr.at[k, kind, b], device_id={"blk": b}, device_id_type=MESH)

    loads[8].wait()
    chosen = lax.broadcasted_iota(jnp.int32, gain.shape, 1) == mz * nb + mb
    factor = jnp.sum(jnp.where(chosen, gain[...], 0.0), axis=-1, keepdims=True) * (LOG2E / math.sqrt(width))

    def await_heads(k, kind):
        for j in range(1, nb):
            heads_from(k, kind, lax.rem(mb + j, nb)).wait_recv()

    def flip(k):
        vt[:, k * span : (k + 1) * span] = kv_r[k * span : (k + 1) * span, :].T[width:, :]

    def scored(k, c, first, last):
        q = q_r[k * span + c * SUB : k * span + (c + 1) * SUB, :]
        return lax.dot_general(
            kv_r[first * span : last * span, :], q, (((1,), (1,)), ((), ())), preferred_element_type=jnp.float32)

    def begin(k, c, first, last):
        scores = scored(k, c, first, last)
        top = jnp.max(scores, axis=0, keepdims=True)
        expo = jnp.exp2((scores - top) * factor)
        total = jnp.sum(expo, axis=0, keepdims=True)
        summed = jnp.dot(vt[:, first * span : last * span], expo.astype(jnp.bfloat16), preferred_element_type=jnp.float32)
        return top, total, summed

    def keep(k, first, last):
        for c in range(span // SUB):
            cols = slice(c * SUB, (c + 1) * SUB)
            top_v[k, :, cols], sum_v[k, :, cols], acc_v[k, :, cols] = begin(k, c, first, last)

    def more(k, c, first, last):
        cols = slice(c * SUB, (c + 1) * SUB)
        scores = scored(k, c, first, last)
        old = top_v[k, :, cols]
        top = jnp.maximum(old, jnp.max(scores, axis=0, keepdims=True))
        shrink = jnp.exp2((old - top) * factor)
        expo = jnp.exp2((scores - top) * factor)
        total = sum_v[k, :, cols] * shrink + jnp.sum(expo, axis=0, keepdims=True)
        summed = jnp.dot(vt[:, first * span : last * span], expo.astype(jnp.bfloat16), preferred_element_type=jnp.float32)
        return total, acc_v[k, :, cols] * shrink + summed

    def first_attend():
        for k in (0, 1):
            await_heads(k, 0)
            await_heads(k, 1)
            flip(k)
        for k in (0, 1):
            keep(k, 0, 2)

    def piece(k, carry):
        @pl.when((k == 3) & jnp.logical_not(middle))
        def _():
            first_attend()

        query = key = value = None
        for c in range(chunks):
            @pl.when((k > 0) & (jnp.logical_not(middle) | (k == 1)))
            def _():
                landed(k, c).wait_recv()

            @pl.when(middle & (k > 0) & (k < 3))
            def _():
                landed(k + 1, c).wait_recv()
                forward(k + 1, c).start()

            x = mod[k, c]
            deeps = slice(c * deep, (c + 1) * deep)
            more_k = jnp.dot(x, wk_v[deeps, :], preferred_element_type=jnp.float32)
            more_v = jnp.dot(x, wv_v[deeps, :], preferred_element_type=jnp.float32)
            more_q = jnp.dot(x, wq_v[deeps, :], preferred_element_type=jnp.float32)
            key = more_k if c == 0 else key + more_k
            value = more_v if c == 0 else value + more_v
            query = more_q if c == 0 else query + more_q

        def unit(part):
            power = jnp.mean(part * part, axis=-1, keepdims=True)
            return part * lax.rsqrt(power + 1e-06)

        def send(kind):
            def one(j, carry):
                heads_to(k, kind, lax.rem(mb + j, nb)).start()
                return carry

            lax.fori_loop(1, nb, one, 0)

        for h in range(nb):
            cols = slice(h * width, (h + 1) * width)
            kv_s[k, h] = jnp.concatenate([unit(key[:, cols]), value[:, cols]], axis=1).astype(jnp.bfloat16)
        send(0)
        kv_r[place(k, mb), :] = kv_s[k, mb]
        for h in range(nb):
            cols = slice(h * width, (h + 1) * width)
            line = unit(query[:, cols])
            q_s[k, h] = jnp.concatenate([line, jnp.zeros_like(line)], axis=1).astype(jnp.bfloat16)
        send(1)
        q_r[place(k, mb), :] = q_s[k, mb]
        return carry

    lax.fori_loop(0, 4, piece, 0)

    @pl.when(middle)
    def _():
        first_attend()

    await_heads(2, 0)
    await_heads(2, 1)
    flip(2)
    keep(2, 0, 3)
    await_heads(3, 0)
    flip(3)

    def back_to(j, b):
        return pltpu.make_async_remote_copy(
            src_ref=att_s.at[j, pl.ds(pl.multiple_of(b * rows, rows), rows), :], dst_ref=att_r.at[j, mb],
            send_sem=bs.at[j, b], recv_sem=br.at[j, mb], device_id={"blk": b}, device_id_type=MESH)

    def back_from(j, b):
        return pltpu.make_async_remote_copy(
            src_ref=att_s.at[j, pl.ds(pl.multiple_of(b * rows, rows), rows), :], dst_ref=att_r.at[j, b],
            send_sem=bs.at[j, b], recv_sem=br.at[j, b], device_id={"blk": b}, device_id_type=MESH)

    def finished(k, c):
        if k == 3:
            unused, total, summed = begin(k, c, 0, 4)
        else:
            total, summed = more(k, c, 3 if k == 2 else 2, 4)
        return summed / total

    def finish(j):
        if j == 0:
            lower = [finished(2, c) for c in range(span // SUB)]
            await_heads(3, 1)
            upper = [finished(3, c) for c in range(span // SUB)]
        else:
            lower = [finished(1, c) for c in range(span // SUB)]
            upper = [finished(0, c) for c in range(span // SUB)]
        for c in range(span // SUB):
            both = jnp.concatenate([lower[c], upper[c]], axis=0)
            att_s[j, c * SUB : (c + 1) * SUB, :] = both.T.astype(jnp.bfloat16)

        def one(i, carry):
            back_to(j, lax.rem(mb + i, nb)).start()
            return carry

        lax.fori_loop(1, nb, one, 0)
        att_r[j, mb] = att_s[j, pl.ds(pl.multiple_of(mb * rows, rows), rows), :]

    def near_to(n):
        return pltpu.make_async_remote_copy(
            src_ref=part_s.at[1, n], dst_ref=near_r.at[n], send_sem=rs.at[1, n], recv_sem=rr.at[1, n],
            device_id={"uly": near}, device_id_type=MESH)

    def pair_to(k, n):
        return pltpu.make_async_remote_copy(
            src_ref=part_s.at[k, n], dst_ref=pair_r.at[k - 2, n], send_sem=rs.at[k, n], recv_sem=rr.at[k, n],
            device_id={"uly": near}, device_id_type=MESH)

    def far_to(k, n):
        return pltpu.make_async_remote_copy(
            src_ref=part_s.at[k, n], dst_ref=far_r.at[n], send_sem=rs.at[k, n], recv_sem=rr.at[0, n],
            device_id={"uly": inner if k == 2 else outer}, device_id_type=MESH)

    def project(j):
        for i in range(1, nb):
            back_from(j, lax.rem(mb + i, nb)).wait_recv()
        pieces = [att_r[j, h] for h in range(nb)]
        attended = jnp.concatenate(
            [
                jnp.concatenate([one[:, :width] for one in pieces], axis=1),
                jnp.concatenate([one[:, width:] for one in pieces], axis=1),
            ],
            axis=0,
        )
        for n in range(parts):
            part = jnp.dot(attended, wo_v[:, n * tile : (n + 1) * tile], preferred_element_type=jnp.float32)
            if j == 0:
                for k in (2, 3):
                    mine = part[(k - 2) * rows : (k - 1) * rows]
                    part_v[k, n] = mine
                    part_s[k, n] = mine.astype(jnp.bfloat16)

                @pl.when(jnp.logical_not(middle))
                def _():
                    for k in (2, 3):
                        pair_to(k, n).start()
            else:
                part_s[1, n] = part[:rows].astype(jnp.bfloat16)
                near_to(n).start()
                part_v[0, n] = part[rows:]

    finish(0)
    finish(1)
    loads[6].wait()
    loads[7].wait()
    project(0)
    project(1)

    @pl.when(middle)
    def _():
        for n in range(parts):
            for k in (2, 3):
                pair_to(k, n).wait_recv()
                part_s[k, n] = (part_v[k, n] + pair_r[k - 2, n].astype(jnp.float32)).astype(jnp.bfloat16)
                far_to(k, n).start()

    for n in range(parts):
        far_to(2, n).wait_recv()
        near_to(n).wait_recv()
        total = part_v[0, n] + near_r[n].astype(jnp.float32) + far_r[n].astype(jnp.float32)
        cols = slice(n * tile, (n + 1) * tile)
        out[:, cols] = (tok[:, cols].astype(jnp.float32) + gate[:, cols] * total).astype(jnp.bfloat16)

    for way in (0, 1):
        for c in range(chunks):
            gather(way, c).wait_send()

    @pl.when(middle)
    def _():
        for k in (2, 3):
            for c in range(chunks):
                forward(k, c).wait_send()

    def sent(i, carry):
        b = lax.rem(mb + 1 + lax.rem(i, nb - 1), nb)
        k = i // (nb - 1)
        heads_to(k, 0, b).wait_send()
        heads_to(k, 1, b).wait_send()
        return carry

    lax.fori_loop(0, 4 * (nb - 1), sent, 0)
    for j in (0, 1):
        for i in range(1, nb):
            back_to(j, lax.rem(mb + i, nb)).wait_send()
    for k in (1, 2, 3):
        for n in range(parts):
            near_to(n).wait_send() if k == 1 else pair_to(k, n).wait_send()


def fused(nb, tokens, mod_shift, mod_scale, mod_gate, w_query, w_key, w_value, w_out, score_gain):
    rows = tokens.shape[0]
    cols = w_query.shape[1]
    chunks = 4
    tile = 512
    parts = D // tile
    span = nb * rows
    bf16, f32 = jnp.bfloat16, jnp.float32
    vmem = pl.BlockSpec(memory_space=pltpu.VMEM)
    hbm = pl.BlockSpec(memory_space=pltpu.HBM)
    dma = pltpu.SemaphoreType.DMA
    return pl.pallas_call(
        functools.partial(kernel, nb),
        out_shape=jax.ShapeDtypeStruct((rows, D), bf16),
        in_specs=[hbm] * 9,
        out_specs=vmem,
        scratch_shapes=[
            pltpu.VMEM((rows, D), bf16),
            pltpu.VMEM((1, D), f32),
            pltpu.VMEM((1, D), f32),
            pltpu.VMEM((1, D), f32),
            pltpu.VMEM((1, HEADS), f32),
            pltpu.VMEM((4, chunks, rows, D // chunks), bf16),
            pltpu.VMEM((D, cols), bf16),
            pltpu.VMEM((D, cols), bf16),
            pltpu.VMEM((D, cols), bf16),
            pltpu.VMEM((cols, D), bf16),
            pltpu.VMEM((4, nb, rows, 128), bf16),
            pltpu.VMEM((4, nb, rows, 128), bf16),
            pltpu.VMEM((4 * span, 128), bf16),
            pltpu.VMEM((4 * span, 128), bf16),
            pltpu.VMEM((64, 4 * span), bf16),
            pltpu.VMEM((4, 1, span), f32),
            pltpu.VMEM((4, 1, span), f32),
            pltpu.VMEM((4, 64, span), f32),
            pltpu.VMEM((2, span, 128), bf16),
            pltpu.VMEM((2, nb, rows, 128), bf16),
            pltpu.VMEM((4, parts, rows, tile), f32),
            pltpu.VMEM((4, parts, rows, tile), bf16),
            pltpu.VMEM((2, parts, rows, tile), bf16),
            pltpu.VMEM((parts, rows, tile), bf16),
            pltpu.VMEM((parts, rows, tile), bf16),
            dma((9,)),
            dma((2, chunks)),
            dma((4, chunks)),
            dma((4, chunks)),
            dma((4, 2, nb)),
            dma((4, 2, nb)),
            dma((2, nb)),
            dma((2, nb)),
            dma((4, parts)),
            dma((4, parts)),
        ],
        compiler_params=pltpu.CompilerParams(
            collective_id=0, has_side_effects=True, vmem_limit_bytes=56 * 1024 * 1024
        ),
    )(
        tokens, mod_shift[None], mod_scale[None], mod_gate[None], score_gain[None],
        w_query, w_key, w_value, w_out,
    )


def modulate(tokens, mod_shift, mod_scale):
    values = tokens.astype(jnp.float32)
    center = values - jnp.mean(values, axis=-1, keepdims=True)
    spread = jnp.mean(center * center, axis=-1, keepdims=True)
    normed = center * lax.rsqrt(spread + 1e-06)
    return (normed * (1.0 + mod_scale) + mod_shift).astype(jnp.bfloat16)


def head_norm(projected, width):
    count = projected.shape[0]
    split = projected.reshape(count, -1, width)
    power = jnp.mean(split * split, axis=-1, keepdims=True)
    return (split * lax.rsqrt(power + 1e-06)).reshape(count, -1).astype(jnp.bfloat16)


def body(tokens, mod_shift, mod_scale, mod_gate, w_query, w_key, w_value, w_out, score_gain):
    width = D // HEADS
    local_cols = w_query.shape[1]
    local_heads = local_cols // width
    modded = modulate(tokens, mod_shift, mod_scale)
    piece = lax.all_gather(modded, "uly", axis=0, tiled=True)
    joined = jnp.concatenate(
        [
            jnp.dot(piece, w_query, preferred_element_type=jnp.float32),
            jnp.dot(piece, w_key, preferred_element_type=jnp.float32),
            jnp.dot(piece, w_value, preferred_element_type=jnp.float32),
        ],
        axis=1,
    )
    queries = head_norm(joined[:, :local_cols], width)
    keys = head_norm(joined[:, local_cols : 2 * local_cols], width)
    values = joined[:, 2 * local_cols :].astype(jnp.bfloat16)
    gains = lax.dynamic_slice_in_dim(score_gain, lax.axis_index("uly") * local_heads, local_heads)
    factors = gains / math.sqrt(width)
    rows = queries.shape[0]
    query_heads = queries.reshape(rows, local_heads, width)
    initial = (
        jnp.full((local_heads, rows), -jnp.inf, jnp.float32),
        jnp.zeros((local_heads, rows), jnp.float32),
        jnp.zeros((local_heads, rows, width), jnp.float32),
    )
    key_piece = lax.all_gather(keys, "blk", axis=0, tiled=True)
    value_piece = lax.all_gather(values, "blk", axis=0, tiled=True)
    count = key_piece.shape[0]
    groups = count // rows
    limit = max(rows, 1024)
    depth = max(
        [step for step in range(1, groups + 1) if groups % step == 0 and step * rows <= limit]
    )
    stride = depth * rows
    key_blocks = key_piece.reshape(count // stride, stride, local_heads, width)
    value_blocks = value_piece.reshape(count // stride, stride, local_heads, width)

    def one_block(carry, blocks):
        run_max, run_total, run_acc = carry
        key_block, value_block = blocks
        scores = jnp.einsum(
            "rhd,khd->hrk", query_heads, key_block, preferred_element_type=jnp.float32
        )
        scores = scores * factors[:, None, None]
        new_max = jnp.maximum(run_max, jnp.max(scores, axis=-1))
        expo = jnp.exp(scores - new_max[..., None])
        rescale = jnp.exp(run_max - new_max)
        new_total = run_total * rescale + jnp.sum(expo, axis=-1)
        summed = jnp.einsum(
            "hrk,khd->hrd",
            expo.astype(jnp.bfloat16),
            value_block,
            preferred_element_type=jnp.float32,
        )
        new_acc = run_acc * rescale[..., None] + summed
        return ((new_max, new_total, new_acc), None)

    result, unused = lax.scan(one_block, initial, (key_blocks, value_blocks))
    run_max, run_total, run_acc = result
    attended = (run_acc / run_total[..., None]).astype(jnp.bfloat16)
    attended = attended.transpose(1, 0, 2).reshape(rows, local_cols)
    returned = lax.all_to_all(attended, "uly", split_axis=0, concat_axis=1, tiled=True)
    projected = jnp.dot(
        returned,
        lax.all_gather(w_out, "uly", axis=0, tiled=True),
        preferred_element_type=jnp.float32,
    )
    return (tokens.astype(jnp.float32) + mod_gate * projected).astype(jnp.bfloat16)


def solution(mesh):
    in_specs = (
        P(("blk", "uly"), None),
        P(),
        P(),
        P(),
        P(None, "uly"),
        P(None, "uly"),
        P(None, "uly"),
        P("uly", None),
        P(),
    )
    out_specs = P(("blk", "uly"), None)
    nb, nz = mesh.shape["blk"], mesh.shape["uly"]
    run = body
    if HEADS == nb * nz and nz == 4:
        run = functools.partial(fused, nb)
    return jax.shard_map(run, mesh=mesh, in_specs=in_specs, out_specs=out_specs, check_vma=False)
```

```python
import functools
import math

import jax
import jax.numpy as jnp
from jax import lax
from jax.experimental import pallas as pl
from jax.experimental.pallas import tpu as pltpu
from jax.sharding import PartitionSpec as P

D = 2048
HEADS = 32
LOG2E = math.log2(math.e)
MESH = pl.DeviceIdType.MESH
SUB = 384


def kernel(
    nb, tok_h, shift_h, scale_h, gate_h, gain_h, wq, wk, wv, wo, out,
    tok, shift, scale, gate, gain, mod, wq_v, wk_v, wv_v, wo_v, kv_s, q_s, kv_r, q_r, vt, top_v, sum_v, acc_v,
    att_s, att_r, part_v, part_s, pair_r, near_r, far_r,
    wsem, gs, gr, fs, hs, hr, bs, br, rs, rr,
):
    width = D // HEADS
    rows = tok.shape[0]
    span = nb * rows
    chunks = mod.shape[1]
    deep = mod.shape[3]
    tile = part_s.shape[-1]
    parts = D // tile
    mb, mz = lax.axis_index("blk"), lax.axis_index("uly")
    high = mz // 2
    middle = (mz + 1) // 2 == 1
    near = mz + 1 - 2 * lax.rem(mz, 2)
    inner = 2 - high
    outer = 3 - 3 * high

    barrier = pltpu.get_barrier_semaphore()
    for z in (inner, near):
        pl.semaphore_signal(barrier, inc=1, device_id={"uly": z}, device_id_type=MESH)

    @pl.when(middle)
    def _():
        pl.semaphore_signal(barrier, inc=1, device_id={"uly": outer}, device_id_type=MESH)

    for j in range(1, nb):
        pl.semaphore_signal(barrier, inc=1, device_id={"blk": lax.rem(mb + j, nb)}, device_id_type=MESH)

    pairs = (
        (tok_h, tok), (shift_h, shift), (scale_h, scale), (wk, wk_v), (wv, wv_v), (wq, wq_v),
        (wo, wo_v), (gate_h, gate), (gain_h, gain),
    )
    loads = [
        pltpu.make_async_copy(src, dst, wsem.at[i])
        for i, (src, dst) in enumerate(pairs)
    ]
    for load in loads:
        load.start()
    for load in loads[:3]:
        load.wait()

    values = tok[...].astype(jnp.float32)
    center = values - jnp.mean(values, axis=-1, keepdims=True)
    spread = jnp.mean(center * center, axis=-1, keepdims=True)
    normed = center * lax.rsqrt(spread + 1e-06)
    modded = (normed * (1.0 + scale[...]) + shift[...]).astype(jnp.bfloat16)
    for c in range(chunks):
        mod[0, c] = modded[:, c * deep : (c + 1) * deep]

    pl.semaphore_wait(barrier, nb + 1 + middle.astype(jnp.int32))

    def gather(way, c):
        slot = 1 if way == 0 else 3 - middle.astype(jnp.int32)
        return pltpu.make_async_remote_copy(
            src_ref=mod.at[0, c], dst_ref=mod.at[slot, c], send_sem=gs.at[way, c], recv_sem=gr.at[slot, c],
            device_id={"uly": inner if way else near}, device_id_type=MESH)

    def landed(k, c):
        return pltpu.make_async_remote_copy(
            src_ref=mod.at[0, c], dst_ref=mod.at[k, c], send_sem=gs.at[0, c], recv_sem=gr.at[k, c],
            device_id={"uly": near}, device_id_type=MESH)

    def forward(k, c):
        return pltpu.make_async_remote_copy(
            src_ref=mod.at[k, c], dst_ref=mod.at[k, c], send_sem=fs.at[k, c], recv_sem=gr.at[k, c],
            device_id={"uly": near}, device_id_type=MESH)

    @pl.when(middle)
    def _():
        for c in range(chunks):
            for way in (0, 1):
                gather(way, c).start()

    @pl.when(jnp.logical_not(middle))
    def _():
        for way in (0, 1):
            for c in range(chunks):
                gather(way, c).start()

    for load in loads[3:6]:
        load.wait()

    def place(k, b):
        return pl.ds(pl.multiple_of(k * span + b * rows, rows), rows)

    def heads_to(k, kind, b):
        src, dst = ((kv_s, kv_r), (q_s, q_r))[kind]
        return pltpu.make_async_remote_copy(
            src_ref=src.at[k, b], dst_ref=dst.at[place(k, mb), :], send_sem=hs.at[k, kind, b],
            recv_sem=hr.at[k, kind, mb], device_id={"blk": b}, device_id_type=MESH)

    def heads_from(k, kind, b):
        src, dst = ((kv_s, kv_r), (q_s, q_r))[kind]
        return pltpu.make_async_remote_copy(
            src_ref=src.at[k, b], dst_ref=dst.at[place(k, b), :], send_sem=hs.at[k, kind, b],
            recv_sem=hr.at[k, kind, b], device_id={"blk": b}, device_id_type=MESH)

    loads[8].wait()
    chosen = lax.broadcasted_iota(jnp.int32, gain.shape, 1) == mz * nb + mb
    factor = jnp.sum(jnp.where(chosen, gain[...], 0.0), axis=-1, keepdims=True) * (LOG2E / math.sqrt(width))

    def await_heads(k, kind):
        for j in range(1, nb):
            heads_from(k, kind, lax.rem(mb + j, nb)).wait_recv()

    def flip(k):
        vt[:, k * span : (k + 1) * span] = kv_r[k * span : (k + 1) * span, :].T[width:, :]

    def scored(k, c, first, last):
        q = q_r[k * span + c * SUB : k * span + (c + 1) * SUB, :]
        return lax.dot_general(
            kv_r[first * span : last * span, :], q, (((1,), (1,)), ((), ())), preferred_element_type=jnp.float32)

    def begin(k, c, first, last):
        scores = scored(k, c, first, last)
        top = jnp.max(scores, axis=0, keepdims=True)
        expo = jnp.exp2((scores - top) * factor)
        total = jnp.sum(expo, axis=0, keepdims=True)
        summed = jnp.dot(vt[:, first * span : last * span], expo.astype(jnp.bfloat16), preferred_element_type=jnp.float32)
        return top, total, summed

    def keep(k, first, last):
        for c in range(span // SUB):
            cols = slice(c * SUB, (c + 1) * SUB)
            top_v[k, :, cols], sum_v[k, :, cols], acc_v[k, :, cols] = begin(k, c, first, last)

    def more(k, c, first, last):
        cols = slice(c * SUB, (c + 1) * SUB)
        scores = scored(k, c, first, last)
        old = top_v[k, :, cols]
        top = jnp.maximum(old, jnp.max(scores, axis=0, keepdims=True))
        shrink = jnp.exp2((old - top) * factor)
        expo = jnp.exp2((scores - top) * factor)
        total = sum_v[k, :, cols] * shrink + jnp.sum(expo, axis=0, keepdims=True)
        summed = jnp.dot(vt[:, first * span : last * span], expo.astype(jnp.bfloat16), preferred_element_type=jnp.float32)
        return total, acc_v[k, :, cols] * shrink + summed

    def first_attend():
        for k in (0, 1):
            await_heads(k, 0)
            await_heads(k, 1)
            flip(k)
        for k in (0, 1):
            keep(k, 0, 2)

    def piece(k, carry):
        @pl.when((k == 3) & jnp.logical_not(middle))
        def _():
            first_attend()

        query = key = value = None
        for c in range(chunks):
            @pl.when((k > 0) & (jnp.logical_not(middle) | (k == 1)))
            def _():
                landed(k, c).wait_recv()

            @pl.when(middle & (k > 0) & (k < 3))
            def _():
                landed(k + 1, c).wait_recv()
                forward(k + 1, c).start()

            x = mod[k, c]
            deeps = slice(c * deep, (c + 1) * deep)
            more_k = jnp.dot(x, wk_v[deeps, :], preferred_element_type=jnp.float32)
            more_v = jnp.dot(x, wv_v[deeps, :], preferred_element_type=jnp.float32)
            more_q = jnp.dot(x, wq_v[deeps, :], preferred_element_type=jnp.float32)
            key = more_k if c == 0 else key + more_k
            value = more_v if c == 0 else value + more_v
            query = more_q if c == 0 else query + more_q

        def unit(part):
            power = jnp.mean(part * part, axis=-1, keepdims=True)
            return part * lax.rsqrt(power + 1e-06)

        def send(kind):
            def one(j, carry):
                heads_to(k, kind, lax.rem(mb + j, nb)).start()
                return carry

            lax.fori_loop(1, nb, one, 0)

        for h in range(nb):
            cols = slice(h * width, (h + 1) * width)
            kv_s[k, h] = jnp.concatenate([unit(key[:, cols]), value[:, cols]], axis=1).astype(jnp.bfloat16)
        send(0)
        kv_r[place(k, mb), :] = kv_s[k, mb]
        for h in range(nb):
            cols = slice(h * width, (h + 1) * width)
            line = unit(query[:, cols])
            q_s[k, h] = jnp.concatenate([line, jnp.zeros_like(line)], axis=1).astype(jnp.bfloat16)
        send(1)
        q_r[place(k, mb), :] = q_s[k, mb]
        return carry

    lax.fori_loop(0, 4, piece, 0)

    @pl.when(middle)
    def _():
        first_attend()

    await_heads(2, 0)
    await_heads(2, 1)
    flip(2)
    keep(2, 0, 3)
    await_heads(3, 0)
    flip(3)

    def back_to(j, b):
        return pltpu.make_async_remote_copy(
            src_ref=att_s.at[j, pl.ds(pl.multiple_of(b * rows, rows), rows), :], dst_ref=att_r.at[j, mb],
            send_sem=bs.at[j, b], recv_sem=br.at[j, mb], device_id={"blk": b}, device_id_type=MESH)

    def back_from(j, b):
        return pltpu.make_async_remote_copy(
            src_ref=att_s.at[j, pl.ds(pl.multiple_of(b * rows, rows), rows), :], dst_ref=att_r.at[j, b],
            send_sem=bs.at[j, b], recv_sem=br.at[j, b], device_id={"blk": b}, device_id_type=MESH)

    def finished(k, c):
        if k == 3:
            unused, total, summed = begin(k, c, 0, 4)
        else:
            total, summed = more(k, c, 3 if k == 2 else 2, 4)
        return summed / total

    def finish(j):
        if j == 0:
            lower = [finished(2, c) for c in range(span // SUB)]
            await_heads(3, 1)
            upper = [finished(3, c) for c in range(span // SUB)]
        else:
            lower = [finished(1, c) for c in range(span // SUB)]
            upper = [finished(0, c) for c in range(span // SUB)]
        for c in range(span // SUB):
            both = jnp.concatenate([lower[c], upper[c]], axis=0)
            att_s[j, c * SUB : (c + 1) * SUB, :] = both.T.astype(jnp.bfloat16)

        def one(i, carry):
            back_to(j, lax.rem(mb + i, nb)).start()
            return carry

        lax.fori_loop(1, nb, one, 0)
        att_r[j, mb] = att_s[j, pl.ds(pl.multiple_of(mb * rows, rows), rows), :]

    def near_to(n):
        return pltpu.make_async_remote_copy(
            src_ref=part_s.at[1, n], dst_ref=near_r.at[n], send_sem=rs.at[1, n], recv_sem=rr.at[1, n],
            device_id={"uly": near}, device_id_type=MESH)

    def pair_to(k, n):
        return pltpu.make_async_remote_copy(
            src_ref=part_s.at[k, n], dst_ref=pair_r.at[k - 2, n], send_sem=rs.at[k, n], recv_sem=rr.at[k, n],
            device_id={"uly": near}, device_id_type=MESH)

    def far_to(k, n):
        return pltpu.make_async_remote_copy(
            src_ref=part_s.at[k, n], dst_ref=far_r.at[n], send_sem=rs.at[k, n], recv_sem=rr.at[0, n],
            device_id={"uly": inner if k == 2 else outer}, device_id_type=MESH)

    def project(j):
        for i in range(1, nb):
            back_from(j, lax.rem(mb + i, nb)).wait_recv()
        pieces = [att_r[j, h] for h in range(nb)]
        attended = jnp.concatenate(
            [
                jnp.concatenate([one[:, :width] for one in pieces], axis=1),
                jnp.concatenate([one[:, width:] for one in pieces], axis=1),
            ],
            axis=0,
        )
        for n in range(parts):
            part = jnp.dot(attended, wo_v[:, n * tile : (n + 1) * tile], preferred_element_type=jnp.float32)
            if j == 0:
                for k in (2, 3):
                    mine = part[(k - 2) * rows : (k - 1) * rows]
                    part_v[k, n] = mine
                    part_s[k, n] = mine.astype(jnp.bfloat16)

                @pl.when(jnp.logical_not(middle))
                def _():
                    pair_to(3, n).start()
            else:
                part_s[1, n] = part[:rows].astype(jnp.bfloat16)
                near_to(n).start()
                part_v[0, n] = part[rows:]
        if j == 0:
            @pl.when(jnp.logical_not(middle))
            def _():
                for n in range(parts):
                    pair_to(2, n).start()

    finish(0)
    finish(1)
    loads[6].wait()
    loads[7].wait()
    project(0)
    project(1)

    @pl.when(middle)
    def _():
        for k in (3, 2):
            for n in range(parts):
                pair_to(k, n).wait_recv()
                part_s[k, n] = (part_v[k, n] + pair_r[k - 2, n].astype(jnp.float32)).astype(jnp.bfloat16)
                far_to(k, n).start()

    for n in range(parts):
        far_to(2, n).wait_recv()
        near_to(n).wait_recv()
        total = part_v[0, n] + near_r[n].astype(jnp.float32) + far_r[n].astype(jnp.float32)
        cols = slice(n * tile, (n + 1) * tile)
        out[:, cols] = (tok[:, cols].astype(jnp.float32) + gate[:, cols] * total).astype(jnp.bfloat16)

    for way in (0, 1):
        for c in range(chunks):
            gather(way, c).wait_send()

    @pl.when(middle)
    def _():
        for k in (2, 3):
            for c in range(chunks):
                forward(k, c).wait_send()

    def sent(i, carry):
        b = lax.rem(mb + 1 + lax.rem(i, nb - 1), nb)
        k = i // (nb - 1)
        heads_to(k, 0, b).wait_send()
        heads_to(k, 1, b).wait_send()
        return carry

    lax.fori_loop(0, 4 * (nb - 1), sent, 0)
    for j in (0, 1):
        for i in range(1, nb):
            back_to(j, lax.rem(mb + i, nb)).wait_send()
    for k in (1, 2, 3):
        for n in range(parts):
            near_to(n).wait_send() if k == 1 else pair_to(k, n).wait_send()


def fused(nb, tokens, mod_shift, mod_scale, mod_gate, w_query, w_key, w_value, w_out, score_gain):
    rows = tokens.shape[0]
    cols = w_query.shape[1]
    chunks = 4
    tile = 512
    parts = D // tile
    span = nb * rows
    bf16, f32 = jnp.bfloat16, jnp.float32
    vmem = pl.BlockSpec(memory_space=pltpu.VMEM)
    hbm = pl.BlockSpec(memory_space=pltpu.HBM)
    dma = pltpu.SemaphoreType.DMA
    return pl.pallas_call(
        functools.partial(kernel, nb),
        out_shape=jax.ShapeDtypeStruct((rows, D), bf16),
        in_specs=[hbm] * 9,
        out_specs=vmem,
        scratch_shapes=[
            pltpu.VMEM((rows, D), bf16),
            pltpu.VMEM((1, D), f32),
            pltpu.VMEM((1, D), f32),
            pltpu.VMEM((1, D), f32),
            pltpu.VMEM((1, HEADS), f32),
            pltpu.VMEM((4, chunks, rows, D // chunks), bf16),
            pltpu.VMEM((D, cols), bf16),
            pltpu.VMEM((D, cols), bf16),
            pltpu.VMEM((D, cols), bf16),
            pltpu.VMEM((cols, D), bf16),
            pltpu.VMEM((4, nb, rows, 128), bf16),
            pltpu.VMEM((4, nb, rows, 128), bf16),
            pltpu.VMEM((4 * span, 128), bf16),
            pltpu.VMEM((4 * span, 128), bf16),
            pltpu.VMEM((64, 4 * span), bf16),
            pltpu.VMEM((4, 1, span), f32),
            pltpu.VMEM((4, 1, span), f32),
            pltpu.VMEM((4, 64, span), f32),
            pltpu.VMEM((2, span, 128), bf16),
            pltpu.VMEM((2, nb, rows, 128), bf16),
            pltpu.VMEM((4, parts, rows, tile), f32),
            pltpu.VMEM((4, parts, rows, tile), bf16),
            pltpu.VMEM((2, parts, rows, tile), bf16),
            pltpu.VMEM((parts, rows, tile), bf16),
            pltpu.VMEM((parts, rows, tile), bf16),
            dma((9,)),
            dma((2, chunks)),
            dma((4, chunks)),
            dma((4, chunks)),
            dma((4, 2, nb)),
            dma((4, 2, nb)),
            dma((2, nb)),
            dma((2, nb)),
            dma((4, parts)),
            dma((4, parts)),
        ],
        compiler_params=pltpu.CompilerParams(
            collective_id=0, has_side_effects=True, vmem_limit_bytes=56 * 1024 * 1024
        ),
    )(
        tokens, mod_shift[None], mod_scale[None], mod_gate[None], score_gain[None],
        w_query, w_key, w_value, w_out,
    )


def modulate(tokens, mod_shift, mod_scale):
    values = tokens.astype(jnp.float32)
    center = values - jnp.mean(values, axis=-1, keepdims=True)
    spread = jnp.mean(center * center, axis=-1, keepdims=True)
    normed = center * lax.rsqrt(spread + 1e-06)
    return (normed * (1.0 + mod_scale) + mod_shift).astype(jnp.bfloat16)


def head_norm(projected, width):
    count = projected.shape[0]
    split = projected.reshape(count, -1, width)
    power = jnp.mean(split * split, axis=-1, keepdims=True)
    return (split * lax.rsqrt(power + 1e-06)).reshape(count, -1).astype(jnp.bfloat16)


def body(tokens, mod_shift, mod_scale, mod_gate, w_query, w_key, w_value, w_out, score_gain):
    width = D // HEADS
    local_cols = w_query.shape[1]
    local_heads = local_cols // width
    modded = modulate(tokens, mod_shift, mod_scale)
    piece = lax.all_gather(modded, "uly", axis=0, tiled=True)
    joined = jnp.concatenate(
        [
            jnp.dot(piece, w_query, preferred_element_type=jnp.float32),
            jnp.dot(piece, w_key, preferred_element_type=jnp.float32),
            jnp.dot(piece, w_value, preferred_element_type=jnp.float32),
        ],
        axis=1,
    )
    queries = head_norm(joined[:, :local_cols], width)
    keys = head_norm(joined[:, local_cols : 2 * local_cols], width)
    values = joined[:, 2 * local_cols :].astype(jnp.bfloat16)
    gains = lax.dynamic_slice_in_dim(score_gain, lax.axis_index("uly") * local_heads, local_heads)
    factors = gains / math.sqrt(width)
    rows = queries.shape[0]
    query_heads = queries.reshape(rows, local_heads, width)
    initial = (
        jnp.full((local_heads, rows), -jnp.inf, jnp.float32),
        jnp.zeros((local_heads, rows), jnp.float32),
        jnp.zeros((local_heads, rows, width), jnp.float32),
    )
    key_piece = lax.all_gather(keys, "blk", axis=0, tiled=True)
    value_piece = lax.all_gather(values, "blk", axis=0, tiled=True)
    count = key_piece.shape[0]
    groups = count // rows
    limit = max(rows, 1024)
    depth = max(
        [step for step in range(1, groups + 1) if groups % step == 0 and step * rows <= limit]
    )
    stride = depth * rows
    key_blocks = key_piece.reshape(count // stride, stride, local_heads, width)
    value_blocks = value_piece.reshape(count // stride, stride, local_heads, width)

    def one_block(carry, blocks):
        run_max, run_total, run_acc = carry
        key_block, value_block = blocks
        scores = jnp.einsum(
            "rhd,khd->hrk", query_heads, key_block, preferred_element_type=jnp.float32
        )
        scores = scores * factors[:, None, None]
        new_max = jnp.maximum(run_max, jnp.max(scores, axis=-1))
        expo = jnp.exp(scores - new_max[..., None])
        rescale = jnp.exp(run_max - new_max)
        new_total = run_total * rescale + jnp.sum(expo, axis=-1)
        summed = jnp.einsum(
            "hrk,khd->hrd",
            expo.astype(jnp.bfloat16),
            value_block,
            preferred_element_type=jnp.float32,
        )
        new_acc = run_acc * rescale[..., None] + summed
        return ((new_max, new_total, new_acc), None)

    result, unused = lax.scan(one_block, initial, (key_blocks, value_blocks))
    run_max, run_total, run_acc = result
    attended = (run_acc / run_total[..., None]).astype(jnp.bfloat16)
    attended = attended.transpose(1, 0, 2).reshape(rows, local_cols)
    returned = lax.all_to_all(attended, "uly", split_axis=0, concat_axis=1, tiled=True)
    projected = jnp.dot(
        returned,
        lax.all_gather(w_out, "uly", axis=0, tiled=True),
        preferred_element_type=jnp.float32,
    )
    return (tokens.astype(jnp.float32) + mod_gate * projected).astype(jnp.bfloat16)


def solution(mesh):
    in_specs = (
        P(("blk", "uly"), None),
        P(),
        P(),
        P(),
        P(None, "uly"),
        P(None, "uly"),
        P(None, "uly"),
        P("uly", None),
        P(),
    )
    out_specs = P(("blk", "uly"), None)
    nb, nz = mesh.shape["blk"], mesh.shape["uly"]
    run = body
    if HEADS == nb * nz and nz == 4:
        run = functools.partial(fused, nb)
    return jax.shard_map(run, mesh=mesh, in_specs=in_specs, out_specs=out_specs, check_vma=False)
```

```python
import functools
import math

import jax
import jax.numpy as jnp
from jax import lax
from jax.experimental import pallas as pl
from jax.experimental.pallas import tpu as pltpu
from jax.sharding import PartitionSpec as P

D = 2048
HEADS = 32
LOG2E = math.log2(math.e)
MESH = pl.DeviceIdType.MESH
SUB = 384
TWIN = 1024


def kernel(
    nb, tok_h, shift_h, scale_h, gate_h, gain_h, wq, wk, wv, wo, out,
    tok, shift, scale, gate, gain, mod, wq_v, wk_v, wv_v, wo_v, kv_s, q_s, kv_r, q_r, vt, top_v, sum_v, acc_v,
    att_s, att_r, full_v, full_r, twin_v, part_v, part_s, pair_r, near_r, far_r,
    wsem, gs, gr, fs, hs, hr, bs, br, rs, rr, es, er, ts, tr,
):
    width = D // HEADS
    rows = tok.shape[0]
    span = nb * rows
    chunks = mod.shape[1]
    deep = mod.shape[3]
    tile = part_s.shape[-1]
    parts = D // tile
    apart = parts - twin_v.shape[1] // tile
    mb, mz = lax.axis_index("blk"), lax.axis_index("uly")
    high = mz // 2
    middle = (mz + 1) // 2 == 1
    near = mz + 1 - 2 * lax.rem(mz, 2)
    inner = 2 - high
    outer = 3 - 3 * high

    barrier = pltpu.get_barrier_semaphore()
    for z in (inner, near):
        pl.semaphore_signal(barrier, inc=1, device_id={"uly": z}, device_id_type=MESH)

    @pl.when(middle)
    def _():
        pl.semaphore_signal(barrier, inc=1, device_id={"uly": outer}, device_id_type=MESH)

    for j in range(1, nb):
        pl.semaphore_signal(barrier, inc=1, device_id={"blk": lax.rem(mb + j, nb)}, device_id_type=MESH)

    pairs = (
        (tok_h, tok), (shift_h, shift), (scale_h, scale), (wk, wk_v), (wv, wv_v), (wq, wq_v),
        (wo, wo_v), (gate_h, gate), (gain_h, gain),
    )
    loads = [
        pltpu.make_async_copy(src, dst, wsem.at[i])
        for i, (src, dst) in enumerate(pairs)
    ]
    for load in loads:
        load.start()
    for load in loads[:3]:
        load.wait()

    values = tok[...].astype(jnp.float32)
    center = values - jnp.mean(values, axis=-1, keepdims=True)
    spread = jnp.mean(center * center, axis=-1, keepdims=True)
    normed = center * lax.rsqrt(spread + 1e-06)
    modded = (normed * (1.0 + scale[...]) + shift[...]).astype(jnp.bfloat16)
    for c in range(chunks):
        mod[0, c] = modded[:, c * deep : (c + 1) * deep]

    pl.semaphore_wait(barrier, nb + 1 + middle.astype(jnp.int32))

    def gather(way, c):
        slot = 1 if way == 0 else 3 - middle.astype(jnp.int32)
        return pltpu.make_async_remote_copy(
            src_ref=mod.at[0, c], dst_ref=mod.at[slot, c], send_sem=gs.at[way, c], recv_sem=gr.at[slot, c],
            device_id={"uly": inner if way else near}, device_id_type=MESH)

    def landed(k, c):
        return pltpu.make_async_remote_copy(
            src_ref=mod.at[0, c], dst_ref=mod.at[k, c], send_sem=gs.at[0, c], recv_sem=gr.at[k, c],
            device_id={"uly": near}, device_id_type=MESH)

    def forward(k, c):
        return pltpu.make_async_remote_copy(
            src_ref=mod.at[k, c], dst_ref=mod.at[k, c], send_sem=fs.at[k, c], recv_sem=gr.at[k, c],
            device_id={"uly": near}, device_id_type=MESH)

    @pl.when(middle)
    def _():
        for c in range(chunks):
            for way in (0, 1):
                gather(way, c).start()

    @pl.when(jnp.logical_not(middle))
    def _():
        for way in (0, 1):
            for c in range(chunks):
                gather(way, c).start()

    for load in loads[3:6]:
        load.wait()

    def place(k, b):
        return pl.ds(pl.multiple_of(k * span + b * rows, rows), rows)

    depth = wo_v.shape[0] // nb
    sibling = mb + 1 - 2 * lax.rem(mb, 2)

    def slab(b):
        return pl.ds(pl.multiple_of(b * depth, depth), depth)

    def twin_out():
        return pltpu.make_async_remote_copy(
            src_ref=wo_v.at[slab(mb), apart * tile :], dst_ref=twin_v.at[slab(mb), :], send_sem=ts.at[0, 0],
            recv_sem=tr.at[mb], device_id={"uly": near}, device_id_type=MESH)

    def twin_in(b):
        return pltpu.make_async_remote_copy(
            src_ref=twin_v.at[slab(b), :], dst_ref=twin_v.at[slab(b), :], send_sem=ts.at[0, 0],
            recv_sem=tr.at[b], device_id={"uly": near}, device_id_type=MESH)

    def twin_share(j):
        return pltpu.make_async_remote_copy(
            src_ref=twin_v.at[slab(mb), :], dst_ref=twin_v.at[slab(mb), :], send_sem=ts.at[0, j],
            recv_sem=tr.at[mb], device_id={"blk": sibling if j == 0 else lax.rem(mb + 2 * j, nb)}, device_id_type=MESH)

    def twin_pass(j):
        b = lax.rem(mb + 2 * j, nb)
        return pltpu.make_async_remote_copy(
            src_ref=twin_v.at[slab(b), :], dst_ref=twin_v.at[slab(b), :], send_sem=ts.at[1, j],
            recv_sem=tr.at[b], device_id={"blk": sibling}, device_id_type=MESH)

    def full_to(k):
        return pltpu.make_async_remote_copy(
            src_ref=full_v.at[k], dst_ref=full_r.at[k], send_sem=es.at[k], recv_sem=er.at[k],
            device_id={"uly": near}, device_id_type=MESH)

    def heads_to(k, kind, b):
        src, dst = ((kv_s, kv_r), (q_s, q_r))[kind]
        return pltpu.make_async_remote_copy(
            src_ref=src.at[k, b], dst_ref=dst.at[place(k, mb), :], send_sem=hs.at[k, kind, b],
            recv_sem=hr.at[k, kind, mb], device_id={"blk": b}, device_id_type=MESH)

    def heads_from(k, kind, b):
        src, dst = ((kv_s, kv_r), (q_s, q_r))[kind]
        return pltpu.make_async_remote_copy(
            src_ref=src.at[k, b], dst_ref=dst.at[place(k, b), :], send_sem=hs.at[k, kind, b],
            recv_sem=hr.at[k, kind, b], device_id={"blk": b}, device_id_type=MESH)

    loads[8].wait()
    chosen = lax.broadcasted_iota(jnp.int32, gain.shape, 1) == mz * nb + mb
    factor = jnp.sum(jnp.where(chosen, gain[...], 0.0), axis=-1, keepdims=True) * (LOG2E / math.sqrt(width))

    def await_heads(k, kind):
        for j in range(1, nb):
            heads_from(k, kind, lax.rem(mb + j, nb)).wait_recv()

    def flip(k):
        vt[:, k * span : (k + 1) * span] = kv_r[k * span : (k + 1) * span, :].T[width:, :]

    def scored(k, c, first, last):
        q = q_r[k * span + c * SUB : k * span + (c + 1) * SUB, :]
        return lax.dot_general(
            kv_r[first * span : last * span, :], q, (((1,), (1,)), ((), ())), preferred_element_type=jnp.float32)

    def begin(k, c, first, last):
        scores = scored(k, c, first, last)
        top = jnp.max(scores, axis=0, keepdims=True)
        expo = jnp.exp2((scores - top) * factor)
        total = jnp.sum(expo, axis=0, keepdims=True)
        summed = jnp.dot(vt[:, first * span : last * span], expo.astype(jnp.bfloat16), preferred_element_type=jnp.float32)
        return top, total, summed

    def keep(k, first, last):
        for c in range(span // SUB):
            cols = slice(c * SUB, (c + 1) * SUB)
            top_v[k, :, cols], sum_v[k, :, cols], acc_v[k, :, cols] = begin(k, c, first, last)

    def more(k, c, first, last):
        cols = slice(c * SUB, (c + 1) * SUB)
        scores = scored(k, c, first, last)
        old = top_v[k, :, cols]
        top = jnp.maximum(old, jnp.max(scores, axis=0, keepdims=True))
        shrink = jnp.exp2((old - top) * factor)
        expo = jnp.exp2((scores - top) * factor)
        total = sum_v[k, :, cols] * shrink + jnp.sum(expo, axis=0, keepdims=True)
        summed = jnp.dot(vt[:, first * span : last * span], expo.astype(jnp.bfloat16), preferred_element_type=jnp.float32)
        return total, acc_v[k, :, cols] * shrink + summed

    def first_attend():
        for k in (0, 1):
            await_heads(k, 0)
            await_heads(k, 1)
            flip(k)
        for k in (0, 1):
            keep(k, 0, 2)

    def piece(k, carry):
        @pl.when((k == 3) & jnp.logical_not(middle))
        def _():
            first_attend()

        @pl.when((k == 1) & jnp.logical_not(middle))
        def _():
            loads[6].wait()
            twin_out().start()

        query = key = value = None
        for c in range(chunks):
            @pl.when((k > 0) & (jnp.logical_not(middle) | (k == 1)))
            def _():
                landed(k, c).wait_recv()

            @pl.when(middle & (k > 0) & (k < 3))
            def _():
                landed(k + 1, c).wait_recv()
                forward(k + 1, c).start()

            x = mod[k, c]
            deeps = slice(c * deep, (c + 1) * deep)
            more_k = jnp.dot(x, wk_v[deeps, :], preferred_element_type=jnp.float32)
            more_v = jnp.dot(x, wv_v[deeps, :], preferred_element_type=jnp.float32)
            more_q = jnp.dot(x, wq_v[deeps, :], preferred_element_type=jnp.float32)
            key = more_k if c == 0 else key + more_k
            value = more_v if c == 0 else value + more_v
            query = more_q if c == 0 else query + more_q

        def unit(part):
            power = jnp.mean(part * part, axis=-1, keepdims=True)
            return part * lax.rsqrt(power + 1e-06)

        def send(kind):
            def one(j, carry):
                heads_to(k, kind, lax.rem(mb + j, nb)).start()
                return carry

            lax.fori_loop(1, nb, one, 0)

        for h in range(nb):
            cols = slice(h * width, (h + 1) * width)
            kv_s[k, h] = jnp.concatenate([unit(key[:, cols]), value[:, cols]], axis=1).astype(jnp.bfloat16)
        send(0)
        kv_r[place(k, mb), :] = kv_s[k, mb]
        for h in range(nb):
            cols = slice(h * width, (h + 1) * width)
            line = unit(query[:, cols])
            q_s[k, h] = jnp.concatenate([line, jnp.zeros_like(line)], axis=1).astype(jnp.bfloat16)
        send(1)
        q_r[place(k, mb), :] = q_s[k, mb]
        return carry

    lax.fori_loop(0, 4, piece, 0)

    @pl.when(middle)
    def _():
        loads[6].wait()
        twin_in(mb).wait_recv()
        for j in range(1, nb // 2):
            twin_share(j).start()
        twin_share(0).start()
        first_attend()

    await_heads(2, 0)
    await_heads(2, 1)
    flip(2)
    keep(2, 0, 3)
    await_heads(3, 0)
    flip(3)

    def back_to(j, b):
        return pltpu.make_async_remote_copy(
            src_ref=att_s.at[j, pl.ds(pl.multiple_of(b * rows, rows), rows), :], dst_ref=att_r.at[j, mb],
            send_sem=bs.at[j, b], recv_sem=br.at[j, mb], device_id={"blk": b}, device_id_type=MESH)

    def back_from(j, b):
        return pltpu.make_async_remote_copy(
            src_ref=att_s.at[j, pl.ds(pl.multiple_of(b * rows, rows), rows), :], dst_ref=att_r.at[j, b],
            send_sem=bs.at[j, b], recv_sem=br.at[j, b], device_id={"blk": b}, device_id_type=MESH)

    def finished(k, c):
        if k == 3:
            unused, total, summed = begin(k, c, 0, 4)
        else:
            total, summed = more(k, c, 3 if k == 2 else 2, 4)
        return summed / total

    def finish(j):
        if j == 0:
            lower = [finished(2, c) for c in range(span // SUB)]
            await_heads(3, 1)
            upper = [finished(3, c) for c in range(span // SUB)]
        else:
            lower = [finished(1, c) for c in range(span // SUB)]
            upper = [finished(0, c) for c in range(span // SUB)]
        for c in range(span // SUB):
            both = jnp.concatenate([lower[c], upper[c]], axis=0)
            att_s[j, c * SUB : (c + 1) * SUB, :] = both.T.astype(jnp.bfloat16)

        def one(i, carry):
            back_to(j, lax.rem(mb + i, nb)).start()
            return carry

        lax.fori_loop(1, nb, one, 0)
        att_r[j, mb] = att_s[j, pl.ds(pl.multiple_of(mb * rows, rows), rows), :]

    def near_to(n):
        return pltpu.make_async_remote_copy(
            src_ref=part_s.at[1, n], dst_ref=near_r.at[n], send_sem=rs.at[1, n], recv_sem=rr.at[1, n],
            device_id={"uly": near}, device_id_type=MESH)

    def pair_to(k, n):
        return pltpu.make_async_remote_copy(
            src_ref=part_s.at[k, n], dst_ref=pair_r.at[k - 2, n], send_sem=rs.at[k, n], recv_sem=rr.at[k, n],
            device_id={"uly": near}, device_id_type=MESH)

    def far_to(k, n):
        return pltpu.make_async_remote_copy(
            src_ref=part_s.at[k, n], dst_ref=far_r.at[n], send_sem=rs.at[k, n], recv_sem=rr.at[0, n],
            device_id={"uly": inner if k == 2 else outer}, device_id_type=MESH)

    def project(j):
        for i in range(1, nb):
            back_from(j, lax.rem(mb + i, nb)).wait_recv()
        pieces = [att_r[j, h] for h in range(nb)]
        attended = jnp.concatenate(
            [
                jnp.concatenate([one[:, :width] for one in pieces], axis=1),
                jnp.concatenate([one[:, width:] for one in pieces], axis=1),
            ],
            axis=0,
        )
        if j == 0:
            full_v[2] = attended[:rows]
            full_v[3] = attended[rows:]
        else:
            full_v[1] = attended[:rows]

        @pl.when(jnp.logical_not(middle))
        def _():
            full_to(3 if j == 0 else 1).start()

        for n in range(apart):
            part = jnp.dot(attended, wo_v[:, n * tile : (n + 1) * tile], preferred_element_type=jnp.float32)
            if j == 0:
                for k in (2, 3):
                    mine = part[(k - 2) * rows : (k - 1) * rows]
                    part_v[k, n] = mine
                    part_s[k, n] = mine.astype(jnp.bfloat16)

                @pl.when(jnp.logical_not(middle))
                def _():
                    pair_to(3, n).start()
            else:
                part_s[1, n] = part[:rows].astype(jnp.bfloat16)
                near_to(n).start()
                part_v[0, n] = part[rows:]
        if j == 0:
            @pl.when(jnp.logical_not(middle))
            def _():
                full_to(2).start()
                for n in range(apart):
                    pair_to(2, n).start()

            @pl.when(middle)
            def _():
                for n in range(apart, parts):
                    part = jnp.dot(attended, wo_v[:, n * tile : (n + 1) * tile], preferred_element_type=jnp.float32)
                    for k in (2, 3):
                        part_v[k, n] = part[(k - 2) * rows : (k - 1) * rows]
        else:
            for n in range(apart, parts):
                part = jnp.dot(attended, wo_v[:, n * tile : (n + 1) * tile], preferred_element_type=jnp.float32)
                part_s[1, n] = part[:rows].astype(jnp.bfloat16)

                @pl.when(middle)
                def _():
                    near_to(n).start()

                part_v[0, n] = part[rows:]

    finish(0)
    finish(1)

    @pl.when(middle)
    def _():
        for j in range(1, nb // 2):
            twin_in(lax.rem(mb + 2 * j, nb)).wait_recv()
            twin_pass(j).start()

    loads[7].wait()
    project(0)
    project(1)

    def twin(k, n):
        cols = slice((n - apart) * tile, (n - apart + 1) * tile)
        return jnp.dot(full_r[k], twin_v[:, cols], preferred_element_type=jnp.float32)

    @pl.when(middle)
    def _():
        twin_in(sibling).wait_recv()
        for j in range(1, nb // 2):
            twin_in(lax.rem(sibling + 2 * j, nb)).wait_recv()
        for k in (3, 2):
            full_to(k).wait_recv()
            for n in range(apart, parts):
                part_s[k, n] = (part_v[k, n] + twin(k, n)).astype(jnp.bfloat16)
                far_to(k, n).start()
            for n in range(apart):
                pair_to(k, n).wait_recv()
                part_s[k, n] = (part_v[k, n] + pair_r[k - 2, n].astype(jnp.float32)).astype(jnp.bfloat16)
                far_to(k, n).start()
        full_to(1).wait_recv()
        for n in range(apart, parts):
            part_v[0, n] += twin(1, n)

    def settle(n, extra):
        total = part_v[0, n] + far_r[n].astype(jnp.float32)
        if extra:
            total = total + near_r[n].astype(jnp.float32)
        cols = slice(n * tile, (n + 1) * tile)
        out[:, cols] = (tok[:, cols].astype(jnp.float32) + gate[:, cols] * total).astype(jnp.bfloat16)

    for n in range(apart, parts):
        far_to(2, n).wait_recv()

        @pl.when(middle)
        def _():
            settle(n, False)

        @pl.when(jnp.logical_not(middle))
        def _():
            near_to(n).wait_recv()
            settle(n, True)

    for n in range(apart):
        far_to(2, n).wait_recv()
        near_to(n).wait_recv()
        settle(n, True)

    for way in (0, 1):
        for c in range(chunks):
            gather(way, c).wait_send()

    @pl.when(middle)
    def _():
        for k in (2, 3):
            for c in range(chunks):
                forward(k, c).wait_send()

    def sent(i, carry):
        b = lax.rem(mb + 1 + lax.rem(i, nb - 1), nb)
        k = i // (nb - 1)
        heads_to(k, 0, b).wait_send()
        heads_to(k, 1, b).wait_send()
        return carry

    lax.fori_loop(0, 4 * (nb - 1), sent, 0)
    for j in (0, 1):
        for i in range(1, nb):
            back_to(j, lax.rem(mb + i, nb)).wait_send()
    for k in (1, 2, 3):
        for n in range(apart):
            near_to(n).wait_send() if k == 1 else pair_to(k, n).wait_send()

    @pl.when(middle)
    def _():
        for k in (1, 2, 3):
            for n in range(apart, parts):
                near_to(n).wait_send() if k == 1 else pair_to(k, n).wait_send()
        for j in range(nb // 2):
            twin_share(j).wait_send()
        for j in range(1, nb // 2):
            twin_pass(j).wait_send()

    @pl.when(jnp.logical_not(middle))
    def _():
        twin_out().wait_send()
        for k in (1, 2, 3):
            full_to(k).wait_send()


def fused(nb, tokens, mod_shift, mod_scale, mod_gate, w_query, w_key, w_value, w_out, score_gain):
    rows = tokens.shape[0]
    cols = w_query.shape[1]
    chunks = 4
    tile = 512
    parts = D // tile
    span = nb * rows
    bf16, f32 = jnp.bfloat16, jnp.float32
    vmem = pl.BlockSpec(memory_space=pltpu.VMEM)
    hbm = pl.BlockSpec(memory_space=pltpu.HBM)
    dma = pltpu.SemaphoreType.DMA
    return pl.pallas_call(
        functools.partial(kernel, nb),
        out_shape=jax.ShapeDtypeStruct((rows, D), bf16),
        in_specs=[hbm] * 9,
        out_specs=vmem,
        scratch_shapes=[
            pltpu.VMEM((rows, D), bf16),
            pltpu.VMEM((1, D), f32),
            pltpu.VMEM((1, D), f32),
            pltpu.VMEM((1, D), f32),
            pltpu.VMEM((1, HEADS), f32),
            pltpu.VMEM((4, chunks, rows, D // chunks), bf16),
            pltpu.VMEM((D, cols), bf16),
            pltpu.VMEM((D, cols), bf16),
            pltpu.VMEM((D, cols), bf16),
            pltpu.VMEM((cols, D), bf16),
            pltpu.VMEM((4, nb, rows, 128), bf16),
            pltpu.VMEM((4, nb, rows, 128), bf16),
            pltpu.VMEM((4 * span, 128), bf16),
            pltpu.VMEM((4 * span, 128), bf16),
            pltpu.VMEM((64, 4 * span), bf16),
            pltpu.VMEM((4, 1, span), f32),
            pltpu.VMEM((4, 1, span), f32),
            pltpu.VMEM((4, 64, span), f32),
            pltpu.VMEM((2, span, 128), bf16),
            pltpu.VMEM((2, nb, rows, 128), bf16),
            pltpu.VMEM((4, rows, cols), bf16),
            pltpu.VMEM((4, rows, cols), bf16),
            pltpu.VMEM((cols, TWIN), bf16),
            pltpu.VMEM((4, parts, rows, tile), f32),
            pltpu.VMEM((4, parts, rows, tile), bf16),
            pltpu.VMEM((2, parts, rows, tile), bf16),
            pltpu.VMEM((parts, rows, tile), bf16),
            pltpu.VMEM((parts, rows, tile), bf16),
            dma((9,)),
            dma((2, chunks)),
            dma((4, chunks)),
            dma((4, chunks)),
            dma((4, 2, nb)),
            dma((4, 2, nb)),
            dma((2, nb)),
            dma((2, nb)),
            dma((4, parts)),
            dma((4, parts)),
            dma((4,)),
            dma((4,)),
            dma((2, nb // 2)),
            dma((nb,)),
        ],
        compiler_params=pltpu.CompilerParams(
            collective_id=0, has_side_effects=True, vmem_limit_bytes=56 * 1024 * 1024
        ),
    )(
        tokens, mod_shift[None], mod_scale[None], mod_gate[None], score_gain[None],
        w_query, w_key, w_value, w_out,
    )


def modulate(tokens, mod_shift, mod_scale):
    values = tokens.astype(jnp.float32)
    center = values - jnp.mean(values, axis=-1, keepdims=True)
    spread = jnp.mean(center * center, axis=-1, keepdims=True)
    normed = center * lax.rsqrt(spread + 1e-06)
    return (normed * (1.0 + mod_scale) + mod_shift).astype(jnp.bfloat16)


def head_norm(projected, width):
    count = projected.shape[0]
    split = projected.reshape(count, -1, width)
    power = jnp.mean(split * split, axis=-1, keepdims=True)
    return (split * lax.rsqrt(power + 1e-06)).reshape(count, -1).astype(jnp.bfloat16)


def body(tokens, mod_shift, mod_scale, mod_gate, w_query, w_key, w_value, w_out, score_gain):
    width = D // HEADS
    local_cols = w_query.shape[1]
    local_heads = local_cols // width
    modded = modulate(tokens, mod_shift, mod_scale)
    piece = lax.all_gather(modded, "uly", axis=0, tiled=True)
    joined = jnp.concatenate(
        [
            jnp.dot(piece, w_query, preferred_element_type=jnp.float32),
            jnp.dot(piece, w_key, preferred_element_type=jnp.float32),
            jnp.dot(piece, w_value, preferred_element_type=jnp.float32),
        ],
        axis=1,
    )
    queries = head_norm(joined[:, :local_cols], width)
    keys = head_norm(joined[:, local_cols : 2 * local_cols], width)
    values = joined[:, 2 * local_cols :].astype(jnp.bfloat16)
    gains = lax.dynamic_slice_in_dim(score_gain, lax.axis_index("uly") * local_heads, local_heads)
    factors = gains / math.sqrt(width)
    rows = queries.shape[0]
    query_heads = queries.reshape(rows, local_heads, width)
    initial = (
        jnp.full((local_heads, rows), -jnp.inf, jnp.float32),
        jnp.zeros((local_heads, rows), jnp.float32),
        jnp.zeros((local_heads, rows, width), jnp.float32),
    )
    key_piece = lax.all_gather(keys, "blk", axis=0, tiled=True)
    value_piece = lax.all_gather(values, "blk", axis=0, tiled=True)
    count = key_piece.shape[0]
    groups = count // rows
    limit = max(rows, 1024)
    depth = max(
        [step for step in range(1, groups + 1) if groups % step == 0 and step * rows <= limit]
    )
    stride = depth * rows
    key_blocks = key_piece.reshape(count // stride, stride, local_heads, width)
    value_blocks = value_piece.reshape(count // stride, stride, local_heads, width)

    def one_block(carry, blocks):
        run_max, run_total, run_acc = carry
        key_block, value_block = blocks
        scores = jnp.einsum(
            "rhd,khd->hrk", query_heads, key_block, preferred_element_type=jnp.float32
        )
        scores = scores * factors[:, None, None]
        new_max = jnp.maximum(run_max, jnp.max(scores, axis=-1))
        expo = jnp.exp(scores - new_max[..., None])
        rescale = jnp.exp(run_max - new_max)
        new_total = run_total * rescale + jnp.sum(expo, axis=-1)
        summed = jnp.einsum(
            "hrk,khd->hrd",
            expo.astype(jnp.bfloat16),
            value_block,
            preferred_element_type=jnp.float32,
        )
        new_acc = run_acc * rescale[..., None] + summed
        return ((new_max, new_total, new_acc), None)

    result, unused = lax.scan(one_block, initial, (key_blocks, value_blocks))
    run_max, run_total, run_acc = result
    attended = (run_acc / run_total[..., None]).astype(jnp.bfloat16)
    attended = attended.transpose(1, 0, 2).reshape(rows, local_cols)
    returned = lax.all_to_all(attended, "uly", split_axis=0, concat_axis=1, tiled=True)
    projected = jnp.dot(
        returned,
        lax.all_gather(w_out, "uly", axis=0, tiled=True),
        preferred_element_type=jnp.float32,
    )
    return (tokens.astype(jnp.float32) + mod_gate * projected).astype(jnp.bfloat16)


def solution(mesh):
    in_specs = (
        P(("blk", "uly"), None),
        P(),
        P(),
        P(),
        P(None, "uly"),
        P(None, "uly"),
        P(None, "uly"),
        P("uly", None),
        P(),
    )
    out_specs = P(("blk", "uly"), None)
    nb, nz = mesh.shape["blk"], mesh.shape["uly"]
    run = body
    if HEADS == nb * nz and nz == 4 and nb % 2 == 0:
        run = functools.partial(fused, nb)
    return jax.shard_map(run, mesh=mesh, in_specs=in_specs, out_specs=out_specs, check_vma=False)
```

```python
import functools
import math

import jax
import jax.numpy as jnp
from jax import lax
from jax.experimental import pallas as pl
from jax.experimental.pallas import tpu as pltpu
from jax.sharding import PartitionSpec as P

D = 2048
HEADS = 32
LOG2E = math.log2(math.e)
MESH = pl.DeviceIdType.MESH
SUB = 384
TWIN = 1024


def kernel(
    nb, tok_h, shift_h, scale_h, gate_h, gain_h, wq, wk, wv, wo, out,
    tok, shift, scale, gate, gain, mod, wq_v, wk_v, wv_v, wo_v, kv_s, q_s, kv_r, q_r, vt, top_v, sum_v, acc_v,
    att_s, att_r, full_v, full_r, twin_v, part_v, part_s, pair_r, near_r, far_r,
    wsem, gs, gr, fs, hs, hr, bs, br, rs, rr, es, er, ts, tr,
):
    width = D // HEADS
    rows = tok.shape[0]
    span = nb * rows
    chunks = mod.shape[1]
    deep = mod.shape[3]
    tile = part_s.shape[-1]
    parts = D // tile
    apart = parts - twin_v.shape[1] // tile
    mb, mz = lax.axis_index("blk"), lax.axis_index("uly")
    high = mz // 2
    middle = (mz + 1) // 2 == 1
    near = mz + 1 - 2 * lax.rem(mz, 2)
    inner = 2 - high
    outer = 3 - 3 * high

    barrier = pltpu.get_barrier_semaphore()
    for z in (inner, near):
        pl.semaphore_signal(barrier, inc=1, device_id={"uly": z}, device_id_type=MESH)

    @pl.when(middle)
    def _():
        pl.semaphore_signal(barrier, inc=1, device_id={"uly": outer}, device_id_type=MESH)

    for j in range(1, nb):
        pl.semaphore_signal(barrier, inc=1, device_id={"blk": lax.rem(mb + j, nb)}, device_id_type=MESH)

    pairs = (
        (tok_h, tok), (shift_h, shift), (scale_h, scale), (wk, wk_v), (wv, wv_v), (wq, wq_v),
        (wo, wo_v), (gate_h, gate), (gain_h, gain),
    )
    loads = [
        pltpu.make_async_copy(src, dst, wsem.at[i])
        for i, (src, dst) in enumerate(pairs)
    ]
    for load in loads:
        load.start()
    for load in loads[:3]:
        load.wait()

    values = tok[...].astype(jnp.float32)
    center = values - jnp.mean(values, axis=-1, keepdims=True)
    spread = jnp.mean(center * center, axis=-1, keepdims=True)
    normed = center * lax.rsqrt(spread + 1e-06)
    modded = (normed * (1.0 + scale[...]) + shift[...]).astype(jnp.bfloat16)
    for c in range(chunks):
        mod[0, c] = modded[:, c * deep : (c + 1) * deep]

    pl.semaphore_wait(barrier, nb + 1 + middle.astype(jnp.int32))

    def gather(way, c):
        slot = 1 + way
        return pltpu.make_async_remote_copy(
            src_ref=mod.at[0, c], dst_ref=mod.at[slot, c], send_sem=gs.at[way, c], recv_sem=gr.at[slot, c],
            device_id={"uly": inner if way else near}, device_id_type=MESH)

    def landed(k, c):
        return pltpu.make_async_remote_copy(
            src_ref=mod.at[0, c], dst_ref=mod.at[k, c], send_sem=gs.at[0, c], recv_sem=gr.at[k, c],
            device_id={"uly": near}, device_id_type=MESH)

    def forward(k, c):
        return pltpu.make_async_remote_copy(
            src_ref=mod.at[k, c], dst_ref=mod.at[k, c], send_sem=fs.at[k, c], recv_sem=gr.at[k, c],
            device_id={"uly": near}, device_id_type=MESH)

    def across(c):
        return pltpu.make_async_remote_copy(
            src_ref=mod.at[1, c], dst_ref=mod.at[3, c], send_sem=fs.at[1, c], recv_sem=gr.at[3, c],
            device_id={"uly": inner}, device_id_type=MESH)

    @pl.when(middle)
    def _():
        for c in range(chunks):
            for way in (0, 1):
                gather(way, c).start()

    @pl.when(jnp.logical_not(middle))
    def _():
        for c in range(chunks):
            gather(0, c).start()

    for load in loads[3:6]:
        load.wait()

    def place(k, b):
        return pl.ds(pl.multiple_of(k * span + b * rows, rows), rows)

    depth = wo_v.shape[0] // nb
    sibling = mb + 1 - 2 * lax.rem(mb, 2)

    def slab(b):
        return pl.ds(pl.multiple_of(b * depth, depth), depth)

    def twin_out():
        return pltpu.make_async_remote_copy(
            src_ref=wo_v.at[slab(mb), apart * tile :], dst_ref=twin_v.at[slab(mb), :], send_sem=ts.at[0, 0],
            recv_sem=tr.at[mb], device_id={"uly": near}, device_id_type=MESH)

    def twin_in(b):
        return pltpu.make_async_remote_copy(
            src_ref=twin_v.at[slab(b), :], dst_ref=twin_v.at[slab(b), :], send_sem=ts.at[0, 0],
            recv_sem=tr.at[b], device_id={"uly": near}, device_id_type=MESH)

    def twin_share(j):
        return pltpu.make_async_remote_copy(
            src_ref=twin_v.at[slab(mb), :], dst_ref=twin_v.at[slab(mb), :], send_sem=ts.at[0, j],
            recv_sem=tr.at[mb], device_id={"blk": sibling if j == 0 else lax.rem(mb + 2 * j, nb)}, device_id_type=MESH)

    def twin_pass(j):
        b = lax.rem(mb + 2 * j, nb)
        return pltpu.make_async_remote_copy(
            src_ref=twin_v.at[slab(b), :], dst_ref=twin_v.at[slab(b), :], send_sem=ts.at[1, j],
            recv_sem=tr.at[b], device_id={"blk": sibling}, device_id_type=MESH)

    def full_to(k):
        return pltpu.make_async_remote_copy(
            src_ref=full_v.at[k], dst_ref=full_r.at[k], send_sem=es.at[k], recv_sem=er.at[k],
            device_id={"uly": near}, device_id_type=MESH)

    def heads_to(k, kind, b):
        src, dst = ((kv_s, kv_r), (q_s, q_r))[kind]
        return pltpu.make_async_remote_copy(
            src_ref=src.at[k, b], dst_ref=dst.at[place(k, mb), :], send_sem=hs.at[k, kind, b],
            recv_sem=hr.at[k, kind, mb], device_id={"blk": b}, device_id_type=MESH)

    def heads_from(k, kind, b):
        src, dst = ((kv_s, kv_r), (q_s, q_r))[kind]
        return pltpu.make_async_remote_copy(
            src_ref=src.at[k, b], dst_ref=dst.at[place(k, b), :], send_sem=hs.at[k, kind, b],
            recv_sem=hr.at[k, kind, b], device_id={"blk": b}, device_id_type=MESH)

    loads[8].wait()
    chosen = lax.broadcasted_iota(jnp.int32, gain.shape, 1) == mz * nb + mb
    factor = jnp.sum(jnp.where(chosen, gain[...], 0.0), axis=-1, keepdims=True) * (LOG2E / math.sqrt(width))

    def await_heads(k, kind):
        for j in range(1, nb):
            heads_from(k, kind, lax.rem(mb + j, nb)).wait_recv()

    def flip(k):
        vt[:, k * span : (k + 1) * span] = kv_r[k * span : (k + 1) * span, :].T[width:, :]

    def scored(k, c, first, last):
        q = q_r[k * span + c * SUB : k * span + (c + 1) * SUB, :]
        return lax.dot_general(
            kv_r[first * span : last * span, :], q, (((1,), (1,)), ((), ())), preferred_element_type=jnp.float32)

    def begin(k, c, first, last):
        scores = scored(k, c, first, last)
        top = jnp.max(scores, axis=0, keepdims=True)
        expo = jnp.exp2((scores - top) * factor)
        total = jnp.sum(expo, axis=0, keepdims=True)
        summed = jnp.dot(vt[:, first * span : last * span], expo.astype(jnp.bfloat16), preferred_element_type=jnp.float32)
        return top, total, summed

    def keep(k, first, last):
        for c in range(span // SUB):
            cols = slice(c * SUB, (c + 1) * SUB)
            top_v[k, :, cols], sum_v[k, :, cols], acc_v[k, :, cols] = begin(k, c, first, last)

    def more(k, c, first, last):
        cols = slice(c * SUB, (c + 1) * SUB)
        scores = scored(k, c, first, last)
        old = top_v[k, :, cols]
        top = jnp.maximum(old, jnp.max(scores, axis=0, keepdims=True))
        shrink = jnp.exp2((old - top) * factor)
        expo = jnp.exp2((scores - top) * factor)
        total = sum_v[k, :, cols] * shrink + jnp.sum(expo, axis=0, keepdims=True)
        summed = jnp.dot(vt[:, first * span : last * span], expo.astype(jnp.bfloat16), preferred_element_type=jnp.float32)
        return total, acc_v[k, :, cols] * shrink + summed

    def first_attend():
        for k in (0, 1):
            await_heads(k, 0)
            await_heads(k, 1)
            flip(k)
        for k in (0, 1):
            keep(k, 0, 2)

    def piece(k, carry):
        @pl.when((k == 3) & jnp.logical_not(middle))
        def _():
            first_attend()

        @pl.when((k == 1) & jnp.logical_not(middle))
        def _():
            loads[6].wait()
            twin_out().start()

        query = key = value = None
        for c in range(chunks):
            @pl.when((k > 0) & (jnp.logical_not(middle) | (k == 1)))
            def _():
                landed(k, c).wait_recv()

            @pl.when(middle & (k == 1))
            def _():
                across(c).start()

            @pl.when(middle & (k > 0) & (k < 3))
            def _():
                landed(k + 1, c).wait_recv()
                forward(k + 1, c).start()

            x = mod[k, c]
            deeps = slice(c * deep, (c + 1) * deep)
            more_k = jnp.dot(x, wk_v[deeps, :], preferred_element_type=jnp.float32)
            more_v = jnp.dot(x, wv_v[deeps, :], preferred_element_type=jnp.float32)
            more_q = jnp.dot(x, wq_v[deeps, :], preferred_element_type=jnp.float32)
            key = more_k if c == 0 else key + more_k
            value = more_v if c == 0 else value + more_v
            query = more_q if c == 0 else query + more_q

        def unit(part):
            power = jnp.mean(part * part, axis=-1, keepdims=True)
            return part * lax.rsqrt(power + 1e-06)

        def send(kind):
            def one(j, carry):
                heads_to(k, kind, lax.rem(mb + j, nb)).start()
                return carry

            lax.fori_loop(1, nb, one, 0)

        for h in range(nb):
            cols = slice(h * width, (h + 1) * width)
            kv_s[k, h] = jnp.concatenate([unit(key[:, cols]), value[:, cols]], axis=1).astype(jnp.bfloat16)
        send(0)
        kv_r[place(k, mb), :] = kv_s[k, mb]
        for h in range(nb):
            cols = slice(h * width, (h + 1) * width)
            line = unit(query[:, cols])
            q_s[k, h] = jnp.concatenate([line, jnp.zeros_like(line)], axis=1).astype(jnp.bfloat16)
        send(1)
        q_r[place(k, mb), :] = q_s[k, mb]
        return carry

    lax.fori_loop(0, 4, piece, 0)

    @pl.when(middle)
    def _():
        loads[6].wait()
        twin_in(mb).wait_recv()
        for j in range(1, nb // 2):
            twin_share(j).start()
        twin_share(0).start()
        first_attend()

    await_heads(2, 0)
    await_heads(2, 1)
    flip(2)
    keep(2, 0, 3)
    await_heads(3, 0)
    flip(3)

    def back_to(j, b):
        return pltpu.make_async_remote_copy(
            src_ref=att_s.at[j, pl.ds(pl.multiple_of(b * rows, rows), rows), :], dst_ref=att_r.at[j, mb],
            send_sem=bs.at[j, b], recv_sem=br.at[j, mb], device_id={"blk": b}, device_id_type=MESH)

    def back_from(j, b):
        return pltpu.make_async_remote_copy(
            src_ref=att_s.at[j, pl.ds(pl.multiple_of(b * rows, rows), rows), :], dst_ref=att_r.at[j, b],
            send_sem=bs.at[j, b], recv_sem=br.at[j, b], device_id={"blk": b}, device_id_type=MESH)

    def finished(k, c):
        if k == 3:
            unused, total, summed = begin(k, c, 0, 4)
        else:
            total, summed = more(k, c, 3 if k == 2 else 2, 4)
        return summed / total

    def finish(j):
        if j == 0:
            lower = [finished(2, c) for c in range(span // SUB)]
            await_heads(3, 1)
            upper = [finished(3, c) for c in range(span // SUB)]
        else:
            lower = [finished(1, c) for c in range(span // SUB)]
            upper = [finished(0, c) for c in range(span // SUB)]
        for c in range(span // SUB):
            both = jnp.concatenate([lower[c], upper[c]], axis=0)
            att_s[j, c * SUB : (c + 1) * SUB, :] = both.T.astype(jnp.bfloat16)

        def one(i, carry):
            back_to(j, lax.rem(mb + i, nb)).start()
            return carry

        lax.fori_loop(1, nb, one, 0)
        att_r[j, mb] = att_s[j, pl.ds(pl.multiple_of(mb * rows, rows), rows), :]

    def near_to(n):
        return pltpu.make_async_remote_copy(
            src_ref=part_s.at[1, n], dst_ref=near_r.at[n], send_sem=rs.at[1, n], recv_sem=rr.at[1, n],
            device_id={"uly": near}, device_id_type=MESH)

    def pair_to(k, n):
        return pltpu.make_async_remote_copy(
            src_ref=part_s.at[k, n], dst_ref=pair_r.at[k - 2, n], send_sem=rs.at[k, n], recv_sem=rr.at[k, n],
            device_id={"uly": near}, device_id_type=MESH)

    def far_to(k, n):
        return pltpu.make_async_remote_copy(
            src_ref=part_s.at[k, n], dst_ref=far_r.at[n], send_sem=rs.at[k, n], recv_sem=rr.at[0, n],
            device_id={"uly": inner if k == 2 else outer}, device_id_type=MESH)

    def project(j):
        for i in range(1, nb):
            back_from(j, lax.rem(mb + i, nb)).wait_recv()
        pieces = [att_r[j, h] for h in range(nb)]
        attended = jnp.concatenate(
            [
                jnp.concatenate([one[:, :width] for one in pieces], axis=1),
                jnp.concatenate([one[:, width:] for one in pieces], axis=1),
            ],
            axis=0,
        )
        if j == 0:
            full_v[2] = attended[:rows]
            full_v[3] = attended[rows:]
        else:
            full_v[1] = attended[:rows]

        @pl.when(jnp.logical_not(middle))
        def _():
            full_to(3 if j == 0 else 1).start()

        for n in range(apart):
            part = jnp.dot(attended, wo_v[:, n * tile : (n + 1) * tile], preferred_element_type=jnp.float32)
            if j == 0:
                for k in (2, 3):
                    mine = part[(k - 2) * rows : (k - 1) * rows]
                    part_v[k, n] = mine
                    part_s[k, n] = mine.astype(jnp.bfloat16)

                @pl.when(jnp.logical_not(middle))
                def _():
                    pair_to(3, n).start()
            else:
                part_s[1, n] = part[:rows].astype(jnp.bfloat16)
                near_to(n).start()
                part_v[0, n] = part[rows:]
        if j == 0:
            @pl.when(jnp.logical_not(middle))
            def _():
                full_to(2).start()
                for n in range(apart):
                    pair_to(2, n).start()

            @pl.when(middle)
            def _():
                for n in range(apart, parts):
                    part = jnp.dot(attended, wo_v[:, n * tile : (n + 1) * tile], preferred_element_type=jnp.float32)
                    for k in (2, 3):
                        part_v[k, n] = part[(k - 2) * rows : (k - 1) * rows]
        else:
            for n in range(apart, parts):
                part = jnp.dot(attended, wo_v[:, n * tile : (n + 1) * tile], preferred_element_type=jnp.float32)
                part_s[1, n] = part[:rows].astype(jnp.bfloat16)

                @pl.when(middle)
                def _():
                    near_to(n).start()

                part_v[0, n] = part[rows:]

    finish(0)
    finish(1)

    @pl.when(middle)
    def _():
        for j in range(1, nb // 2):
            twin_in(lax.rem(mb + 2 * j, nb)).wait_recv()
            twin_pass(j).start()

    loads[7].wait()
    project(0)
    project(1)

    def twin(k, n):
        cols = slice((n - apart) * tile, (n - apart + 1) * tile)
        return jnp.dot(full_r[k], twin_v[:, cols], preferred_element_type=jnp.float32)

    @pl.when(middle)
    def _():
        twin_in(sibling).wait_recv()
        for j in range(1, nb // 2):
            twin_in(lax.rem(sibling + 2 * j, nb)).wait_recv()
        for k in (3, 2):
            full_to(k).wait_recv()
            for n in range(apart, parts):
                part_s[k, n] = (part_v[k, n] + twin(k, n)).astype(jnp.bfloat16)
                far_to(k, n).start()
            for n in range(apart):
                pair_to(k, n).wait_recv()
                part_s[k, n] = (part_v[k, n] + pair_r[k - 2, n].astype(jnp.float32)).astype(jnp.bfloat16)
                far_to(k, n).start()
        full_to(1).wait_recv()
        for n in range(apart, parts):
            part_v[0, n] += twin(1, n)

    def settle(n, extra):
        total = part_v[0, n] + far_r[n].astype(jnp.float32)
        if extra:
            total = total + near_r[n].astype(jnp.float32)
        cols = slice(n * tile, (n + 1) * tile)
        out[:, cols] = (tok[:, cols].astype(jnp.float32) + gate[:, cols] * total).astype(jnp.bfloat16)

    for n in range(apart, parts):
        far_to(2, n).wait_recv()

        @pl.when(middle)
        def _():
            settle(n, False)

        @pl.when(jnp.logical_not(middle))
        def _():
            near_to(n).wait_recv()
            settle(n, True)

    for n in range(apart):
        far_to(2, n).wait_recv()
        near_to(n).wait_recv()
        settle(n, True)

    for c in range(chunks):
        gather(0, c).wait_send()

    @pl.when(middle)
    def _():
        for c in range(chunks):
            gather(1, c).wait_send()
            across(c).wait_send()
        for k in (2, 3):
            for c in range(chunks):
                forward(k, c).wait_send()

    def sent(i, carry):
        b = lax.rem(mb + 1 + lax.rem(i, nb - 1), nb)
        k = i // (nb - 1)
        heads_to(k, 0, b).wait_send()
        heads_to(k, 1, b).wait_send()
        return carry

    lax.fori_loop(0, 4 * (nb - 1), sent, 0)
    for j in (0, 1):
        for i in range(1, nb):
            back_to(j, lax.rem(mb + i, nb)).wait_send()
    for k in (1, 2, 3):
        for n in range(apart):
            near_to(n).wait_send() if k == 1 else pair_to(k, n).wait_send()

    @pl.when(middle)
    def _():
        for k in (1, 2, 3):
            for n in range(apart, parts):
                near_to(n).wait_send() if k == 1 else pair_to(k, n).wait_send()
        for j in range(nb // 2):
            twin_share(j).wait_send()
        for j in range(1, nb // 2):
            twin_pass(j).wait_send()

    @pl.when(jnp.logical_not(middle))
    def _():
        twin_out().wait_send()
        for k in (1, 2, 3):
            full_to(k).wait_send()


def fused(nb, tokens, mod_shift, mod_scale, mod_gate, w_query, w_key, w_value, w_out, score_gain):
    rows = tokens.shape[0]
    cols = w_query.shape[1]
    chunks = 4
    tile = 512
    parts = D // tile
    span = nb * rows
    bf16, f32 = jnp.bfloat16, jnp.float32
    vmem = pl.BlockSpec(memory_space=pltpu.VMEM)
    hbm = pl.BlockSpec(memory_space=pltpu.HBM)
    dma = pltpu.SemaphoreType.DMA
    return pl.pallas_call(
        functools.partial(kernel, nb),
        out_shape=jax.ShapeDtypeStruct((rows, D), bf16),
        in_specs=[hbm] * 9,
        out_specs=vmem,
        scratch_shapes=[
            pltpu.VMEM((rows, D), bf16),
            pltpu.VMEM((1, D), f32),
            pltpu.VMEM((1, D), f32),
            pltpu.VMEM((1, D), f32),
            pltpu.VMEM((1, HEADS), f32),
            pltpu.VMEM((4, chunks, rows, D // chunks), bf16),
            pltpu.VMEM((D, cols), bf16),
            pltpu.VMEM((D, cols), bf16),
            pltpu.VMEM((D, cols), bf16),
            pltpu.VMEM((cols, D), bf16),
            pltpu.VMEM((4, nb, rows, 128), bf16),
            pltpu.VMEM((4, nb, rows, 128), bf16),
            pltpu.VMEM((4 * span, 128), bf16),
            pltpu.VMEM((4 * span, 128), bf16),
            pltpu.VMEM((64, 4 * span), bf16),
            pltpu.VMEM((4, 1, span), f32),
            pltpu.VMEM((4, 1, span), f32),
            pltpu.VMEM((4, 64, span), f32),
            pltpu.VMEM((2, span, 128), bf16),
            pltpu.VMEM((2, nb, rows, 128), bf16),
            pltpu.VMEM((4, rows, cols), bf16),
            pltpu.VMEM((4, rows, cols), bf16),
            pltpu.VMEM((cols, TWIN), bf16),
            pltpu.VMEM((4, parts, rows, tile), f32),
            pltpu.VMEM((4, parts, rows, tile), bf16),
            pltpu.VMEM((2, parts, rows, tile), bf16),
            pltpu.VMEM((parts, rows, tile), bf16),
            pltpu.VMEM((parts, rows, tile), bf16),
            dma((9,)),
            dma((2, chunks)),
            dma((4, chunks)),
            dma((4, chunks)),
            dma((4, 2, nb)),
            dma((4, 2, nb)),
            dma((2, nb)),
            dma((2, nb)),
            dma((4, parts)),
            dma((4, parts)),
            dma((4,)),
            dma((4,)),
            dma((2, nb // 2)),
            dma((nb,)),
        ],
        compiler_params=pltpu.CompilerParams(
            collective_id=0, has_side_effects=True, vmem_limit_bytes=56 * 1024 * 1024
        ),
    )(
        tokens, mod_shift[None], mod_scale[None], mod_gate[None], score_gain[None],
        w_query, w_key, w_value, w_out,
    )


def modulate(tokens, mod_shift, mod_scale):
    values = tokens.astype(jnp.float32)
    center = values - jnp.mean(values, axis=-1, keepdims=True)
    spread = jnp.mean(center * center, axis=-1, keepdims=True)
    normed = center * lax.rsqrt(spread + 1e-06)
    return (normed * (1.0 + mod_scale) + mod_shift).astype(jnp.bfloat16)


def head_norm(projected, width):
    count = projected.shape[0]
    split = projected.reshape(count, -1, width)
    power = jnp.mean(split * split, axis=-1, keepdims=True)
    return (split * lax.rsqrt(power + 1e-06)).reshape(count, -1).astype(jnp.bfloat16)


def body(tokens, mod_shift, mod_scale, mod_gate, w_query, w_key, w_value, w_out, score_gain):
    width = D // HEADS
    local_cols = w_query.shape[1]
    local_heads = local_cols // width
    modded = modulate(tokens, mod_shift, mod_scale)
    piece = lax.all_gather(modded, "uly", axis=0, tiled=True)
    joined = jnp.concatenate(
        [
            jnp.dot(piece, w_query, preferred_element_type=jnp.float32),
            jnp.dot(piece, w_key, preferred_element_type=jnp.float32),
            jnp.dot(piece, w_value, preferred_element_type=jnp.float32),
        ],
        axis=1,
    )
    queries = head_norm(joined[:, :local_cols], width)
    keys = head_norm(joined[:, local_cols : 2 * local_cols], width)
    values = joined[:, 2 * local_cols :].astype(jnp.bfloat16)
    gains = lax.dynamic_slice_in_dim(score_gain, lax.axis_index("uly") * local_heads, local_heads)
    factors = gains / math.sqrt(width)
    rows = queries.shape[0]
    query_heads = queries.reshape(rows, local_heads, width)
    initial = (
        jnp.full((local_heads, rows), -jnp.inf, jnp.float32),
        jnp.zeros((local_heads, rows), jnp.float32),
        jnp.zeros((local_heads, rows, width), jnp.float32),
    )
    key_piece = lax.all_gather(keys, "blk", axis=0, tiled=True)
    value_piece = lax.all_gather(values, "blk", axis=0, tiled=True)
    count = key_piece.shape[0]
    groups = count // rows
    limit = max(rows, 1024)
    depth = max(
        [step for step in range(1, groups + 1) if groups % step == 0 and step * rows <= limit]
    )
    stride = depth * rows
    key_blocks = key_piece.reshape(count // stride, stride, local_heads, width)
    value_blocks = value_piece.reshape(count // stride, stride, local_heads, width)

    def one_block(carry, blocks):
        run_max, run_total, run_acc = carry
        key_block, value_block = blocks
        scores = jnp.einsum(
            "rhd,khd->hrk", query_heads, key_block, preferred_element_type=jnp.float32
        )
        scores = scores * factors[:, None, None]
        new_max = jnp.maximum(run_max, jnp.max(scores, axis=-1))
        expo = jnp.exp(scores - new_max[..., None])
        rescale = jnp.exp(run_max - new_max)
        new_total = run_total * rescale + jnp.sum(expo, axis=-1)
        summed = jnp.einsum(
            "hrk,khd->hrd",
            expo.astype(jnp.bfloat16),
            value_block,
            preferred_element_type=jnp.float32,
        )
        new_acc = run_acc * rescale[..., None] + summed
        return ((new_max, new_total, new_acc), None)

    result, unused = lax.scan(one_block, initial, (key_blocks, value_blocks))
    run_max, run_total, run_acc = result
    attended = (run_acc / run_total[..., None]).astype(jnp.bfloat16)
    attended = attended.transpose(1, 0, 2).reshape(rows, local_cols)
    returned = lax.all_to_all(attended, "uly", split_axis=0, concat_axis=1, tiled=True)
    projected = jnp.dot(
        returned,
        lax.all_gather(w_out, "uly", axis=0, tiled=True),
        preferred_element_type=jnp.float32,
    )
    return (tokens.astype(jnp.float32) + mod_gate * projected).astype(jnp.bfloat16)


def solution(mesh):
    in_specs = (
        P(("blk", "uly"), None),
        P(),
        P(),
        P(),
        P(None, "uly"),
        P(None, "uly"),
        P(None, "uly"),
        P("uly", None),
        P(),
    )
    out_specs = P(("blk", "uly"), None)
    nb, nz = mesh.shape["blk"], mesh.shape["uly"]
    run = body
    if HEADS == nb * nz and nz == 4 and nb % 2 == 0:
        run = functools.partial(fused, nb)
    return jax.shard_map(run, mesh=mesh, in_specs=in_specs, out_specs=out_specs, check_vma=False)
```

```python
import functools
import math

import jax
import jax.numpy as jnp
from jax import lax
from jax.experimental import pallas as pl
from jax.experimental.pallas import tpu as pltpu
from jax.sharding import PartitionSpec as P

D = 2048
HEADS = 32
LOG2E = math.log2(math.e)
MESH = pl.DeviceIdType.MESH
SUB = 384
TWIN = 1024


def kernel(
    nb, tok_h, shift_h, scale_h, gate_h, gain_h, wq, wk, wv, wo, out,
    tok, shift, scale, gate, gain, mod, wq_v, wk_v, wv_v, wo_v, kv_s, q_s, kv_r, q_r, q_v, vt, top_v, sum_v, acc_v,
    att_s, att_r, full_v, full_r, twin_v, part_v, part_s, pair_r, near_r, far_r,
    wsem, gs, gr, fs, hs, hr, bs, br, rs, rr, es, er, ts, tr,
):
    width = D // HEADS
    rows = tok.shape[0]
    span = nb * rows
    chunks = mod.shape[1]
    deep = mod.shape[3]
    tile = part_s.shape[-1]
    parts = D // tile
    apart = parts - twin_v.shape[1] // tile
    mb, mz = lax.axis_index("blk"), lax.axis_index("uly")
    high = mz // 2
    middle = (mz + 1) // 2 == 1
    near = mz + 1 - 2 * lax.rem(mz, 2)
    inner = 2 - high
    outer = 3 - 3 * high

    barrier = pltpu.get_barrier_semaphore()
    for z in (inner, near):
        pl.semaphore_signal(barrier, inc=1, device_id={"uly": z}, device_id_type=MESH)

    @pl.when(middle)
    def _():
        pl.semaphore_signal(barrier, inc=1, device_id={"uly": outer}, device_id_type=MESH)

    for j in range(1, nb):
        pl.semaphore_signal(barrier, inc=1, device_id={"blk": lax.rem(mb + j, nb)}, device_id_type=MESH)

    pairs = (
        (tok_h, tok), (shift_h, shift), (scale_h, scale), (wk, wk_v), (wv, wv_v), (wq, wq_v),
        (wo, wo_v), (gate_h, gate), (gain_h, gain),
    )
    loads = [
        pltpu.make_async_copy(src, dst, wsem.at[i])
        for i, (src, dst) in enumerate(pairs)
    ]
    for load in loads:
        load.start()
    for load in loads[:3]:
        load.wait()

    values = tok[...].astype(jnp.float32)
    center = values - jnp.mean(values, axis=-1, keepdims=True)
    spread = jnp.mean(center * center, axis=-1, keepdims=True)
    normed = center * lax.rsqrt(spread + 1e-06)
    modded = (normed * (1.0 + scale[...]) + shift[...]).astype(jnp.bfloat16)
    for c in range(chunks):
        mod[0, c] = modded[:, c * deep : (c + 1) * deep]

    pl.semaphore_wait(barrier, nb + 1 + middle.astype(jnp.int32))

    def gather(way, c):
        slot = 1 + way
        return pltpu.make_async_remote_copy(
            src_ref=mod.at[0, c], dst_ref=mod.at[slot, c], send_sem=gs.at[way, c], recv_sem=gr.at[slot, c],
            device_id={"uly": inner if way else near}, device_id_type=MESH)

    def landed(k, c):
        return pltpu.make_async_remote_copy(
            src_ref=mod.at[0, c], dst_ref=mod.at[k, c], send_sem=gs.at[0, c], recv_sem=gr.at[k, c],
            device_id={"uly": near}, device_id_type=MESH)

    def forward(k, c):
        return pltpu.make_async_remote_copy(
            src_ref=mod.at[k, c], dst_ref=mod.at[k, c], send_sem=fs.at[k, c], recv_sem=gr.at[k, c],
            device_id={"uly": near}, device_id_type=MESH)

    def across(c):
        return pltpu.make_async_remote_copy(
            src_ref=mod.at[1, c], dst_ref=mod.at[3, c], send_sem=fs.at[1, c], recv_sem=gr.at[3, c],
            device_id={"uly": inner}, device_id_type=MESH)

    @pl.when(middle)
    def _():
        for c in range(chunks):
            for way in (0, 1):
                gather(way, c).start()

    @pl.when(jnp.logical_not(middle))
    def _():
        for c in range(chunks):
            gather(0, c).start()

    for load in loads[3:6]:
        load.wait()

    most = q_s.shape[2]

    def lower(k, b):
        return pl.ds(pl.multiple_of((k * nb + b) * most, most), most)

    def place(k, b):
        return pl.ds(pl.multiple_of(k * span + b * rows, rows), rows)

    depth = wo_v.shape[0] // nb
    sibling = mb + 1 - 2 * lax.rem(mb, 2)

    def slab(b):
        return pl.ds(pl.multiple_of(b * depth, depth), depth)

    half = twin_v.shape[1] // 2

    def twin_copy(p, b, send, who, src=None):
        here = twin_v.at[slab(b), p * half : (p + 1) * half]
        return pltpu.make_async_remote_copy(
            src_ref=here if src is None else src, dst_ref=here, send_sem=send, recv_sem=tr.at[p, b],
            device_id=who, device_id_type=MESH)

    def twin_out(p):
        left = apart * tile + p * half
        return twin_copy(p, mb, ts.at[p, 0, 0], {"uly": near}, wo_v.at[slab(mb), left : left + half])

    def twin_in(p, b):
        return twin_copy(p, b, ts.at[p, 0, 0], {"uly": near})

    def twin_share(p, j):
        return twin_copy(p, mb, ts.at[p, 0, j], {"blk": sibling if j == 0 else lax.rem(mb + 2 * j, nb)})

    def twin_pass(p, j):
        return twin_copy(p, lax.rem(mb + 2 * j, nb), ts.at[p, 1, j], {"blk": sibling})

    def share(p):
        twin_in(p, mb).wait_recv()
        for j in range(1, nb // 2):
            twin_share(p, j).start()
        twin_share(p, 0).start()

    def relay(p):
        for j in range(1, nb // 2):
            twin_in(p, lax.rem(mb + 2 * j, nb)).wait_recv()
            twin_pass(p, j).start()

    def whole(p):
        twin_in(p, sibling).wait_recv()
        for j in range(1, nb // 2):
            twin_in(p, lax.rem(sibling + 2 * j, nb)).wait_recv()

    def full_to(k):
        return pltpu.make_async_remote_copy(
            src_ref=full_v.at[k], dst_ref=full_r.at[k], send_sem=es.at[k], recv_sem=er.at[k],
            device_id={"uly": near}, device_id_type=MESH)

    def heads_to(k, kind, b):
        src, dst, where = ((kv_s, kv_r, place), (q_s, q_r, lower))[kind]
        return pltpu.make_async_remote_copy(
            src_ref=src.at[k, b], dst_ref=dst.at[where(k, mb), :], send_sem=hs.at[k, kind, b],
            recv_sem=hr.at[k, kind, mb], device_id={"blk": b}, device_id_type=MESH)

    def heads_from(k, kind, b):
        src, dst, where = ((kv_s, kv_r, place), (q_s, q_r, lower))[kind]
        return pltpu.make_async_remote_copy(
            src_ref=src.at[k, b], dst_ref=dst.at[where(k, b), :], send_sem=hs.at[k, kind, b],
            recv_sem=hr.at[k, kind, b], device_id={"blk": b}, device_id_type=MESH)

    loads[8].wait()
    chosen = lax.broadcasted_iota(jnp.int32, gain.shape, 1) == mz * nb + mb
    factor = jnp.sum(jnp.where(chosen, gain[...], 0.0), axis=-1, keepdims=True) * (LOG2E / math.sqrt(width))

    def await_heads(k, kind):
        for j in range(1, nb):
            heads_from(k, kind, lax.rem(mb + j, nb)).wait_recv()

    def flip(k):
        vt[:, k * span : (k + 1) * span] = kv_r[k * span : (k + 1) * span, :].T[width:, :]

    def widen(k):
        for b in range(nb):
            both = q_r[(k * nb + b) * most : (k * nb + b + 1) * most, :]
            clear = jnp.zeros((most, width), jnp.bfloat16)
            start = k * span + b * rows
            q_v[start : start + most, :] = jnp.concatenate([both[:, :width], clear], axis=1)
            q_v[start + most : start + rows, :] = jnp.concatenate(
                [both[: rows - most, width:], clear[: rows - most]], axis=1)

    def scored(k, c, first, last):
        q = q_v[k * span + c * SUB : k * span + (c + 1) * SUB, :]
        return lax.dot_general(
            kv_r[first * span : last * span, :], q, (((1,), (1,)), ((), ())), preferred_element_type=jnp.float32)

    def begin(k, c, first, last):
        scores = scored(k, c, first, last)
        top = jnp.max(scores, axis=0, keepdims=True)
        expo = jnp.exp2((scores - top) * factor)
        total = jnp.sum(expo, axis=0, keepdims=True)
        summed = jnp.dot(vt[:, first * span : last * span], expo.astype(jnp.bfloat16), preferred_element_type=jnp.float32)
        return top, total, summed

    def keep(k, first, last):
        for c in range(span // SUB):
            cols = slice(c * SUB, (c + 1) * SUB)
            top_v[k, :, cols], sum_v[k, :, cols], acc_v[k, :, cols] = begin(k, c, first, last)

    def more(k, c, first, last):
        cols = slice(c * SUB, (c + 1) * SUB)
        scores = scored(k, c, first, last)
        old = top_v[k, :, cols]
        top = jnp.maximum(old, jnp.max(scores, axis=0, keepdims=True))
        shrink = jnp.exp2((old - top) * factor)
        expo = jnp.exp2((scores - top) * factor)
        total = sum_v[k, :, cols] * shrink + jnp.sum(expo, axis=0, keepdims=True)
        summed = jnp.dot(vt[:, first * span : last * span], expo.astype(jnp.bfloat16), preferred_element_type=jnp.float32)
        return total, acc_v[k, :, cols] * shrink + summed

    def first_attend():
        for k in (0, 1):
            await_heads(k, 0)
            await_heads(k, 1)
            flip(k)
            widen(k)
        for k in (0, 1):
            keep(k, 0, 2)

    def piece(k, carry):
        @pl.when((k == 3) & jnp.logical_not(middle))
        def _():
            first_attend()

        @pl.when((k == 1) & jnp.logical_not(middle))
        def _():
            loads[6].wait()
            twin_out(0).start()
            twin_out(1).start()

        query = key = value = None
        for c in range(chunks):
            @pl.when((k > 0) & (jnp.logical_not(middle) | (k == 1)))
            def _():
                landed(k, c).wait_recv()

            @pl.when(middle & (k == 1))
            def _():
                across(c).start()

            @pl.when(middle & (k > 0) & (k < 3))
            def _():
                landed(k + 1, c).wait_recv()
                forward(k + 1, c).start()

            if c == 1:
                @pl.when(middle & (k == 2))
                def _():
                    share(0)

            x = mod[k, c]
            deeps = slice(c * deep, (c + 1) * deep)
            more_k = jnp.dot(x, wk_v[deeps, :], preferred_element_type=jnp.float32)
            more_v = jnp.dot(x, wv_v[deeps, :], preferred_element_type=jnp.float32)
            if c < chunks - 1:
                more_q = jnp.dot(x, wq_v[deeps, :], preferred_element_type=jnp.float32)
            key = more_k if c == 0 else key + more_k
            value = more_v if c == 0 else value + more_v
            if c < chunks - 1:
                query = more_q if c == 0 else query + more_q

        def unit(part):
            power = jnp.mean(part * part, axis=-1, keepdims=True)
            return part * lax.rsqrt(power + 1e-06)

        def send(kind):
            def one(j, carry):
                heads_to(k, kind, lax.rem(mb + j, nb)).start()
                return carry

            lax.fori_loop(1, nb, one, 0)

        for h in range(nb):
            cols = slice(h * width, (h + 1) * width)
            kv_s[k, h] = jnp.concatenate([unit(key[:, cols]), value[:, cols]], axis=1).astype(jnp.bfloat16)
        send(0)
        kv_r[place(k, mb), :] = kv_s[k, mb]
        query = query + jnp.dot(x, wq_v[deeps, :], preferred_element_type=jnp.float32)
        for h in range(nb):
            cols = slice(h * width, (h + 1) * width)
            line = unit(query[:, cols])
            rest = jnp.concatenate([line[most:], jnp.zeros((2 * most - rows, width), jnp.float32)], axis=0)
            q_s[k, h] = jnp.concatenate([line[:most], rest], axis=1).astype(jnp.bfloat16)
        send(1)
        q_r[lower(k, mb), :] = q_s[k, mb]
        return carry

    lax.fori_loop(0, 4, piece, 0)

    @pl.when(middle)
    def _():
        loads[6].wait()
        share(1)
        first_attend()

    await_heads(2, 0)
    await_heads(2, 1)
    flip(2)
    widen(2)
    keep(2, 0, 3)
    @pl.when(middle)
    def _():
        relay(0)

    await_heads(3, 0)
    flip(3)

    def back_to(j, b):
        return pltpu.make_async_remote_copy(
            src_ref=att_s.at[j, pl.ds(pl.multiple_of(b * rows, rows), rows), :], dst_ref=att_r.at[j, mb],
            send_sem=bs.at[j, b], recv_sem=br.at[j, mb], device_id={"blk": b}, device_id_type=MESH)

    def back_from(j, b):
        return pltpu.make_async_remote_copy(
            src_ref=att_s.at[j, pl.ds(pl.multiple_of(b * rows, rows), rows), :], dst_ref=att_r.at[j, b],
            send_sem=bs.at[j, b], recv_sem=br.at[j, b], device_id={"blk": b}, device_id_type=MESH)

    def finished(k, c):
        if k == 3:
            unused, total, summed = begin(k, c, 0, 4)
        else:
            total, summed = more(k, c, 3 if k == 2 else 2, 4)
        return summed / total

    def finish(j):
        if j == 0:
            lower = [finished(2, c) for c in range(span // SUB)]
            await_heads(3, 1)
            widen(3)
            upper = [finished(3, c) for c in range(span // SUB)]
        else:
            lower = [finished(1, c) for c in range(span // SUB)]
            upper = [finished(0, c) for c in range(span // SUB)]
        for c in range(span // SUB):
            both = jnp.concatenate([lower[c], upper[c]], axis=0)
            att_s[j, c * SUB : (c + 1) * SUB, :] = both.T.astype(jnp.bfloat16)

        def one(i, carry):
            back_to(j, lax.rem(mb + i, nb)).start()
            return carry

        lax.fori_loop(1, nb, one, 0)
        att_r[j, mb] = att_s[j, pl.ds(pl.multiple_of(mb * rows, rows), rows), :]

    def near_to(n):
        return pltpu.make_async_remote_copy(
            src_ref=part_s.at[1, n], dst_ref=near_r.at[n], send_sem=rs.at[1, n], recv_sem=rr.at[1, n],
            device_id={"uly": near}, device_id_type=MESH)

    def pair_to(k, n):
        return pltpu.make_async_remote_copy(
            src_ref=part_s.at[k, n], dst_ref=pair_r.at[k - 2, n], send_sem=rs.at[k, n], recv_sem=rr.at[k, n],
            device_id={"uly": near}, device_id_type=MESH)

    def far_to(k, n):
        return pltpu.make_async_remote_copy(
            src_ref=part_s.at[k, n], dst_ref=far_r.at[n], send_sem=rs.at[k, n], recv_sem=rr.at[0, n],
            device_id={"uly": inner if k == 2 else outer}, device_id_type=MESH)

    def project(j):
        for i in range(1, nb):
            back_from(j, lax.rem(mb + i, nb)).wait_recv()
        pieces = [att_r[j, h] for h in range(nb)]
        attended = jnp.concatenate(
            [
                jnp.concatenate([one[:, :width] for one in pieces], axis=1),
                jnp.concatenate([one[:, width:] for one in pieces], axis=1),
            ],
            axis=0,
        )
        if j == 0:
            full_v[2] = attended[:rows]
            full_v[3] = attended[rows:]
        else:
            full_v[1] = attended[:rows]

        @pl.when(jnp.logical_not(middle))
        def _():
            full_to(3 if j == 0 else 1).start()

        for n in range(apart):
            part = jnp.dot(attended, wo_v[:, n * tile : (n + 1) * tile], preferred_element_type=jnp.float32)
            if j == 0:
                for k in (2, 3):
                    mine = part[(k - 2) * rows : (k - 1) * rows]
                    part_v[k, n] = mine
                    part_s[k, n] = mine.astype(jnp.bfloat16)

                @pl.when(jnp.logical_not(middle))
                def _():
                    pair_to(3, n).start()
            else:
                part_s[1, n] = part[:rows].astype(jnp.bfloat16)
                near_to(n).start()
                part_v[0, n] = part[rows:]
        if j == 0:
            @pl.when(jnp.logical_not(middle))
            def _():
                full_to(2).start()
                for n in range(apart):
                    pair_to(2, n).start()

            @pl.when(middle)
            def _():
                for n in range(apart, parts):
                    part = jnp.dot(attended, wo_v[:, n * tile : (n + 1) * tile], preferred_element_type=jnp.float32)
                    for k in (2, 3):
                        part_v[k, n] = part[(k - 2) * rows : (k - 1) * rows]
        else:
            for n in range(apart, parts):
                part = jnp.dot(attended, wo_v[:, n * tile : (n + 1) * tile], preferred_element_type=jnp.float32)
                part_s[1, n] = part[:rows].astype(jnp.bfloat16)

                @pl.when(middle)
                def _():
                    near_to(n).start()

                part_v[0, n] = part[rows:]

    finish(0)
    finish(1)

    @pl.when(middle)
    def _():
        relay(1)

    loads[7].wait()
    project(0)
    project(1)

    def twin(k, n):
        cols = slice((n - apart) * tile, (n - apart + 1) * tile)
        return jnp.dot(full_r[k], twin_v[:, cols], preferred_element_type=jnp.float32)

    @pl.when(middle)
    def _():
        for k in (3, 2):
            full_to(k).wait_recv()
            for n in range(apart, parts):
                if k == 3:
                    if n == apart:
                        whole(0)
                    if n == (apart + parts) // 2:
                        whole(1)
                part_s[k, n] = (part_v[k, n] + twin(k, n)).astype(jnp.bfloat16)
                far_to(k, n).start()
            for n in range(apart):
                pair_to(k, n).wait_recv()
                part_s[k, n] = (part_v[k, n] + pair_r[k - 2, n].astype(jnp.float32)).astype(jnp.bfloat16)
                far_to(k, n).start()
        full_to(1).wait_recv()
        for n in range(apart, parts):
            part_v[0, n] += twin(1, n)

    def settle(n, extra):
        total = part_v[0, n] + far_r[n].astype(jnp.float32)
        if extra:
            total = total + near_r[n].astype(jnp.float32)
        cols = slice(n * tile, (n + 1) * tile)
        out[:, cols] = (tok[:, cols].astype(jnp.float32) + gate[:, cols] * total).astype(jnp.bfloat16)

    for n in range(apart, parts):
        far_to(2, n).wait_recv()

        @pl.when(middle)
        def _():
            settle(n, False)

        @pl.when(jnp.logical_not(middle))
        def _():
            near_to(n).wait_recv()
            settle(n, True)

    for n in range(apart):
        far_to(2, n).wait_recv()
        near_to(n).wait_recv()
        settle(n, True)

    for c in range(chunks):
        gather(0, c).wait_send()

    @pl.when(middle)
    def _():
        for c in range(chunks):
            gather(1, c).wait_send()
            across(c).wait_send()
        for k in (2, 3):
            for c in range(chunks):
                forward(k, c).wait_send()

    def sent(i, carry):
        b = lax.rem(mb + 1 + lax.rem(i, nb - 1), nb)
        k = i // (nb - 1)
        heads_to(k, 0, b).wait_send()
        heads_to(k, 1, b).wait_send()
        return carry

    lax.fori_loop(0, 4 * (nb - 1), sent, 0)
    for j in (0, 1):
        for i in range(1, nb):
            back_to(j, lax.rem(mb + i, nb)).wait_send()
    for k in (1, 2, 3):
        for n in range(apart):
            near_to(n).wait_send() if k == 1 else pair_to(k, n).wait_send()

    @pl.when(middle)
    def _():
        for k in (1, 2, 3):
            for n in range(apart, parts):
                near_to(n).wait_send() if k == 1 else pair_to(k, n).wait_send()
        for p in (0, 1):
            for j in range(nb // 2):
                twin_share(p, j).wait_send()
            for j in range(1, nb // 2):
                twin_pass(p, j).wait_send()

    @pl.when(jnp.logical_not(middle))
    def _():
        twin_out(0).wait_send()
        twin_out(1).wait_send()
        for k in (1, 2, 3):
            full_to(k).wait_send()


def fused(nb, tokens, mod_shift, mod_scale, mod_gate, w_query, w_key, w_value, w_out, score_gain):
    rows = tokens.shape[0]
    cols = w_query.shape[1]
    chunks = 4
    tile = 512
    parts = D // tile
    span = nb * rows
    most = -(-rows // 32) * 16
    bf16, f32 = jnp.bfloat16, jnp.float32
    vmem = pl.BlockSpec(memory_space=pltpu.VMEM)
    hbm = pl.BlockSpec(memory_space=pltpu.HBM)
    dma = pltpu.SemaphoreType.DMA
    return pl.pallas_call(
        functools.partial(kernel, nb),
        out_shape=jax.ShapeDtypeStruct((rows, D), bf16),
        in_specs=[hbm] * 9,
        out_specs=vmem,
        scratch_shapes=[
            pltpu.VMEM((rows, D), bf16),
            pltpu.VMEM((1, D), f32),
            pltpu.VMEM((1, D), f32),
            pltpu.VMEM((1, D), f32),
            pltpu.VMEM((1, HEADS), f32),
            pltpu.VMEM((4, chunks, rows, D // chunks), bf16),
            pltpu.VMEM((D, cols), bf16),
            pltpu.VMEM((D, cols), bf16),
            pltpu.VMEM((D, cols), bf16),
            pltpu.VMEM((cols, D), bf16),
            pltpu.VMEM((4, nb, rows, 128), bf16),
            pltpu.VMEM((4, nb, most, 128), bf16),
            pltpu.VMEM((4 * span, 128), bf16),
            pltpu.VMEM((4 * nb * most, 128), bf16),
            pltpu.VMEM((4 * span, 128), bf16),
            pltpu.VMEM((64, 4 * span), bf16),
            pltpu.VMEM((4, 1, span), f32),
            pltpu.VMEM((4, 1, span), f32),
            pltpu.VMEM((4, 64, span), f32),
            pltpu.VMEM((2, span, 128), bf16),
            pltpu.VMEM((2, nb, rows, 128), bf16),
            pltpu.VMEM((4, rows, cols), bf16),
            pltpu.VMEM((4, rows, cols), bf16),
            pltpu.VMEM((cols, TWIN), bf16),
            pltpu.VMEM((4, parts, rows, tile), f32),
            pltpu.VMEM((4, parts, rows, tile), bf16),
            pltpu.VMEM((2, parts, rows, tile), bf16),
            pltpu.VMEM((parts, rows, tile), bf16),
            pltpu.VMEM((parts, rows, tile), bf16),
            dma((9,)),
            dma((2, chunks)),
            dma((4, chunks)),
            dma((4, chunks)),
            dma((4, 2, nb)),
            dma((4, 2, nb)),
            dma((2, nb)),
            dma((2, nb)),
            dma((4, parts)),
            dma((4, parts)),
            dma((4,)),
            dma((4,)),
            dma((2, 2, nb // 2)),
            dma((2, nb)),
        ],
        compiler_params=pltpu.CompilerParams(
            collective_id=0, has_side_effects=True, vmem_limit_bytes=56 * 1024 * 1024
        ),
    )(
        tokens, mod_shift[None], mod_scale[None], mod_gate[None], score_gain[None],
        w_query, w_key, w_value, w_out,
    )


def modulate(tokens, mod_shift, mod_scale):
    values = tokens.astype(jnp.float32)
    center = values - jnp.mean(values, axis=-1, keepdims=True)
    spread = jnp.mean(center * center, axis=-1, keepdims=True)
    normed = center * lax.rsqrt(spread + 1e-06)
    return (normed * (1.0 + mod_scale) + mod_shift).astype(jnp.bfloat16)


def head_norm(projected, width):
    count = projected.shape[0]
    split = projected.reshape(count, -1, width)
    power = jnp.mean(split * split, axis=-1, keepdims=True)
    return (split * lax.rsqrt(power + 1e-06)).reshape(count, -1).astype(jnp.bfloat16)


def body(tokens, mod_shift, mod_scale, mod_gate, w_query, w_key, w_value, w_out, score_gain):
    width = D // HEADS
    local_cols = w_query.shape[1]
    local_heads = local_cols // width
    modded = modulate(tokens, mod_shift, mod_scale)
    piece = lax.all_gather(modded, "uly", axis=0, tiled=True)
    joined = jnp.concatenate(
        [
            jnp.dot(piece, w_query, preferred_element_type=jnp.float32),
            jnp.dot(piece, w_key, preferred_element_type=jnp.float32),
            jnp.dot(piece, w_value, preferred_element_type=jnp.float32),
        ],
        axis=1,
    )
    queries = head_norm(joined[:, :local_cols], width)
    keys = head_norm(joined[:, local_cols : 2 * local_cols], width)
    values = joined[:, 2 * local_cols :].astype(jnp.bfloat16)
    gains = lax.dynamic_slice_in_dim(score_gain, lax.axis_index("uly") * local_heads, local_heads)
    factors = gains / math.sqrt(width)
    rows = queries.shape[0]
    query_heads = queries.reshape(rows, local_heads, width)
    initial = (
        jnp.full((local_heads, rows), -jnp.inf, jnp.float32),
        jnp.zeros((local_heads, rows), jnp.float32),
        jnp.zeros((local_heads, rows, width), jnp.float32),
    )
    key_piece = lax.all_gather(keys, "blk", axis=0, tiled=True)
    value_piece = lax.all_gather(values, "blk", axis=0, tiled=True)
    count = key_piece.shape[0]
    groups = count // rows
    limit = max(rows, 1024)
    depth = max(
        [step for step in range(1, groups + 1) if groups % step == 0 and step * rows <= limit]
    )
    stride = depth * rows
    key_blocks = key_piece.reshape(count // stride, stride, local_heads, width)
    value_blocks = value_piece.reshape(count // stride, stride, local_heads, width)

    def one_block(carry, blocks):
        run_max, run_total, run_acc = carry
        key_block, value_block = blocks
        scores = jnp.einsum(
            "rhd,khd->hrk", query_heads, key_block, preferred_element_type=jnp.float32
        )
        scores = scores * factors[:, None, None]
        new_max = jnp.maximum(run_max, jnp.max(scores, axis=-1))
        expo = jnp.exp(scores - new_max[..., None])
        rescale = jnp.exp(run_max - new_max)
        new_total = run_total * rescale + jnp.sum(expo, axis=-1)
        summed = jnp.einsum(
            "hrk,khd->hrd",
            expo.astype(jnp.bfloat16),
            value_block,
            preferred_element_type=jnp.float32,
        )
        new_acc = run_acc * rescale[..., None] + summed
        return ((new_max, new_total, new_acc), None)

    result, unused = lax.scan(one_block, initial, (key_blocks, value_blocks))
    run_max, run_total, run_acc = result
    attended = (run_acc / run_total[..., None]).astype(jnp.bfloat16)
    attended = attended.transpose(1, 0, 2).reshape(rows, local_cols)
    returned = lax.all_to_all(attended, "uly", split_axis=0, concat_axis=1, tiled=True)
    projected = jnp.dot(
        returned,
        lax.all_gather(w_out, "uly", axis=0, tiled=True),
        preferred_element_type=jnp.float32,
    )
    return (tokens.astype(jnp.float32) + mod_gate * projected).astype(jnp.bfloat16)


def solution(mesh):
    in_specs = (
        P(("blk", "uly"), None),
        P(),
        P(),
        P(),
        P(None, "uly"),
        P(None, "uly"),
        P(None, "uly"),
        P("uly", None),
        P(),
    )
    out_specs = P(("blk", "uly"), None)
    nb, nz = mesh.shape["blk"], mesh.shape["uly"]
    run = body
    if HEADS == nb * nz and nz == 4 and nb % 2 == 0:
        run = functools.partial(fused, nb)
    return jax.shard_map(run, mesh=mesh, in_specs=in_specs, out_specs=out_specs, check_vma=False)
```

```python
import functools
import math

import jax
import jax.numpy as jnp
from jax import lax
from jax.experimental import pallas as pl
from jax.experimental.pallas import tpu as pltpu
from jax.sharding import PartitionSpec as P

D = 2048
HEADS = 32
LOG2E = math.log2(math.e)
MESH = pl.DeviceIdType.MESH
SUB = 384
TWIN = 1024


def kernel(
    nb, tok_h, shift_h, scale_h, gate_h, gain_h, wq, wk, wv, wo, out,
    tok, shift, scale, gate, gain, mod, wq_v, wk_v, wv_v, wo_v, kv_s, q_s, kv_r, q_r, q_v, vt, top_v, sum_v, acc_v,
    att_s, att_r, full_v, full_r, twin_v, part_v, part_s, pair_r, near_r, far_r,
    wsem, gs, gr, fs, hs, hr, bs, br, rs, rr, es, er, ts, tr,
):
    width = D // HEADS
    rows = tok.shape[0]
    span = nb * rows
    chunks = mod.shape[1]
    deep = mod.shape[3]
    tile = part_s.shape[-1]
    parts = D // tile
    apart = parts - twin_v.shape[1] // tile
    mb, mz = lax.axis_index("blk"), lax.axis_index("uly")
    high = mz // 2
    middle = (mz + 1) // 2 == 1
    near = mz + 1 - 2 * lax.rem(mz, 2)
    inner = 2 - high
    outer = 3 - 3 * high

    barrier = pltpu.get_barrier_semaphore()
    for z in (inner, near):
        pl.semaphore_signal(barrier, inc=1, device_id={"uly": z}, device_id_type=MESH)

    @pl.when(middle)
    def _():
        pl.semaphore_signal(barrier, inc=1, device_id={"uly": outer}, device_id_type=MESH)

    for j in range(1, nb):
        pl.semaphore_signal(barrier, inc=1, device_id={"blk": lax.rem(mb + j, nb)}, device_id_type=MESH)

    pairs = (
        (tok_h, tok), (shift_h, shift), (scale_h, scale), (wk, wk_v), (wv, wv_v), (wq, wq_v),
        (wo, wo_v), (gate_h, gate), (gain_h, gain),
    )
    loads = [
        pltpu.make_async_copy(src, dst, wsem.at[i])
        for i, (src, dst) in enumerate(pairs)
    ]
    for load in loads:
        load.start()
    for load in loads[:3]:
        load.wait()

    values = tok[...].astype(jnp.float32)
    center = values - jnp.mean(values, axis=-1, keepdims=True)
    spread = jnp.mean(center * center, axis=-1, keepdims=True)
    normed = center * lax.rsqrt(spread + 1e-06)
    modded = (normed * (1.0 + scale[...]) + shift[...]).astype(jnp.bfloat16)
    for c in range(chunks):
        mod[0, c] = modded[:, c * deep : (c + 1) * deep]

    pl.semaphore_wait(barrier, nb + 1 + middle.astype(jnp.int32))

    def gather(way, c):
        slot = 1 + way
        return pltpu.make_async_remote_copy(
            src_ref=mod.at[0, c], dst_ref=mod.at[slot, c], send_sem=gs.at[way, c], recv_sem=gr.at[slot, c],
            device_id={"uly": inner if way else near}, device_id_type=MESH)

    def landed(k, c):
        return pltpu.make_async_remote_copy(
            src_ref=mod.at[0, c], dst_ref=mod.at[k, c], send_sem=gs.at[0, c], recv_sem=gr.at[k, c],
            device_id={"uly": near}, device_id_type=MESH)

    def forward(k, c):
        return pltpu.make_async_remote_copy(
            src_ref=mod.at[k, c], dst_ref=mod.at[k, c], send_sem=fs.at[k, c], recv_sem=gr.at[k, c],
            device_id={"uly": near}, device_id_type=MESH)

    def across(c):
        return pltpu.make_async_remote_copy(
            src_ref=mod.at[1, c], dst_ref=mod.at[3, c], send_sem=fs.at[1, c], recv_sem=gr.at[3, c],
            device_id={"uly": inner}, device_id_type=MESH)

    @pl.when(middle)
    def _():
        for c in range(chunks):
            for way in (0, 1):
                gather(way, c).start()

    @pl.when(jnp.logical_not(middle))
    def _():
        for c in range(chunks):
            gather(0, c).start()

    for load in loads[3:6]:
        load.wait()

    most = q_s.shape[2]

    def lower(k, b):
        return pl.ds(pl.multiple_of((k * nb + b) * most, most), most)

    def place(k, b):
        return pl.ds(pl.multiple_of(k * span + b * rows, rows), rows)

    depth = wo_v.shape[0] // nb
    sibling = mb + 1 - 2 * lax.rem(mb, 2)

    def slab(b):
        return pl.ds(pl.multiple_of(b * depth, depth), depth)

    half = twin_v.shape[1] // 2

    def twin_copy(p, b, send, who, src=None):
        here = twin_v.at[slab(b), p * half : (p + 1) * half]
        return pltpu.make_async_remote_copy(
            src_ref=here if src is None else src, dst_ref=here, send_sem=send, recv_sem=tr.at[p, b],
            device_id=who, device_id_type=MESH)

    def twin_out(p):
        left = apart * tile + p * half
        return twin_copy(p, mb, ts.at[p, 0, 0], {"uly": near}, wo_v.at[slab(mb), left : left + half])

    def twin_in(p, b):
        return twin_copy(p, b, ts.at[p, 0, 0], {"uly": near})

    def twin_share(p, j):
        return twin_copy(p, mb, ts.at[p, 0, j], {"blk": sibling if j == 0 else lax.rem(mb + 2 * j, nb)})

    def twin_pass(p, j):
        return twin_copy(p, lax.rem(mb + 2 * j, nb), ts.at[p, 1, j], {"blk": sibling})

    def share(p):
        twin_in(p, mb).wait_recv()
        for j in range(1, nb // 2):
            twin_share(p, j).start()
        twin_share(p, 0).start()

    def relay(p):
        for j in range(1, nb // 2):
            twin_in(p, lax.rem(mb + 2 * j, nb)).wait_recv()
            twin_pass(p, j).start()

    def whole(p):
        twin_in(p, sibling).wait_recv()
        for j in range(1, nb // 2):
            twin_in(p, lax.rem(sibling + 2 * j, nb)).wait_recv()

    def full_to(k):
        return pltpu.make_async_remote_copy(
            src_ref=full_v.at[k], dst_ref=full_r.at[k], send_sem=es.at[k], recv_sem=er.at[k],
            device_id={"uly": near}, device_id_type=MESH)

    def heads_to(k, kind, b):
        src, dst, where = ((kv_s, kv_r, place), (q_s, q_r, lower))[kind]
        return pltpu.make_async_remote_copy(
            src_ref=src.at[k, b], dst_ref=dst.at[where(k, mb), :], send_sem=hs.at[k, kind, b],
            recv_sem=hr.at[k, kind, mb], device_id={"blk": b}, device_id_type=MESH)

    def heads_from(k, kind, b):
        src, dst, where = ((kv_s, kv_r, place), (q_s, q_r, lower))[kind]
        return pltpu.make_async_remote_copy(
            src_ref=src.at[k, b], dst_ref=dst.at[where(k, b), :], send_sem=hs.at[k, kind, b],
            recv_sem=hr.at[k, kind, b], device_id={"blk": b}, device_id_type=MESH)

    loads[8].wait()
    chosen = lax.broadcasted_iota(jnp.int32, gain.shape, 1) == mz * nb + mb
    factor = jnp.sum(jnp.where(chosen, gain[...], 0.0), axis=-1, keepdims=True) * (LOG2E / math.sqrt(width))

    def await_heads(k, kind):
        for j in range(1, nb):
            heads_from(k, kind, lax.rem(mb + j, nb)).wait_recv()

    def flip(k):
        vt[:, k * span : (k + 1) * span] = kv_r[k * span : (k + 1) * span, :].T[width:, :]

    def widen(k):
        for b in range(nb):
            both = q_r[(k * nb + b) * most : (k * nb + b + 1) * most, :]
            clear = jnp.zeros((most, width), jnp.bfloat16)
            start = k * span + b * rows
            q_v[start : start + most, :] = jnp.concatenate([both[:, :width], clear], axis=1)
            q_v[start + most : start + rows, :] = jnp.concatenate(
                [both[: rows - most, width:], clear[: rows - most]], axis=1)

    def scored(k, c, first, last):
        q = q_v[k * span + c * SUB : k * span + (c + 1) * SUB, :]
        return lax.dot_general(
            kv_r[first * span : last * span, :], q, (((1,), (1,)), ((), ())), preferred_element_type=jnp.float32)

    def begin(k, c, first, last):
        scores = scored(k, c, first, last)
        top = jnp.max(scores, axis=0, keepdims=True)
        expo = jnp.exp2((scores - top) * factor)
        total = jnp.sum(expo, axis=0, keepdims=True)
        summed = jnp.dot(vt[:, first * span : last * span], expo.astype(jnp.bfloat16), preferred_element_type=jnp.float32)
        return top, total, summed

    def keep(k, first, last):
        for c in range(span // SUB):
            cols = slice(c * SUB, (c + 1) * SUB)
            top_v[k, :, cols], sum_v[k, :, cols], acc_v[k, :, cols] = begin(k, c, first, last)

    def more(k, c, first, last):
        cols = slice(c * SUB, (c + 1) * SUB)
        scores = scored(k, c, first, last)
        old = top_v[k, :, cols]
        top = jnp.maximum(old, jnp.max(scores, axis=0, keepdims=True))
        shrink = jnp.exp2((old - top) * factor)
        expo = jnp.exp2((scores - top) * factor)
        total = sum_v[k, :, cols] * shrink + jnp.sum(expo, axis=0, keepdims=True)
        summed = jnp.dot(vt[:, first * span : last * span], expo.astype(jnp.bfloat16), preferred_element_type=jnp.float32)
        return total, acc_v[k, :, cols] * shrink + summed

    def first_attend():
        for k in (0, 1):
            await_heads(k, 0)
            await_heads(k, 1)
            flip(k)
            widen(k)
        for k in (0, 1):
            keep(k, 0, 2)

    def piece(k, carry):
        @pl.when((k == 3) & jnp.logical_not(middle))
        def _():
            first_attend()

        @pl.when((k == 1) & jnp.logical_not(middle))
        def _():
            loads[6].wait()
            twin_out(0).start()
            twin_out(1).start()

        query = key = value = None
        for c in range(chunks):
            @pl.when((k > 0) & (jnp.logical_not(middle) | (k == 1)))
            def _():
                landed(k, c).wait_recv()

            @pl.when(middle & (k == 1))
            def _():
                across(c).start()

            @pl.when(middle & (k > 0) & (k < 3))
            def _():
                landed(k + 1, c).wait_recv()
                forward(k + 1, c).start()

            if c == 1:
                @pl.when(middle & (k == 2))
                def _():
                    share(0)

            x = mod[k, c]
            deeps = slice(c * deep, (c + 1) * deep)
            more_q = jnp.dot(x, wq_v[deeps, :], preferred_element_type=jnp.float32)
            query = more_q if c == 0 else query + more_q
            if c < chunks - 1:
                more_k = jnp.dot(x, wk_v[deeps, :], preferred_element_type=jnp.float32)
                more_v = jnp.dot(x, wv_v[deeps, :], preferred_element_type=jnp.float32)
                key = more_k if c == 0 else key + more_k
                value = more_v if c == 0 else value + more_v

        def unit(part):
            power = jnp.mean(part * part, axis=-1, keepdims=True)
            return part * lax.rsqrt(power + 1e-06)

        def send(kind):
            def one(j, carry):
                heads_to(k, kind, lax.rem(mb + j, nb)).start()
                return carry

            lax.fori_loop(1, nb, one, 0)

        for h in range(nb):
            cols = slice(h * width, (h + 1) * width)
            line = unit(query[:, cols])
            rest = jnp.concatenate([line[most:], jnp.zeros((2 * most - rows, width), jnp.float32)], axis=0)
            q_s[k, h] = jnp.concatenate([line[:most], rest], axis=1).astype(jnp.bfloat16)
        send(1)
        q_r[lower(k, mb), :] = q_s[k, mb]
        key = key + jnp.dot(x, wk_v[deeps, :], preferred_element_type=jnp.float32)
        value = value + jnp.dot(x, wv_v[deeps, :], preferred_element_type=jnp.float32)
        for h in range(nb):
            cols = slice(h * width, (h + 1) * width)
            kv_s[k, h] = jnp.concatenate([unit(key[:, cols]), value[:, cols]], axis=1).astype(jnp.bfloat16)
        send(0)
        kv_r[place(k, mb), :] = kv_s[k, mb]
        return carry

    lax.fori_loop(0, 4, piece, 0)

    @pl.when(middle)
    def _():
        loads[6].wait()
        share(1)
        first_attend()

    await_heads(2, 0)
    await_heads(2, 1)
    flip(2)
    widen(2)
    keep(2, 0, 3)
    @pl.when(middle)
    def _():
        relay(0)

    await_heads(3, 1)
    widen(3)
    keep(3, 0, 3)
    await_heads(3, 0)
    flip(3)

    def back_to(j, b):
        return pltpu.make_async_remote_copy(
            src_ref=att_s.at[j, pl.ds(pl.multiple_of(b * rows, rows), rows), :], dst_ref=att_r.at[j, mb],
            send_sem=bs.at[j, b], recv_sem=br.at[j, mb], device_id={"blk": b}, device_id_type=MESH)

    def back_from(j, b):
        return pltpu.make_async_remote_copy(
            src_ref=att_s.at[j, pl.ds(pl.multiple_of(b * rows, rows), rows), :], dst_ref=att_r.at[j, b],
            send_sem=bs.at[j, b], recv_sem=br.at[j, b], device_id={"blk": b}, device_id_type=MESH)

    def finished(k, c):
        total, summed = more(k, c, 3 if k > 1 else 2, 4)
        return summed / total

    def finish(j):
        if j == 0:
            lower = [finished(2, c) for c in range(span // SUB)]
            upper = [finished(3, c) for c in range(span // SUB)]
        else:
            lower = [finished(1, c) for c in range(span // SUB)]
            upper = [finished(0, c) for c in range(span // SUB)]
        for c in range(span // SUB):
            both = jnp.concatenate([lower[c], upper[c]], axis=0)
            att_s[j, c * SUB : (c + 1) * SUB, :] = both.T.astype(jnp.bfloat16)

        def one(i, carry):
            back_to(j, lax.rem(mb + i, nb)).start()
            return carry

        lax.fori_loop(1, nb, one, 0)
        att_r[j, mb] = att_s[j, pl.ds(pl.multiple_of(mb * rows, rows), rows), :]

    def near_to(n):
        return pltpu.make_async_remote_copy(
            src_ref=part_s.at[1, n], dst_ref=near_r.at[n], send_sem=rs.at[1, n], recv_sem=rr.at[1, n],
            device_id={"uly": near}, device_id_type=MESH)

    def pair_to(k, n):
        return pltpu.make_async_remote_copy(
            src_ref=part_s.at[k, n], dst_ref=pair_r.at[k - 2, n], send_sem=rs.at[k, n], recv_sem=rr.at[k, n],
            device_id={"uly": near}, device_id_type=MESH)

    def far_to(k, n):
        return pltpu.make_async_remote_copy(
            src_ref=part_s.at[k, n], dst_ref=far_r.at[n], send_sem=rs.at[k, n], recv_sem=rr.at[0, n],
            device_id={"uly": inner if k == 2 else outer}, device_id_type=MESH)

    def project(j):
        for i in range(1, nb):
            back_from(j, lax.rem(mb + i, nb)).wait_recv()
        pieces = [att_r[j, h] for h in range(nb)]
        attended = jnp.concatenate(
            [
                jnp.concatenate([one[:, :width] for one in pieces], axis=1),
                jnp.concatenate([one[:, width:] for one in pieces], axis=1),
            ],
            axis=0,
        )
        if j == 0:
            full_v[2] = attended[:rows]
            full_v[3] = attended[rows:]
        else:
            full_v[1] = attended[:rows]

        @pl.when(jnp.logical_not(middle))
        def _():
            full_to(3 if j == 0 else 1).start()

        for n in range(apart):
            part = jnp.dot(attended, wo_v[:, n * tile : (n + 1) * tile], preferred_element_type=jnp.float32)
            if j == 0:
                for k in (2, 3):
                    mine = part[(k - 2) * rows : (k - 1) * rows]
                    part_v[k, n] = mine
                    part_s[k, n] = mine.astype(jnp.bfloat16)

                @pl.when(jnp.logical_not(middle))
                def _():
                    pair_to(3, n).start()
            else:
                part_s[1, n] = part[:rows].astype(jnp.bfloat16)
                near_to(n).start()
                part_v[0, n] = part[rows:]
        if j == 0:
            @pl.when(jnp.logical_not(middle))
            def _():
                full_to(2).start()
                for n in range(apart):
                    pair_to(2, n).start()

            @pl.when(middle)
            def _():
                for n in range(apart, parts):
                    part = jnp.dot(attended, wo_v[:, n * tile : (n + 1) * tile], preferred_element_type=jnp.float32)
                    for k in (2, 3):
                        part_v[k, n] = part[(k - 2) * rows : (k - 1) * rows]
        else:
            for n in range(apart, parts):
                part = jnp.dot(attended, wo_v[:, n * tile : (n + 1) * tile], preferred_element_type=jnp.float32)
                part_s[1, n] = part[:rows].astype(jnp.bfloat16)

                @pl.when(middle)
                def _():
                    near_to(n).start()

                part_v[0, n] = part[rows:]

    finish(0)
    finish(1)

    @pl.when(middle)
    def _():
        relay(1)

    loads[7].wait()
    project(0)
    project(1)

    def twin(k, n):
        cols = slice((n - apart) * tile, (n - apart + 1) * tile)
        return jnp.dot(full_r[k], twin_v[:, cols], preferred_element_type=jnp.float32)

    @pl.when(middle)
    def _():
        for k in (3, 2):
            full_to(k).wait_recv()
            for n in range(apart, parts):
                if k == 3:
                    if n == apart:
                        whole(0)
                    if n == (apart + parts) // 2:
                        whole(1)
                part_s[k, n] = (part_v[k, n] + twin(k, n)).astype(jnp.bfloat16)
                far_to(k, n).start()
            for n in range(apart):
                pair_to(k, n).wait_recv()
                part_s[k, n] = (part_v[k, n] + pair_r[k - 2, n].astype(jnp.float32)).astype(jnp.bfloat16)
                far_to(k, n).start()
        full_to(1).wait_recv()
        for n in range(apart, parts):
            part_v[0, n] += twin(1, n)

    def settle(n, extra):
        total = part_v[0, n] + far_r[n].astype(jnp.float32)
        if extra:
            total = total + near_r[n].astype(jnp.float32)
        cols = slice(n * tile, (n + 1) * tile)
        out[:, cols] = (tok[:, cols].astype(jnp.float32) + gate[:, cols] * total).astype(jnp.bfloat16)

    for n in range(apart, parts):
        far_to(2, n).wait_recv()

        @pl.when(middle)
        def _():
            settle(n, False)

        @pl.when(jnp.logical_not(middle))
        def _():
            near_to(n).wait_recv()
            settle(n, True)

    for n in range(apart):
        far_to(2, n).wait_recv()
        near_to(n).wait_recv()
        settle(n, True)

    for c in range(chunks):
        gather(0, c).wait_send()

    @pl.when(middle)
    def _():
        for c in range(chunks):
            gather(1, c).wait_send()
            across(c).wait_send()
        for k in (2, 3):
            for c in range(chunks):
                forward(k, c).wait_send()

    def sent(i, carry):
        b = lax.rem(mb + 1 + lax.rem(i, nb - 1), nb)
        k = i // (nb - 1)
        heads_to(k, 0, b).wait_send()
        heads_to(k, 1, b).wait_send()
        return carry

    lax.fori_loop(0, 4 * (nb - 1), sent, 0)
    for j in (0, 1):
        for i in range(1, nb):
            back_to(j, lax.rem(mb + i, nb)).wait_send()
    for k in (1, 2, 3):
        for n in range(apart):
            near_to(n).wait_send() if k == 1 else pair_to(k, n).wait_send()

    @pl.when(middle)
    def _():
        for k in (1, 2, 3):
            for n in range(apart, parts):
                near_to(n).wait_send() if k == 1 else pair_to(k, n).wait_send()
        for p in (0, 1):
            for j in range(nb // 2):
                twin_share(p, j).wait_send()
            for j in range(1, nb // 2):
                twin_pass(p, j).wait_send()

    @pl.when(jnp.logical_not(middle))
    def _():
        twin_out(0).wait_send()
        twin_out(1).wait_send()
        for k in (1, 2, 3):
            full_to(k).wait_send()


def fused(nb, tokens, mod_shift, mod_scale, mod_gate, w_query, w_key, w_value, w_out, score_gain):
    rows = tokens.shape[0]
    cols = w_query.shape[1]
    chunks = 4
    tile = 512
    parts = D // tile
    span = nb * rows
    most = -(-rows // 32) * 16
    bf16, f32 = jnp.bfloat16, jnp.float32
    vmem = pl.BlockSpec(memory_space=pltpu.VMEM)
    hbm = pl.BlockSpec(memory_space=pltpu.HBM)
    dma = pltpu.SemaphoreType.DMA
    return pl.pallas_call(
        functools.partial(kernel, nb),
        out_shape=pltpu.VMEM((rows, D), bf16),
        in_specs=[hbm] * 9,
        out_specs=vmem,
        scratch_shapes=[
            pltpu.VMEM((rows, D), bf16),
            pltpu.VMEM((1, D), f32),
            pltpu.VMEM((1, D), f32),
            pltpu.VMEM((1, D), f32),
            pltpu.VMEM((1, HEADS), f32),
            pltpu.VMEM((4, chunks, rows, D // chunks), bf16),
            pltpu.VMEM((D, cols), bf16),
            pltpu.VMEM((D, cols), bf16),
            pltpu.VMEM((D, cols), bf16),
            pltpu.VMEM((cols, D), bf16),
            pltpu.VMEM((4, nb, rows, 128), bf16),
            pltpu.VMEM((4, nb, most, 128), bf16),
            pltpu.VMEM((4 * span, 128), bf16),
            pltpu.VMEM((4 * nb * most, 128), bf16),
            pltpu.VMEM((4 * span, 128), bf16),
            pltpu.VMEM((64, 4 * span), bf16),
            pltpu.VMEM((4, 1, span), f32),
            pltpu.VMEM((4, 1, span), f32),
            pltpu.VMEM((4, 64, span), f32),
            pltpu.VMEM((2, span, 128), bf16),
            pltpu.VMEM((2, nb, rows, 128), bf16),
            pltpu.VMEM((4, rows, cols), bf16),
            pltpu.VMEM((4, rows, cols), bf16),
            pltpu.VMEM((cols, TWIN), bf16),
            pltpu.VMEM((4, parts, rows, tile), f32),
            pltpu.VMEM((4, parts, rows, tile), bf16),
            pltpu.VMEM((2, parts, rows, tile), bf16),
            pltpu.VMEM((parts, rows, tile), bf16),
            pltpu.VMEM((parts, rows, tile), bf16),
            dma((9,)),
            dma((2, chunks)),
            dma((4, chunks)),
            dma((4, chunks)),
            dma((4, 2, nb)),
            dma((4, 2, nb)),
            dma((2, nb)),
            dma((2, nb)),
            dma((4, parts)),
            dma((4, parts)),
            dma((4,)),
            dma((4,)),
            dma((2, 2, nb // 2)),
            dma((2, nb)),
        ],
        compiler_params=pltpu.CompilerParams(
            collective_id=0, has_side_effects=True, vmem_limit_bytes=56 * 1024 * 1024
        ),
    )(
        tokens, mod_shift[None], mod_scale[None], mod_gate[None], score_gain[None],
        w_query, w_key, w_value, w_out,
    )


def modulate(tokens, mod_shift, mod_scale):
    values = tokens.astype(jnp.float32)
    center = values - jnp.mean(values, axis=-1, keepdims=True)
    spread = jnp.mean(center * center, axis=-1, keepdims=True)
    normed = center * lax.rsqrt(spread + 1e-06)
    return (normed * (1.0 + mod_scale) + mod_shift).astype(jnp.bfloat16)


def head_norm(projected, width):
    count = projected.shape[0]
    split = projected.reshape(count, -1, width)
    power = jnp.mean(split * split, axis=-1, keepdims=True)
    return (split * lax.rsqrt(power + 1e-06)).reshape(count, -1).astype(jnp.bfloat16)


def body(tokens, mod_shift, mod_scale, mod_gate, w_query, w_key, w_value, w_out, score_gain):
    width = D // HEADS
    local_cols = w_query.shape[1]
    local_heads = local_cols // width
    modded = modulate(tokens, mod_shift, mod_scale)
    piece = lax.all_gather(modded, "uly", axis=0, tiled=True)
    joined = jnp.concatenate(
        [
            jnp.dot(piece, w_query, preferred_element_type=jnp.float32),
            jnp.dot(piece, w_key, preferred_element_type=jnp.float32),
            jnp.dot(piece, w_value, preferred_element_type=jnp.float32),
        ],
        axis=1,
    )
    queries = head_norm(joined[:, :local_cols], width)
    keys = head_norm(joined[:, local_cols : 2 * local_cols], width)
    values = joined[:, 2 * local_cols :].astype(jnp.bfloat16)
    gains = lax.dynamic_slice_in_dim(score_gain, lax.axis_index("uly") * local_heads, local_heads)
    factors = gains / math.sqrt(width)
    rows = queries.shape[0]
    query_heads = queries.reshape(rows, local_heads, width)
    initial = (
        jnp.full((local_heads, rows), -jnp.inf, jnp.float32),
        jnp.zeros((local_heads, rows), jnp.float32),
        jnp.zeros((local_heads, rows, width), jnp.float32),
    )
    key_piece = lax.all_gather(keys, "blk", axis=0, tiled=True)
    value_piece = lax.all_gather(values, "blk", axis=0, tiled=True)
    count = key_piece.shape[0]
    groups = count // rows
    limit = max(rows, 1024)
    depth = max(
        [step for step in range(1, groups + 1) if groups % step == 0 and step * rows <= limit]
    )
    stride = depth * rows
    key_blocks = key_piece.reshape(count // stride, stride, local_heads, width)
    value_blocks = value_piece.reshape(count // stride, stride, local_heads, width)

    def one_block(carry, blocks):
        run_max, run_total, run_acc = carry
        key_block, value_block = blocks
        scores = jnp.einsum(
            "rhd,khd->hrk", query_heads, key_block, preferred_element_type=jnp.float32
        )
        scores = scores * factors[:, None, None]
        new_max = jnp.maximum(run_max, jnp.max(scores, axis=-1))
        expo = jnp.exp(scores - new_max[..., None])
        rescale = jnp.exp(run_max - new_max)
        new_total = run_total * rescale + jnp.sum(expo, axis=-1)
        summed = jnp.einsum(
            "hrk,khd->hrd",
            expo.astype(jnp.bfloat16),
            value_block,
            preferred_element_type=jnp.float32,
        )
        new_acc = run_acc * rescale[..., None] + summed
        return ((new_max, new_total, new_acc), None)

    result, unused = lax.scan(one_block, initial, (key_blocks, value_blocks))
    run_max, run_total, run_acc = result
    attended = (run_acc / run_total[..., None]).astype(jnp.bfloat16)
    attended = attended.transpose(1, 0, 2).reshape(rows, local_cols)
    returned = lax.all_to_all(attended, "uly", split_axis=0, concat_axis=1, tiled=True)
    projected = jnp.dot(
        returned,
        lax.all_gather(w_out, "uly", axis=0, tiled=True),
        preferred_element_type=jnp.float32,
    )
    return (tokens.astype(jnp.float32) + mod_gate * projected).astype(jnp.bfloat16)


def solution(mesh):
    in_specs = (
        P(("blk", "uly"), None),
        P(),
        P(),
        P(),
        P(None, "uly"),
        P(None, "uly"),
        P(None, "uly"),
        P("uly", None),
        P(),
    )
    out_specs = P(("blk", "uly"), None)
    nb, nz = mesh.shape["blk"], mesh.shape["uly"]
    run = body
    if HEADS == nb * nz and nz == 4 and nb % 2 == 0:
        run = functools.partial(fused, nb)
    return jax.shard_map(run, mesh=mesh, in_specs=in_specs, out_specs=out_specs, check_vma=False)
```

```python
import functools
import math

import jax
import jax.numpy as jnp
from jax import lax
from jax.experimental import pallas as pl
from jax.experimental.pallas import tpu as pltpu
from jax.sharding import PartitionSpec as P

D = 2048
HEADS = 32
LOG2E = math.log2(math.e)
MESH = pl.DeviceIdType.MESH
SUB = 384
TWIN = 1024


def kernel(
    nb, tok_h, shift_h, scale_h, gate_h, gain_h, wq, wk, wv, wo, out,
    tok, shift, scale, gate, gain, mod, wq_v, wk_v, wv_v, wo_v, kv_s, q_s, kv_r, q_r, q_v, vt, top_v, sum_v, acc_v,
    att_s, att_r, full_v, full_r, twin_v, part_v, part_s, pair_r, near_r, far_r,
    wsem, gs, gr, fs, hs, hr, bs, br, rs, rr, es, er, ts, tr, ready,
):
    width = D // HEADS
    rows = tok.shape[0]
    span = nb * rows
    chunks = mod.shape[1]
    deep = mod.shape[3]
    tile = part_s.shape[-1]
    parts = D // tile
    apart = parts - twin_v.shape[1] // tile
    mb, mz = lax.axis_index("blk"), lax.axis_index("uly")
    high = mz // 2
    middle = (mz + 1) // 2 == 1
    near = mz + 1 - 2 * lax.rem(mz, 2)
    inner = 2 - high
    outer = 3 - 3 * high

    barrier = pltpu.get_barrier_semaphore()
    core = lax.rem(mb, 2)
    beside = mb + 2 - 4 * lax.rem(mb // 2, 2)
    behind = mb + 4 - 8 * (mb // 4)
    pl.semaphore_signal(barrier, inc=1, device_id={"uly": near}, device_id_type=MESH)

    @pl.when(middle)
    def _():
        pl.semaphore_signal(barrier, inc=1, device_id={"uly": inner}, device_id_type=MESH)

    for b in (mb, beside, behind):
        if b is not mb:
            pl.semaphore_signal(barrier, inc=1, device_id={"blk": b}, device_id_type=MESH)
        pl.semaphore_signal(barrier, inc=1, device_id={"blk": b + 1 - 2 * core}, device_id_type=MESH)

    pairs = (
        (tok_h, tok), (shift_h, shift), (scale_h, scale), (wk, wk_v), (wv, wv_v), (wq, wq_v),
        (wo, wo_v), (gate_h, gate), (gain_h, gain),
    )
    loads = [
        pltpu.make_async_copy(src, dst, wsem.at[i])
        for i, (src, dst) in enumerate(pairs)
    ]
    for load in loads:
        load.start()
    for load in loads[:3]:
        load.wait()

    values = tok[...].astype(jnp.float32)
    center = values - jnp.mean(values, axis=-1, keepdims=True)
    spread = jnp.mean(center * center, axis=-1, keepdims=True)
    normed = center * lax.rsqrt(spread + 1e-06)
    modded = (normed * (1.0 + scale[...]) + shift[...]).astype(jnp.bfloat16)
    for c in range(chunks):
        mod[0, c] = modded[:, c * deep : (c + 1) * deep]

    pl.semaphore_wait(barrier, 6 + middle.astype(jnp.int32))
    pl.semaphore_signal(ready, inc=1, device_id={"blk": beside}, device_id_type=MESH)

    def gather(way, c):
        slot = 1 + way
        return pltpu.make_async_remote_copy(
            src_ref=mod.at[0, c], dst_ref=mod.at[slot, c], send_sem=gs.at[way, c], recv_sem=gr.at[slot, c],
            device_id={"uly": inner if way else near}, device_id_type=MESH)

    def landed(k, c):
        return pltpu.make_async_remote_copy(
            src_ref=mod.at[0, c], dst_ref=mod.at[k, c], send_sem=gs.at[0, c], recv_sem=gr.at[k, c],
            device_id={"uly": near}, device_id_type=MESH)

    def forward(k, c):
        return pltpu.make_async_remote_copy(
            src_ref=mod.at[k, c], dst_ref=mod.at[k, c], send_sem=fs.at[k, c], recv_sem=gr.at[k, c],
            device_id={"uly": near}, device_id_type=MESH)

    def across(c):
        return pltpu.make_async_remote_copy(
            src_ref=mod.at[1, c], dst_ref=mod.at[3, c], send_sem=fs.at[1, c], recv_sem=gr.at[3, c],
            device_id={"uly": inner}, device_id_type=MESH)

    @pl.when(middle)
    def _():
        for c in range(chunks):
            for way in (0, 1):
                gather(way, c).start()

    @pl.when(jnp.logical_not(middle))
    def _():
        for c in range(chunks):
            gather(0, c).start()

    for load in loads[3:6]:
        load.wait()
    pl.semaphore_wait(ready, 1)

    most = q_s.shape[2]

    def lower(k, b):
        return pl.ds(pl.multiple_of((k * nb + b) * most, most), most)

    def place(k, b):
        return pl.ds(pl.multiple_of(k * span + b * rows, rows), rows)

    depth = wo_v.shape[0] // nb
    sibling = mb + 1 - 2 * lax.rem(mb, 2)

    def slab(b):
        return pl.ds(pl.multiple_of(b * depth, depth), depth)

    half = twin_v.shape[1] // 2

    def twin_copy(p, b, send, who, src=None):
        here = twin_v.at[slab(b), p * half : (p + 1) * half]
        return pltpu.make_async_remote_copy(
            src_ref=here if src is None else src, dst_ref=here, send_sem=send, recv_sem=tr.at[p, b],
            device_id=who, device_id_type=MESH)

    def twin_out(p):
        left = apart * tile + p * half
        return twin_copy(p, mb, ts.at[p, 0, 0], {"uly": near}, wo_v.at[slab(mb), left : left + half])

    def twin_in(p, b):
        return twin_copy(p, b, ts.at[p, 0, 0], {"uly": near})

    def twin_share(p, j):
        return twin_copy(p, mb, ts.at[p, 0, j], {"blk": sibling if j == 0 else lax.rem(mb + 2 * j, nb)})

    def twin_pass(p, j):
        return twin_copy(p, lax.rem(mb + 2 * j, nb), ts.at[p, 1, j], {"blk": sibling})

    def share(p):
        twin_in(p, mb).wait_recv()
        for j in range(1, nb // 2):
            twin_share(p, j).start()
        twin_share(p, 0).start()

    def relay(p):
        for j in range(1, nb // 2):
            twin_in(p, lax.rem(mb + 2 * j, nb)).wait_recv()
            twin_pass(p, j).start()

    def whole(p):
        twin_in(p, sibling).wait_recv()
        for j in range(1, nb // 2):
            twin_in(p, lax.rem(sibling + 2 * j, nb)).wait_recv()

    def full_to(k):
        return pltpu.make_async_remote_copy(
            src_ref=full_v.at[k], dst_ref=full_r.at[k], send_sem=es.at[k], recv_sem=er.at[k],
            device_id={"uly": near}, device_id_type=MESH)

    def heads_to(k, kind, b):
        src, dst, where = ((kv_s, kv_r, place), (q_s, q_r, lower))[kind]
        return pltpu.make_async_remote_copy(
            src_ref=src.at[k, b], dst_ref=dst.at[where(k, mb), :], send_sem=hs.at[k, kind, b],
            recv_sem=hr.at[k, kind, mb], device_id={"blk": b}, device_id_type=MESH)

    def heads_from(k, kind, b):
        src, dst, where = ((kv_s, kv_r, place), (q_s, q_r, lower))[kind]
        return pltpu.make_async_remote_copy(
            src_ref=src.at[k, b], dst_ref=dst.at[where(k, b), :], send_sem=hs.at[k, kind, b],
            recv_sem=hr.at[k, kind, b], device_id={"blk": b}, device_id_type=MESH)

    loads[8].wait()
    chosen = lax.broadcasted_iota(jnp.int32, gain.shape, 1) == mz * nb + mb
    factor = jnp.sum(jnp.where(chosen, gain[...], 0.0), axis=-1, keepdims=True) * (LOG2E / math.sqrt(width))

    def await_heads(k, kind):
        for j in range(1, nb):
            heads_from(k, kind, lax.rem(mb + j, nb)).wait_recv()

    def flip(k):
        vt[:, k * span : (k + 1) * span] = kv_r[k * span : (k + 1) * span, :].T[width:, :]

    def widen(k):
        for b in range(nb):
            both = q_r[(k * nb + b) * most : (k * nb + b + 1) * most, :]
            clear = jnp.zeros((most, width), jnp.bfloat16)
            start = k * span + b * rows
            q_v[start : start + most, :] = jnp.concatenate([both[:, :width], clear], axis=1)
            q_v[start + most : start + rows, :] = jnp.concatenate(
                [both[: rows - most, width:], clear[: rows - most]], axis=1)

    def scored(k, c, first, last):
        q = q_v[k * span + c * SUB : k * span + (c + 1) * SUB, :]
        return lax.dot_general(
            kv_r[first * span : last * span, :], q, (((1,), (1,)), ((), ())), preferred_element_type=jnp.float32)

    def begin(k, c, first, last):
        scores = scored(k, c, first, last)
        top = jnp.max(scores, axis=0, keepdims=True)
        expo = jnp.exp2((scores - top) * factor)
        total = jnp.sum(expo, axis=0, keepdims=True)
        summed = jnp.dot(vt[:, first * span : last * span], expo.astype(jnp.bfloat16), preferred_element_type=jnp.float32)
        return top, total, summed

    def keep(k, first, last):
        for c in range(span // SUB):
            cols = slice(c * SUB, (c + 1) * SUB)
            top_v[k, :, cols], sum_v[k, :, cols], acc_v[k, :, cols] = begin(k, c, first, last)

    def more(k, c, first, last):
        cols = slice(c * SUB, (c + 1) * SUB)
        scores = scored(k, c, first, last)
        old = top_v[k, :, cols]
        top = jnp.maximum(old, jnp.max(scores, axis=0, keepdims=True))
        shrink = jnp.exp2((old - top) * factor)
        expo = jnp.exp2((scores - top) * factor)
        total = sum_v[k, :, cols] * shrink + jnp.sum(expo, axis=0, keepdims=True)
        summed = jnp.dot(vt[:, first * span : last * span], expo.astype(jnp.bfloat16), preferred_element_type=jnp.float32)
        return total, acc_v[k, :, cols] * shrink + summed

    def first_attend():
        for k in (0, 1):
            await_heads(k, 0)
            await_heads(k, 1)
            flip(k)
            widen(k)
        for k in (0, 1):
            keep(k, 0, 2)

    def piece(k, carry):
        @pl.when((k == 3) & jnp.logical_not(middle))
        def _():
            first_attend()

        @pl.when((k == 1) & jnp.logical_not(middle))
        def _():
            loads[6].wait()
            twin_out(0).start()
            twin_out(1).start()

        query = key = value = None
        for c in range(chunks):
            @pl.when((k > 0) & (jnp.logical_not(middle) | (k == 1)))
            def _():
                landed(k, c).wait_recv()

            @pl.when(middle & (k == 1))
            def _():
                across(c).start()

            @pl.when(middle & (k > 0) & (k < 3))
            def _():
                landed(k + 1, c).wait_recv()
                forward(k + 1, c).start()

            if c == 1:
                @pl.when(middle & (k == 2))
                def _():
                    share(0)

            x = mod[k, c]
            deeps = slice(c * deep, (c + 1) * deep)
            more_k = jnp.dot(x, wk_v[deeps, :], preferred_element_type=jnp.float32)
            more_v = jnp.dot(x, wv_v[deeps, :], preferred_element_type=jnp.float32)
            if c < chunks - 1:
                more_q = jnp.dot(x, wq_v[deeps, :], preferred_element_type=jnp.float32)
            key = more_k if c == 0 else key + more_k
            value = more_v if c == 0 else value + more_v
            if c < chunks - 1:
                query = more_q if c == 0 else query + more_q

        def unit(part):
            power = jnp.mean(part * part, axis=-1, keepdims=True)
            return part * lax.rsqrt(power + 1e-06)

        def send(kind):
            def one(j, carry):
                heads_to(k, kind, lax.rem(mb + j, nb)).start()
                return carry

            lax.fori_loop(1, nb, one, 0)

        for h in range(nb):
            cols = slice(h * width, (h + 1) * width)
            kv_s[k, h] = jnp.concatenate([unit(key[:, cols]), value[:, cols]], axis=1).astype(jnp.bfloat16)
        send(0)
        kv_r[place(k, mb), :] = kv_s[k, mb]
        query = query + jnp.dot(x, wq_v[deeps, :], preferred_element_type=jnp.float32)
        for h in range(nb):
            cols = slice(h * width, (h + 1) * width)
            line = unit(query[:, cols])
            rest = jnp.concatenate([line[most:], jnp.zeros((2 * most - rows, width), jnp.float32)], axis=0)
            q_s[k, h] = jnp.concatenate([line[:most], rest], axis=1).astype(jnp.bfloat16)
        send(1)
        q_r[lower(k, mb), :] = q_s[k, mb]
        return carry

    lax.fori_loop(0, 4, piece, 0)

    @pl.when(middle)
    def _():
        loads[6].wait()
        share(1)
        first_attend()

    await_heads(2, 0)
    await_heads(2, 1)
    flip(2)
    widen(2)
    keep(2, 0, 3)
    @pl.when(middle)
    def _():
        relay(0)

    await_heads(3, 0)
    flip(3)

    def back_to(j, b):
        return pltpu.make_async_remote_copy(
            src_ref=att_s.at[j, pl.ds(pl.multiple_of(b * rows, rows), rows), :], dst_ref=att_r.at[j, mb],
            send_sem=bs.at[j, b], recv_sem=br.at[j, mb], device_id={"blk": b}, device_id_type=MESH)

    def back_from(j, b):
        return pltpu.make_async_remote_copy(
            src_ref=att_s.at[j, pl.ds(pl.multiple_of(b * rows, rows), rows), :], dst_ref=att_r.at[j, b],
            send_sem=bs.at[j, b], recv_sem=br.at[j, b], device_id={"blk": b}, device_id_type=MESH)

    def finished(k, c):
        if k == 3:
            unused, total, summed = begin(k, c, 0, 4)
        else:
            total, summed = more(k, c, 3 if k == 2 else 2, 4)
        return summed / total

    def finish(j):
        if j == 0:
            lower = [finished(2, c) for c in range(span // SUB)]
            await_heads(3, 1)
            widen(3)
            upper = [finished(3, c) for c in range(span // SUB)]
        else:
            lower = [finished(1, c) for c in range(span // SUB)]
            upper = [finished(0, c) for c in range(span // SUB)]
        for c in range(span // SUB):
            both = jnp.concatenate([lower[c], upper[c]], axis=0)
            att_s[j, c * SUB : (c + 1) * SUB, :] = both.T.astype(jnp.bfloat16)

        def one(i, carry):
            back_to(j, lax.rem(mb + i, nb)).start()
            return carry

        lax.fori_loop(1, nb, one, 0)
        att_r[j, mb] = att_s[j, pl.ds(pl.multiple_of(mb * rows, rows), rows), :]

    def near_to(n):
        return pltpu.make_async_remote_copy(
            src_ref=part_s.at[1, n], dst_ref=near_r.at[n], send_sem=rs.at[1, n], recv_sem=rr.at[1, n],
            device_id={"uly": near}, device_id_type=MESH)

    def pair_to(k, n):
        return pltpu.make_async_remote_copy(
            src_ref=part_s.at[k, n], dst_ref=pair_r.at[k - 2, n], send_sem=rs.at[k, n], recv_sem=rr.at[k, n],
            device_id={"uly": near}, device_id_type=MESH)

    def far_to(k, n):
        return pltpu.make_async_remote_copy(
            src_ref=part_s.at[k, n], dst_ref=far_r.at[n], send_sem=rs.at[k, n], recv_sem=rr.at[0, n],
            device_id={"uly": inner if k == 2 else outer}, device_id_type=MESH)

    def project(j):
        for i in range(1, nb):
            back_from(j, lax.rem(mb + i, nb)).wait_recv()
        pieces = [att_r[j, h] for h in range(nb)]
        attended = jnp.concatenate(
            [
                jnp.concatenate([one[:, :width] for one in pieces], axis=1),
                jnp.concatenate([one[:, width:] for one in pieces], axis=1),
            ],
            axis=0,
        )
        if j == 0:
            full_v[2] = attended[:rows]
            full_v[3] = attended[rows:]
        else:
            full_v[1] = attended[:rows]

        @pl.when(jnp.logical_not(middle))
        def _():
            full_to(3 if j == 0 else 1).start()

        for n in range(apart):
            part = jnp.dot(attended, wo_v[:, n * tile : (n + 1) * tile], preferred_element_type=jnp.float32)
            if j == 0:
                for k in (2, 3):
                    mine = part[(k - 2) * rows : (k - 1) * rows]
                    part_v[k, n] = mine
                    part_s[k, n] = mine.astype(jnp.bfloat16)

                @pl.when(jnp.logical_not(middle))
                def _():
                    pair_to(3, n).start()
            else:
                part_s[1, n] = part[:rows].astype(jnp.bfloat16)
                near_to(n).start()
                part_v[0, n] = part[rows:]
        if j == 0:
            @pl.when(jnp.logical_not(middle))
            def _():
                full_to(2).start()
                for n in range(apart):
                    pair_to(2, n).start()

            @pl.when(middle)
            def _():
                for n in range(apart, parts):
                    part = jnp.dot(attended, wo_v[:, n * tile : (n + 1) * tile], preferred_element_type=jnp.float32)
                    for k in (2, 3):
                        part_v[k, n] = part[(k - 2) * rows : (k - 1) * rows]
        else:
            for n in range(apart, parts):
                part = jnp.dot(attended, wo_v[:, n * tile : (n + 1) * tile], preferred_element_type=jnp.float32)
                part_s[1, n] = part[:rows].astype(jnp.bfloat16)

                @pl.when(middle)
                def _():
                    near_to(n).start()

                part_v[0, n] = part[rows:]

    finish(0)
    finish(1)

    @pl.when(middle)
    def _():
        relay(1)

    loads[7].wait()
    project(0)
    project(1)

    def twin(k, n):
        cols = slice((n - apart) * tile, (n - apart + 1) * tile)
        return jnp.dot(full_r[k], twin_v[:, cols], preferred_element_type=jnp.float32)

    @pl.when(middle)
    def _():
        for k in (3, 2):
            full_to(k).wait_recv()
            for n in range(apart, parts):
                if k == 3:
                    if n == apart:
                        whole(0)
                    if n == (apart + parts) // 2:
                        whole(1)
                part_s[k, n] = (part_v[k, n] + twin(k, n)).astype(jnp.bfloat16)
                far_to(k, n).start()
            for n in range(apart):
                pair_to(k, n).wait_recv()
                part_s[k, n] = (part_v[k, n] + pair_r[k - 2, n].astype(jnp.float32)).astype(jnp.bfloat16)
                far_to(k, n).start()
        full_to(1).wait_recv()
        for n in range(apart, parts):
            part_v[0, n] += twin(1, n)

    def settle(n, extra):
        total = part_v[0, n] + far_r[n].astype(jnp.float32)
        if extra:
            total = total + near_r[n].astype(jnp.float32)
        cols = slice(n * tile, (n + 1) * tile)
        out[:, cols] = (tok[:, cols].astype(jnp.float32) + gate[:, cols] * total).astype(jnp.bfloat16)

    for n in range(apart, parts):
        far_to(2, n).wait_recv()

        @pl.when(middle)
        def _():
            settle(n, False)

        @pl.when(jnp.logical_not(middle))
        def _():
            near_to(n).wait_recv()
            settle(n, True)

    for n in range(apart):
        far_to(2, n).wait_recv()
        near_to(n).wait_recv()
        settle(n, True)

    for c in range(chunks):
        gather(0, c).wait_send()

    @pl.when(middle)
    def _():
        for c in range(chunks):
            gather(1, c).wait_send()
            across(c).wait_send()
        for k in (2, 3):
            for c in range(chunks):
                forward(k, c).wait_send()

    def sent(i, carry):
        b = lax.rem(mb + 1 + lax.rem(i, nb - 1), nb)
        k = i // (nb - 1)
        heads_to(k, 0, b).wait_send()
        heads_to(k, 1, b).wait_send()
        return carry

    lax.fori_loop(0, 4 * (nb - 1), sent, 0)
    for j in (0, 1):
        for i in range(1, nb):
            back_to(j, lax.rem(mb + i, nb)).wait_send()
    for k in (1, 2, 3):
        for n in range(apart):
            near_to(n).wait_send() if k == 1 else pair_to(k, n).wait_send()

    @pl.when(middle)
    def _():
        for k in (1, 2, 3):
            for n in range(apart, parts):
                near_to(n).wait_send() if k == 1 else pair_to(k, n).wait_send()
        for p in (0, 1):
            for j in range(nb // 2):
                twin_share(p, j).wait_send()
            for j in range(1, nb // 2):
                twin_pass(p, j).wait_send()

    @pl.when(jnp.logical_not(middle))
    def _():
        twin_out(0).wait_send()
        twin_out(1).wait_send()
        for k in (1, 2, 3):
            full_to(k).wait_send()


def fused(nb, tokens, mod_shift, mod_scale, mod_gate, w_query, w_key, w_value, w_out, score_gain):
    rows = tokens.shape[0]
    cols = w_query.shape[1]
    chunks = 4
    tile = 512
    parts = D // tile
    span = nb * rows
    most = -(-rows // 32) * 16
    bf16, f32 = jnp.bfloat16, jnp.float32
    vmem = pl.BlockSpec(memory_space=pltpu.VMEM)
    hbm = pl.BlockSpec(memory_space=pltpu.HBM)
    dma = pltpu.SemaphoreType.DMA
    return pl.pallas_call(
        functools.partial(kernel, nb),
        out_shape=pltpu.VMEM((rows, D), bf16),
        in_specs=[hbm] * 9,
        out_specs=vmem,
        scratch_shapes=[
            pltpu.VMEM((rows, D), bf16),
            pltpu.VMEM((1, D), f32),
            pltpu.VMEM((1, D), f32),
            pltpu.VMEM((1, D), f32),
            pltpu.VMEM((1, HEADS), f32),
            pltpu.VMEM((4, chunks, rows, D // chunks), bf16),
            pltpu.VMEM((D, cols), bf16),
            pltpu.VMEM((D, cols), bf16),
            pltpu.VMEM((D, cols), bf16),
            pltpu.VMEM((cols, D), bf16),
            pltpu.VMEM((4, nb, rows, 128), bf16),
            pltpu.VMEM((4, nb, most, 128), bf16),
            pltpu.VMEM((4 * span, 128), bf16),
            pltpu.VMEM((4 * nb * most, 128), bf16),
            pltpu.VMEM((4 * span, 128), bf16),
            pltpu.VMEM((64, 4 * span), bf16),
            pltpu.VMEM((4, 1, span), f32),
            pltpu.VMEM((4, 1, span), f32),
            pltpu.VMEM((4, 64, span), f32),
            pltpu.VMEM((2, span, 128), bf16),
            pltpu.VMEM((2, nb, rows, 128), bf16),
            pltpu.VMEM((4, rows, cols), bf16),
            pltpu.VMEM((4, rows, cols), bf16),
            pltpu.VMEM((cols, TWIN), bf16),
            pltpu.VMEM((4, parts, rows, tile), f32),
            pltpu.VMEM((4, parts, rows, tile), bf16),
            pltpu.VMEM((2, parts, rows, tile), bf16),
            pltpu.VMEM((parts, rows, tile), bf16),
            pltpu.VMEM((parts, rows, tile), bf16),
            dma((9,)),
            dma((2, chunks)),
            dma((4, chunks)),
            dma((4, chunks)),
            dma((4, 2, nb)),
            dma((4, 2, nb)),
            dma((2, nb)),
            dma((2, nb)),
            dma((4, parts)),
            dma((4, parts)),
            dma((4,)),
            dma((4,)),
            dma((2, 2, nb // 2)),
            dma((2, nb)),
            pltpu.SemaphoreType.REGULAR,
        ],
        compiler_params=pltpu.CompilerParams(
            collective_id=0, has_side_effects=True, vmem_limit_bytes=56 * 1024 * 1024
        ),
    )(
        tokens, mod_shift[None], mod_scale[None], mod_gate[None], score_gain[None],
        w_query, w_key, w_value, w_out,
    )


def modulate(tokens, mod_shift, mod_scale):
    values = tokens.astype(jnp.float32)
    center = values - jnp.mean(values, axis=-1, keepdims=True)
    spread = jnp.mean(center * center, axis=-1, keepdims=True)
    normed = center * lax.rsqrt(spread + 1e-06)
    return (normed * (1.0 + mod_scale) + mod_shift).astype(jnp.bfloat16)


def head_norm(projected, width):
    count = projected.shape[0]
    split = projected.reshape(count, -1, width)
    power = jnp.mean(split * split, axis=-1, keepdims=True)
    return (split * lax.rsqrt(power + 1e-06)).reshape(count, -1).astype(jnp.bfloat16)


def body(tokens, mod_shift, mod_scale, mod_gate, w_query, w_key, w_value, w_out, score_gain):
    width = D // HEADS
    local_cols = w_query.shape[1]
    local_heads = local_cols // width
    modded = modulate(tokens, mod_shift, mod_scale)
    piece = lax.all_gather(modded, "uly", axis=0, tiled=True)
    joined = jnp.concatenate(
        [
            jnp.dot(piece, w_query, preferred_element_type=jnp.float32),
            jnp.dot(piece, w_key, preferred_element_type=jnp.float32),
            jnp.dot(piece, w_value, preferred_element_type=jnp.float32),
        ],
        axis=1,
    )
    queries = head_norm(joined[:, :local_cols], width)
    keys = head_norm(joined[:, local_cols : 2 * local_cols], width)
    values = joined[:, 2 * local_cols :].astype(jnp.bfloat16)
    gains = lax.dynamic_slice_in_dim(score_gain, lax.axis_index("uly") * local_heads, local_heads)
    factors = gains / math.sqrt(width)
    rows = queries.shape[0]
    query_heads = queries.reshape(rows, local_heads, width)
    initial = (
        jnp.full((local_heads, rows), -jnp.inf, jnp.float32),
        jnp.zeros((local_heads, rows), jnp.float32),
        jnp.zeros((local_heads, rows, width), jnp.float32),
    )
    key_piece = lax.all_gather(keys, "blk", axis=0, tiled=True)
    value_piece = lax.all_gather(values, "blk", axis=0, tiled=True)
    count = key_piece.shape[0]
    groups = count // rows
    limit = max(rows, 1024)
    depth = max(
        [step for step in range(1, groups + 1) if groups % step == 0 and step * rows <= limit]
    )
    stride = depth * rows
    key_blocks = key_piece.reshape(count // stride, stride, local_heads, width)
    value_blocks = value_piece.reshape(count // stride, stride, local_heads, width)

    def one_block(carry, blocks):
        run_max, run_total, run_acc = carry
        key_block, value_block = blocks
        scores = jnp.einsum(
            "rhd,khd->hrk", query_heads, key_block, preferred_element_type=jnp.float32
        )
        scores = scores * factors[:, None, None]
        new_max = jnp.maximum(run_max, jnp.max(scores, axis=-1))
        expo = jnp.exp(scores - new_max[..., None])
        rescale = jnp.exp(run_max - new_max)
        new_total = run_total * rescale + jnp.sum(expo, axis=-1)
        summed = jnp.einsum(
            "hrk,khd->hrd",
            expo.astype(jnp.bfloat16),
            value_block,
            preferred_element_type=jnp.float32,
        )
        new_acc = run_acc * rescale[..., None] + summed
        return ((new_max, new_total, new_acc), None)

    result, unused = lax.scan(one_block, initial, (key_blocks, value_blocks))
    run_max, run_total, run_acc = result
    attended = (run_acc / run_total[..., None]).astype(jnp.bfloat16)
    attended = attended.transpose(1, 0, 2).reshape(rows, local_cols)
    returned = lax.all_to_all(attended, "uly", split_axis=0, concat_axis=1, tiled=True)
    projected = jnp.dot(
        returned,
        lax.all_gather(w_out, "uly", axis=0, tiled=True),
        preferred_element_type=jnp.float32,
    )
    return (tokens.astype(jnp.float32) + mod_gate * projected).astype(jnp.bfloat16)


def solution(mesh):
    in_specs = (
        P(("blk", "uly"), None),
        P(),
        P(),
        P(),
        P(None, "uly"),
        P(None, "uly"),
        P(None, "uly"),
        P("uly", None),
        P(),
    )
    out_specs = P(("blk", "uly"), None)
    nb, nz = mesh.shape["blk"], mesh.shape["uly"]
    run = body
    if HEADS == nb * nz and nz == 4 and nb == 8:
        run = functools.partial(fused, nb)
    return jax.shard_map(run, mesh=mesh, in_specs=in_specs, out_specs=out_specs, check_vma=False)
```

```python
import functools
import math

import jax
import jax.numpy as jnp
from jax import lax
from jax.experimental import pallas as pl
from jax.experimental.pallas import tpu as pltpu
from jax.sharding import PartitionSpec as P

D = 2048
HEADS = 32
LOG2E = math.log2(math.e)
MESH = pl.DeviceIdType.MESH
SUB = 384
TWIN = 1024


def kernel(
    nb, tok_h, shift_h, scale_h, gate_h, gain_h, wq, wk, wv, wo, out,
    tok, shift, scale, gate, gain, mod, wq_v, wk_v, wv_v, wo_v, kv_s, q_s, kv_r, q_r, q_v, vt, top_v, sum_v, acc_v,
    att_s, att_r, full_v, full_r, twin_v, part_v, part_s, pair_r, near_r, far_r,
    wsem, gs, gr, fs, hs, hr, bs, br, rs, rr, es, er, ts, tr, ready,
):
    width = D // HEADS
    rows = tok.shape[0]
    span = nb * rows
    chunks = mod.shape[1]
    deep = mod.shape[3]
    tile = part_s.shape[-1]
    parts = D // tile
    apart = parts - twin_v.shape[1] // tile
    mb, mz = lax.axis_index("blk"), lax.axis_index("uly")
    high = mz // 2
    middle = (mz + 1) // 2 == 1
    near = mz + 1 - 2 * lax.rem(mz, 2)
    inner = 2 - high
    outer = 3 - 3 * high

    pairs = (
        (tok_h, tok), (shift_h, shift), (scale_h, scale), (wk, wk_v), (wv, wv_v), (wq, wq_v),
        (wo, wo_v), (gate_h, gate), (gain_h, gain),
    )
    loads = [
        pltpu.make_async_copy(src, dst, wsem.at[i])
        for i, (src, dst) in enumerate(pairs)
    ]
    for load in loads[:3]:
        load.start()

    barrier = pltpu.get_barrier_semaphore()
    core = lax.rem(mb, 2)
    beside = mb + 2 - 4 * lax.rem(mb // 2, 2)
    behind = mb + 4 - 8 * (mb // 4)
    pl.semaphore_signal(barrier, inc=1, device_id={"uly": near}, device_id_type=MESH)

    @pl.when(middle)
    def _():
        pl.semaphore_signal(barrier, inc=1, device_id={"uly": inner}, device_id_type=MESH)

    for b in (mb, beside, behind):
        if b is not mb:
            pl.semaphore_signal(barrier, inc=1, device_id={"blk": b}, device_id_type=MESH)
        pl.semaphore_signal(barrier, inc=1, device_id={"blk": b + 1 - 2 * core}, device_id_type=MESH)

    for load in loads[3:]:
        load.start()
    for load in loads[:3]:
        load.wait()

    values = tok[...].astype(jnp.float32)
    center = values - jnp.mean(values, axis=-1, keepdims=True)
    spread = jnp.mean(center * center, axis=-1, keepdims=True)
    normed = center * lax.rsqrt(spread + 1e-06)
    modded = (normed * (1.0 + scale[...]) + shift[...]).astype(jnp.bfloat16)
    for c in range(chunks):
        mod[0, c] = modded[:, c * deep : (c + 1) * deep]

    pl.semaphore_wait(barrier, 6 + middle.astype(jnp.int32))
    pl.semaphore_signal(ready, inc=1, device_id={"blk": beside}, device_id_type=MESH)

    def gather(way, c):
        slot = 1 + way
        return pltpu.make_async_remote_copy(
            src_ref=mod.at[0, c], dst_ref=mod.at[slot, c], send_sem=gs.at[way, c], recv_sem=gr.at[slot, c],
            device_id={"uly": inner if way else near}, device_id_type=MESH)

    def landed(k, c):
        return pltpu.make_async_remote_copy(
            src_ref=mod.at[0, c], dst_ref=mod.at[k, c], send_sem=gs.at[0, c], recv_sem=gr.at[k, c],
            device_id={"uly": near}, device_id_type=MESH)

    def forward(k, c):
        return pltpu.make_async_remote_copy(
            src_ref=mod.at[k, c], dst_ref=mod.at[k, c], send_sem=fs.at[k, c], recv_sem=gr.at[k, c],
            device_id={"uly": near}, device_id_type=MESH)

    def across(c):
        return pltpu.make_async_remote_copy(
            src_ref=mod.at[1, c], dst_ref=mod.at[3, c], send_sem=fs.at[1, c], recv_sem=gr.at[3, c],
            device_id={"uly": inner}, device_id_type=MESH)

    @pl.when(middle)
    def _():
        for c in range(chunks):
            for way in (0, 1):
                gather(way, c).start()

    @pl.when(jnp.logical_not(middle))
    def _():
        for c in range(chunks):
            gather(0, c).start()

    for load in loads[3:6]:
        load.wait()
    pl.semaphore_wait(ready, 1)

    most = q_s.shape[2]

    def lower(k, b):
        return pl.ds(pl.multiple_of((k * nb + b) * most, most), most)

    def place(k, b):
        return pl.ds(pl.multiple_of(k * span + b * rows, rows), rows)

    depth = wo_v.shape[0] // nb
    sibling = mb + 1 - 2 * lax.rem(mb, 2)

    def slab(b):
        return pl.ds(pl.multiple_of(b * depth, depth), depth)

    half = twin_v.shape[1] // 2

    def twin_copy(p, b, send, who, src=None):
        here = twin_v.at[slab(b), p * half : (p + 1) * half]
        return pltpu.make_async_remote_copy(
            src_ref=here if src is None else src, dst_ref=here, send_sem=send, recv_sem=tr.at[p, b],
            device_id=who, device_id_type=MESH)

    def twin_out(p):
        left = apart * tile + p * half
        return twin_copy(p, mb, ts.at[p, 0, 0], {"uly": near}, wo_v.at[slab(mb), left : left + half])

    def twin_in(p, b):
        return twin_copy(p, b, ts.at[p, 0, 0], {"uly": near})

    def twin_share(p, j):
        return twin_copy(p, mb, ts.at[p, 0, j], {"blk": sibling if j == 0 else lax.rem(mb + 2 * j, nb)})

    def twin_pass(p, j):
        return twin_copy(p, lax.rem(mb + 2 * j, nb), ts.at[p, 1, j], {"blk": sibling})

    def share(p):
        twin_in(p, mb).wait_recv()
        for j in range(1, nb // 2):
            twin_share(p, j).start()
        twin_share(p, 0).start()

    def relay(p):
        for j in range(1, nb // 2):
            twin_in(p, lax.rem(mb + 2 * j, nb)).wait_recv()
            twin_pass(p, j).start()

    def whole(p):
        twin_in(p, sibling).wait_recv()
        for j in range(1, nb // 2):
            twin_in(p, lax.rem(sibling + 2 * j, nb)).wait_recv()

    def full_to(k):
        return pltpu.make_async_remote_copy(
            src_ref=full_v.at[k], dst_ref=full_r.at[k], send_sem=es.at[k], recv_sem=er.at[k],
            device_id={"uly": near}, device_id_type=MESH)

    def heads_to(k, kind, b):
        src, dst, where = ((kv_s, kv_r, place), (q_s, q_r, lower))[kind]
        return pltpu.make_async_remote_copy(
            src_ref=src.at[k, b], dst_ref=dst.at[where(k, mb), :], send_sem=hs.at[k, kind, b],
            recv_sem=hr.at[k, kind, mb], device_id={"blk": b}, device_id_type=MESH)

    def heads_from(k, kind, b):
        src, dst, where = ((kv_s, kv_r, place), (q_s, q_r, lower))[kind]
        return pltpu.make_async_remote_copy(
            src_ref=src.at[k, b], dst_ref=dst.at[where(k, b), :], send_sem=hs.at[k, kind, b],
            recv_sem=hr.at[k, kind, b], device_id={"blk": b}, device_id_type=MESH)

    loads[8].wait()
    chosen = lax.broadcasted_iota(jnp.int32, gain.shape, 1) == mz * nb + mb
    factor = jnp.sum(jnp.where(chosen, gain[...], 0.0), axis=-1, keepdims=True) * (LOG2E / math.sqrt(width))

    def await_heads(k, kind):
        for j in range(1, nb):
            heads_from(k, kind, lax.rem(mb + j, nb)).wait_recv()

    def flip(k):
        vt[:, k * span : (k + 1) * span] = kv_r[k * span : (k + 1) * span, :].T[width:, :]

    def widen(k):
        for b in range(nb):
            both = q_r[(k * nb + b) * most : (k * nb + b + 1) * most, :]
            clear = jnp.zeros((most, width), jnp.bfloat16)
            start = k * span + b * rows
            q_v[start : start + most, :] = jnp.concatenate([both[:, :width], clear], axis=1)
            q_v[start + most : start + rows, :] = jnp.concatenate(
                [both[: rows - most, width:], clear[: rows - most]], axis=1)

    def scored(k, c, first, last):
        q = q_v[k * span + c * SUB : k * span + (c + 1) * SUB, :]
        return lax.dot_general(
            kv_r[first * span : last * span, :], q, (((1,), (1,)), ((), ())), preferred_element_type=jnp.float32)

    def begin(k, c, first, last):
        scores = scored(k, c, first, last)
        top = jnp.max(scores, axis=0, keepdims=True)
        expo = jnp.exp2((scores - top) * factor)
        total = jnp.sum(expo, axis=0, keepdims=True)
        summed = jnp.dot(vt[:, first * span : last * span], expo.astype(jnp.bfloat16), preferred_element_type=jnp.float32)
        return top, total, summed

    def keep(k, first, last):
        for c in range(span // SUB):
            cols = slice(c * SUB, (c + 1) * SUB)
            top_v[k, :, cols], sum_v[k, :, cols], acc_v[k, :, cols] = begin(k, c, first, last)

    def more(k, c, first, last):
        cols = slice(c * SUB, (c + 1) * SUB)
        scores = scored(k, c, first, last)
        old = top_v[k, :, cols]
        top = jnp.maximum(old, jnp.max(scores, axis=0, keepdims=True))
        shrink = jnp.exp2((old - top) * factor)
        expo = jnp.exp2((scores - top) * factor)
        total = sum_v[k, :, cols] * shrink + jnp.sum(expo, axis=0, keepdims=True)
        summed = jnp.dot(vt[:, first * span : last * span], expo.astype(jnp.bfloat16), preferred_element_type=jnp.float32)
        return total, acc_v[k, :, cols] * shrink + summed

    def first_attend():
        for k in (0, 1):
            await_heads(k, 0)
            await_heads(k, 1)
            flip(k)
            widen(k)
        for k in (0, 1):
            keep(k, 0, 2)

    def piece(k, carry):
        @pl.when((k == 1) & jnp.logical_not(middle))
        def _():
            loads[6].wait()
            twin_out(0).start()
            twin_out(1).start()

        query = key = value = None
        for c in range(chunks):
            @pl.when((k > 0) & (jnp.logical_not(middle) | (k == 1)))
            def _():
                landed(k, c).wait_recv()

            @pl.when(middle & (k == 1))
            def _():
                across(c).start()

            @pl.when(middle & (k > 0) & (k < 3))
            def _():
                landed(k + 1, c).wait_recv()
                forward(k + 1, c).start()

            if c == 1:
                @pl.when(middle & (k == 2))
                def _():
                    share(0)

            x = mod[k, c]
            deeps = slice(c * deep, (c + 1) * deep)
            more_k = jnp.dot(x, wk_v[deeps, :], preferred_element_type=jnp.float32)
            more_v = jnp.dot(x, wv_v[deeps, :], preferred_element_type=jnp.float32)
            if c < chunks - 1:
                more_q = jnp.dot(x, wq_v[deeps, :], preferred_element_type=jnp.float32)
            key = more_k if c == 0 else key + more_k
            value = more_v if c == 0 else value + more_v
            if c < chunks - 1:
                query = more_q if c == 0 else query + more_q

        def unit(part):
            power = jnp.mean(part * part, axis=-1, keepdims=True)
            return part * lax.rsqrt(power + 1e-06)

        def send(kind):
            def one(j, carry):
                heads_to(k, kind, lax.rem(mb + j, nb)).start()
                return carry

            lax.fori_loop(1, nb, one, 0)

        for h in range(nb):
            cols = slice(h * width, (h + 1) * width)
            kv_s[k, h] = jnp.concatenate([unit(key[:, cols]), value[:, cols]], axis=1).astype(jnp.bfloat16)
        send(0)
        kv_r[place(k, mb), :] = kv_s[k, mb]
        query = query + jnp.dot(x, wq_v[deeps, :], preferred_element_type=jnp.float32)
        for h in range(nb):
            cols = slice(h * width, (h + 1) * width)
            line = unit(query[:, cols])
            rest = jnp.concatenate([line[most:], jnp.zeros((2 * most - rows, width), jnp.float32)], axis=0)
            q_s[k, h] = jnp.concatenate([line[:most], rest], axis=1).astype(jnp.bfloat16)
        send(1)
        q_r[lower(k, mb), :] = q_s[k, mb]
        return carry

    lax.fori_loop(0, 4, piece, 0)

    @pl.when(middle)
    def _():
        loads[6].wait()
        share(1)

    first_attend()
    await_heads(2, 0)
    await_heads(2, 1)
    flip(2)
    widen(2)
    keep(2, 0, 3)
    @pl.when(middle)
    def _():
        relay(0)

    await_heads(3, 0)
    flip(3)

    def back_to(j, b):
        return pltpu.make_async_remote_copy(
            src_ref=att_s.at[j, pl.ds(pl.multiple_of(b * rows, rows), rows), :], dst_ref=att_r.at[j, mb],
            send_sem=bs.at[j, b], recv_sem=br.at[j, mb], device_id={"blk": b}, device_id_type=MESH)

    def back_from(j, b):
        return pltpu.make_async_remote_copy(
            src_ref=att_s.at[j, pl.ds(pl.multiple_of(b * rows, rows), rows), :], dst_ref=att_r.at[j, b],
            send_sem=bs.at[j, b], recv_sem=br.at[j, b], device_id={"blk": b}, device_id_type=MESH)

    def finished(k, c):
        if k == 3:
            unused, total, summed = begin(k, c, 0, 4)
        else:
            total, summed = more(k, c, 3 if k == 2 else 2, 4)
        return summed / total

    def finish(j):
        if j == 0:
            lower = [finished(2, c) for c in range(span // SUB)]
            await_heads(3, 1)
            widen(3)
            upper = [finished(3, c) for c in range(span // SUB)]
        else:
            lower = [finished(1, c) for c in range(span // SUB)]
            upper = [finished(0, c) for c in range(span // SUB)]
        for c in range(span // SUB):
            both = jnp.concatenate([lower[c], upper[c]], axis=0)
            att_s[j, c * SUB : (c + 1) * SUB, :] = both.T.astype(jnp.bfloat16)

        def one(i, carry):
            back_to(j, lax.rem(mb + i, nb)).start()
            return carry

        lax.fori_loop(1, nb, one, 0)
        att_r[j, mb] = att_s[j, pl.ds(pl.multiple_of(mb * rows, rows), rows), :]

    def near_to(n):
        return pltpu.make_async_remote_copy(
            src_ref=part_s.at[1, n], dst_ref=near_r.at[n], send_sem=rs.at[1, n], recv_sem=rr.at[1, n],
            device_id={"uly": near}, device_id_type=MESH)

    def pair_to(k, n):
        return pltpu.make_async_remote_copy(
            src_ref=part_s.at[k, n], dst_ref=pair_r.at[k - 2, n], send_sem=rs.at[k, n], recv_sem=rr.at[k, n],
            device_id={"uly": near}, device_id_type=MESH)

    def far_to(k, n):
        return pltpu.make_async_remote_copy(
            src_ref=part_s.at[k, n], dst_ref=far_r.at[n], send_sem=rs.at[k, n], recv_sem=rr.at[0, n],
            device_id={"uly": inner if k == 2 else outer}, device_id_type=MESH)

    def project(j):
        for i in range(1, nb):
            back_from(j, lax.rem(mb + i, nb)).wait_recv()
        pieces = [att_r[j, h] for h in range(nb)]
        attended = jnp.concatenate(
            [
                jnp.concatenate([one[:, :width] for one in pieces], axis=1),
                jnp.concatenate([one[:, width:] for one in pieces], axis=1),
            ],
            axis=0,
        )
        if j == 0:
            full_v[2] = attended[:rows]
            full_v[3] = attended[rows:]
        else:
            full_v[1] = attended[:rows]

        @pl.when(jnp.logical_not(middle))
        def _():
            full_to(3 if j == 0 else 1).start()

        for n in range(apart):
            part = jnp.dot(attended, wo_v[:, n * tile : (n + 1) * tile], preferred_element_type=jnp.float32)
            if j == 0:
                for k in (2, 3):
                    mine = part[(k - 2) * rows : (k - 1) * rows]
                    part_v[k, n] = mine
                    part_s[k, n] = mine.astype(jnp.bfloat16)

                @pl.when(jnp.logical_not(middle))
                def _():
                    pair_to(3, n).start()
            else:
                part_s[1, n] = part[:rows].astype(jnp.bfloat16)
                near_to(n).start()
                part_v[0, n] = part[rows:]
        if j == 0:
            @pl.when(jnp.logical_not(middle))
            def _():
                full_to(2).start()
                for n in range(apart):
                    pair_to(2, n).start()

            @pl.when(middle)
            def _():
                for n in range(apart, parts):
                    part = jnp.dot(attended, wo_v[:, n * tile : (n + 1) * tile], preferred_element_type=jnp.float32)
                    for k in (2, 3):
                        part_v[k, n] = part[(k - 2) * rows : (k - 1) * rows]
        else:
            for n in range(apart, parts):
                part = jnp.dot(attended, wo_v[:, n * tile : (n + 1) * tile], preferred_element_type=jnp.float32)
                part_s[1, n] = part[:rows].astype(jnp.bfloat16)

                @pl.when(middle)
                def _():
                    near_to(n).start()

                part_v[0, n] = part[rows:]

    finish(0)
    finish(1)

    @pl.when(middle)
    def _():
        relay(1)

    loads[7].wait()
    project(0)
    project(1)

    def twin(k, n):
        cols = slice((n - apart) * tile, (n - apart + 1) * tile)
        return jnp.dot(full_r[k], twin_v[:, cols], preferred_element_type=jnp.float32)

    @pl.when(middle)
    def _():
        for k in (3, 2):
            full_to(k).wait_recv()
            for n in range(apart, parts):
                if k == 3:
                    if n == apart:
                        whole(0)
                    if n == (apart + parts) // 2:
                        whole(1)
                part_s[k, n] = (part_v[k, n] + twin(k, n)).astype(jnp.bfloat16)
                far_to(k, n).start()
            for n in range(apart):
                pair_to(k, n).wait_recv()
                part_s[k, n] = (part_v[k, n] + pair_r[k - 2, n].astype(jnp.float32)).astype(jnp.bfloat16)
                far_to(k, n).start()
        full_to(1).wait_recv()
        for n in range(apart, parts):
            part_v[0, n] += twin(1, n)

    def settle(n, extra):
        total = part_v[0, n] + far_r[n].astype(jnp.float32)
        if extra:
            total = total + near_r[n].astype(jnp.float32)
        cols = slice(n * tile, (n + 1) * tile)
        out[:, cols] = (tok[:, cols].astype(jnp.float32) + gate[:, cols] * total).astype(jnp.bfloat16)

    for n in range(apart, parts):
        far_to(2, n).wait_recv()

        @pl.when(middle)
        def _():
            settle(n, False)

        @pl.when(jnp.logical_not(middle))
        def _():
            near_to(n).wait_recv()
            settle(n, True)

    for n in range(apart):
        far_to(2, n).wait_recv()
        near_to(n).wait_recv()
        settle(n, True)

    for c in range(chunks):
        gather(0, c).wait_send()

    @pl.when(middle)
    def _():
        for c in range(chunks):
            gather(1, c).wait_send()
            across(c).wait_send()
        for k in (2, 3):
            for c in range(chunks):
                forward(k, c).wait_send()

    def sent(i, carry):
        b = lax.rem(mb + 1 + lax.rem(i, nb - 1), nb)
        k = i // (nb - 1)
        heads_to(k, 0, b).wait_send()
        heads_to(k, 1, b).wait_send()
        return carry

    lax.fori_loop(0, 4 * (nb - 1), sent, 0)
    for j in (0, 1):
        for i in range(1, nb):
            back_to(j, lax.rem(mb + i, nb)).wait_send()
    for k in (1, 2, 3):
        for n in range(apart):
            near_to(n).wait_send() if k == 1 else pair_to(k, n).wait_send()

    @pl.when(middle)
    def _():
        for k in (1, 2, 3):
            for n in range(apart, parts):
                near_to(n).wait_send() if k == 1 else pair_to(k, n).wait_send()
        for p in (0, 1):
            for j in range(nb // 2):
                twin_share(p, j).wait_send()
            for j in range(1, nb // 2):
                twin_pass(p, j).wait_send()

    @pl.when(jnp.logical_not(middle))
    def _():
        twin_out(0).wait_send()
        twin_out(1).wait_send()
        for k in (1, 2, 3):
            full_to(k).wait_send()


def fused(nb, tokens, mod_shift, mod_scale, mod_gate, w_query, w_key, w_value, w_out, score_gain):
    rows = tokens.shape[0]
    cols = w_query.shape[1]
    chunks = 4
    tile = 512
    parts = D // tile
    span = nb * rows
    most = -(-rows // 32) * 16
    bf16, f32 = jnp.bfloat16, jnp.float32
    vmem = pl.BlockSpec(memory_space=pltpu.VMEM)
    hbm = pl.BlockSpec(memory_space=pltpu.HBM)
    dma = pltpu.SemaphoreType.DMA
    return pl.pallas_call(
        functools.partial(kernel, nb),
        out_shape=pltpu.VMEM((rows, D), bf16),
        in_specs=[hbm] * 9,
        out_specs=vmem,
        scratch_shapes=[
            pltpu.VMEM((rows, D), bf16),
            pltpu.VMEM((1, D), f32),
            pltpu.VMEM((1, D), f32),
            pltpu.VMEM((1, D), f32),
            pltpu.VMEM((1, HEADS), f32),
            pltpu.VMEM((4, chunks, rows, D // chunks), bf16),
            pltpu.VMEM((D, cols), bf16),
            pltpu.VMEM((D, cols), bf16),
            pltpu.VMEM((D, cols), bf16),
            pltpu.VMEM((cols, D), bf16),
            pltpu.VMEM((4, nb, rows, 128), bf16),
            pltpu.VMEM((4, nb, most, 128), bf16),
            pltpu.VMEM((4 * span, 128), bf16),
            pltpu.VMEM((4 * nb * most, 128), bf16),
            pltpu.VMEM((4 * span, 128), bf16),
            pltpu.VMEM((64, 4 * span), bf16),
            pltpu.VMEM((4, 1, span), f32),
            pltpu.VMEM((4, 1, span), f32),
            pltpu.VMEM((4, 64, span), f32),
            pltpu.VMEM((2, span, 128), bf16),
            pltpu.VMEM((2, nb, rows, 128), bf16),
            pltpu.VMEM((4, rows, cols), bf16),
            pltpu.VMEM((4, rows, cols), bf16),
            pltpu.VMEM((cols, TWIN), bf16),
            pltpu.VMEM((4, parts, rows, tile), f32),
            pltpu.VMEM((4, parts, rows, tile), bf16),
            pltpu.VMEM((2, parts, rows, tile), bf16),
            pltpu.VMEM((parts, rows, tile), bf16),
            pltpu.VMEM((parts, rows, tile), bf16),
            dma((9,)),
            dma((2, chunks)),
            dma((4, chunks)),
            dma((4, chunks)),
            dma((4, 2, nb)),
            dma((4, 2, nb)),
            dma((2, nb)),
            dma((2, nb)),
            dma((4, parts)),
            dma((4, parts)),
            dma((4,)),
            dma((4,)),
            dma((2, 2, nb // 2)),
            dma((2, nb)),
            pltpu.SemaphoreType.REGULAR,
        ],
        compiler_params=pltpu.CompilerParams(
            collective_id=0, has_side_effects=True, vmem_limit_bytes=56 * 1024 * 1024
        ),
    )(
        tokens, mod_shift[None], mod_scale[None], mod_gate[None], score_gain[None],
        w_query, w_key, w_value, w_out,
    )


def modulate(tokens, mod_shift, mod_scale):
    values = tokens.astype(jnp.float32)
    center = values - jnp.mean(values, axis=-1, keepdims=True)
    spread = jnp.mean(center * center, axis=-1, keepdims=True)
    normed = center * lax.rsqrt(spread + 1e-06)
    return (normed * (1.0 + mod_scale) + mod_shift).astype(jnp.bfloat16)


def head_norm(projected, width):
    count = projected.shape[0]
    split = projected.reshape(count, -1, width)
    power = jnp.mean(split * split, axis=-1, keepdims=True)
    return (split * lax.rsqrt(power + 1e-06)).reshape(count, -1).astype(jnp.bfloat16)


def body(tokens, mod_shift, mod_scale, mod_gate, w_query, w_key, w_value, w_out, score_gain):
    width = D // HEADS
    local_cols = w_query.shape[1]
    local_heads = local_cols // width
    modded = modulate(tokens, mod_shift, mod_scale)
    piece = lax.all_gather(modded, "uly", axis=0, tiled=True)
    joined = jnp.concatenate(
        [
            jnp.dot(piece, w_query, preferred_element_type=jnp.float32),
            jnp.dot(piece, w_key, preferred_element_type=jnp.float32),
            jnp.dot(piece, w_value, preferred_element_type=jnp.float32),
        ],
        axis=1,
    )
    queries = head_norm(joined[:, :local_cols], width)
    keys = head_norm(joined[:, local_cols : 2 * local_cols], width)
    values = joined[:, 2 * local_cols :].astype(jnp.bfloat16)
    gains = lax.dynamic_slice_in_dim(score_gain, lax.axis_index("uly") * local_heads, local_heads)
    factors = gains / math.sqrt(width)
    rows = queries.shape[0]
    query_heads = queries.reshape(rows, local_heads, width)
    initial = (
        jnp.full((local_heads, rows), -jnp.inf, jnp.float32),
        jnp.zeros((local_heads, rows), jnp.float32),
        jnp.zeros((local_heads, rows, width), jnp.float32),
    )
    key_piece = lax.all_gather(keys, "blk", axis=0, tiled=True)
    value_piece = lax.all_gather(values, "blk", axis=0, tiled=True)
    count = key_piece.shape[0]
    groups = count // rows
    limit = max(rows, 1024)
    depth = max(
        [step for step in range(1, groups + 1) if groups % step == 0 and step * rows <= limit]
    )
    stride = depth * rows
    key_blocks = key_piece.reshape(count // stride, stride, local_heads, width)
    value_blocks = value_piece.reshape(count // stride, stride, local_heads, width)

    def one_block(carry, blocks):
        run_max, run_total, run_acc = carry
        key_block, value_block = blocks
        scores = jnp.einsum(
            "rhd,khd->hrk", query_heads, key_block, preferred_element_type=jnp.float32
        )
        scores = scores * factors[:, None, None]
        new_max = jnp.maximum(run_max, jnp.max(scores, axis=-1))
        expo = jnp.exp(scores - new_max[..., None])
        rescale = jnp.exp(run_max - new_max)
        new_total = run_total * rescale + jnp.sum(expo, axis=-1)
        summed = jnp.einsum(
            "hrk,khd->hrd",
            expo.astype(jnp.bfloat16),
            value_block,
            preferred_element_type=jnp.float32,
        )
        new_acc = run_acc * rescale[..., None] + summed
        return ((new_max, new_total, new_acc), None)

    result, unused = lax.scan(one_block, initial, (key_blocks, value_blocks))
    run_max, run_total, run_acc = result
    attended = (run_acc / run_total[..., None]).astype(jnp.bfloat16)
    attended = attended.transpose(1, 0, 2).reshape(rows, local_cols)
    returned = lax.all_to_all(attended, "uly", split_axis=0, concat_axis=1, tiled=True)
    projected = jnp.dot(
        returned,
        lax.all_gather(w_out, "uly", axis=0, tiled=True),
        preferred_element_type=jnp.float32,
    )
    return (tokens.astype(jnp.float32) + mod_gate * projected).astype(jnp.bfloat16)


def solution(mesh):
    in_specs = (
        P(("blk", "uly"), None),
        P(),
        P(),
        P(),
        P(None, "uly"),
        P(None, "uly"),
        P(None, "uly"),
        P("uly", None),
        P(),
    )
    out_specs = P(("blk", "uly"), None)
    nb, nz = mesh.shape["blk"], mesh.shape["uly"]
    run = body
    if HEADS == nb * nz and nz == 4 and nb == 8:
        run = functools.partial(fused, nb)
    return jax.shard_map(run, mesh=mesh, in_specs=in_specs, out_specs=out_specs, check_vma=False)
```
